32 devices in a mesh: gx: 4 (over x, core), gy: 8 (over z, y).
Axes of the slice: x: 2, y: 2, z: 4, core: 2. Of those that a mesh axis runs over, the one named last changes fastest.
Arguments:
- theta: float32 [4, 64, 1024], P(None, 'gy', 'gx'), may hold values from -3.140625 to 3.140625
- phi: float32 [4, 64, 1024], P(None, 'gy', 'gx'), may hold values from -3.140625 to 3.140625
- labels: int32 [4, 64, 1024], P(None, 'gy', 'gx'), may hold values from 0 to 15
- ms_region: float32 [16], replicated, may hold values from 0.4 to 1
- aex_region: float32 [16], replicated, may hold values from 0.5 to 2
- kernel: bfloat16 [6, 8, 2048, 128], P(None, None, ('gx', 'gy')), may hold values from -0.5 to 1.5
Outputs:
- field: float32 [3, 4, 64, 1024], P(None, None, 'gy', 'gx')
- predicted: float32 [3, 4, 64, 1024], P(None, None, 'gy', 'gx')
The draws below stay inside these ranges and needn't reach their ends.
All inputs are finite; a program needn't handle non-finite values.
Results may differ from the reference program's by a relative error of at most 0.0003.
Values sent between devices are 32-bit elements; how exact they have to be, the bound alone decides.
No kernel may reach another device: no remote copies, remote signals or barrier semaphores. Data moves between devices by JAX's collectives and lax.ppermute only.
A program may use at most 64 MiB of HBM per device.

```python
import math
import jax
import jax.numpy as jnp
from jax import lax

NZ = 4
REGIONS = 16
NX = 1024
NY = 64


def folded(length):
    index = jnp.arange(length)
    return jnp.minimum(index, length - index)


def draw_kernel(key, part):
    key = jax.random.fold_in(key, 7)
    depth, along_x, along_y = (2 * NZ, 2 * NX, 2 * NY)
    key_amp, key_base = jax.random.split(key)
    shape = (3, NZ + 1, NX + 1, NY + 1)
    amplitude = jnp.exp(jax.random.uniform(key_amp, shape, jnp.float32, math.log(0.2), 0.0))
    baseline = jax.random.uniform(key_base, shape[1:], jnp.float32, 0.0, 0.5)
    index_z = folded(depth)[:, None, None]
    index_x = folded(along_x)[None, :, None]
    index_y = folded(along_y)[None, None, :]
    spread = amplitude[:, index_z, index_x, index_y]
    base_grid = baseline[index_z, index_x, index_y]
    sine_x = jnp.sin(2.0 * math.pi * jnp.arange(along_x) / along_x).astype(jnp.float32)[None, :, None]
    sine_y = jnp.sin(2.0 * math.pi * jnp.arange(along_y) / along_y).astype(jnp.float32)[None, None, :]
    sine_z = jnp.sin(2.0 * math.pi * jnp.arange(depth) / depth).astype(jnp.float32)[:, None, None]
    part_x = sine_x * spread[0]
    part_y = sine_y * spread[1]
    part_z = sine_z * spread[2]
    denom = part_x * part_x + part_y * part_y + part_z * part_z + 0.5
    return jnp.stack([part_x * part_x / denom, part_y * part_y / denom, part_z * part_z / denom + base_grid, part_x * part_y / denom, part_x * part_z / denom, part_y * part_z / denom]).astype(jnp.bfloat16)


def with_ends(result, key, smallest, top_value):
    dims = result.shape
    spot = [jax.random.randint(jax.random.fold_in(key, axis), (), 0, dims[axis]) for axis in range(len(dims))]
    result = result.at[tuple(spot)].set(smallest)
    longest = dims.index(max(dims))
    spot[longest] = (spot[longest] + 1) % dims[longest]
    return result.at[tuple(spot)].set(top_value)


def setup_inputs(seed: int = 0) -> dict:
    arg_keys = jax.random.split(jax.random.key(seed), 7)
    return {
        "theta": jnp.clip(jax.random.uniform(arg_keys[0], (NZ, NY, NX), jnp.float32, -3.140625, 3.140625), -3.140625, 3.140625),
        "phi": jnp.clip(jax.random.uniform(arg_keys[1], (NZ, NY, NX), jnp.float32, -3.140625, 3.140625), -3.140625, 3.140625),
        "labels": with_ends(jax.random.randint(arg_keys[2], (NZ, NY, NX), 0, REGIONS), jax.random.fold_in(arg_keys[2], 1), 0, REGIONS - 1).astype(jnp.int32),
        "ms_region": jnp.clip(jnp.exp(jax.random.uniform(arg_keys[3], (REGIONS,), jnp.float32, math.log(0.4), math.log(1.0))), 0.4, 1.0),
        "aex_region": jnp.clip(jnp.exp(jax.random.uniform(arg_keys[4], (REGIONS,), jnp.float32, math.log(0.5), math.log(2.0))), 0.5, 2.0),
        "kernel": draw_kernel(jax.random.fold_in(arg_keys[6], 71), 0),
    }


damping = 0.5
time_step = 0.2
side_weight = 0.25
layer_weight = 0.5

def directions(theta, phi):
    lateral = jnp.sin(theta)
    return jnp.stack([lateral * jnp.cos(phi), lateral * jnp.sin(phi), jnp.cos(theta)])

def exchange_term(padded, unit, stiffness, saturation):
    depth, height, width = stiffness.shape
    offsets = [(1, 0, 0, layer_weight), (-1, 0, 0, layer_weight), (0, 1, 0, side_weight), (0, -1, 0, side_weight), (0, 0, 1, side_weight), (0, 0, -1, side_weight)]
    total = jnp.zeros_like(unit)
    for shift_z, shift_y, shift_x, weight in offsets:
        beside_all = padded[:, 1 + shift_z:1 + shift_z + depth, 1 + shift_y:1 + shift_y + height, 1 + shift_x:1 + shift_x + width]
        coupling = 2.0 * stiffness * beside_all[3] / (stiffness + beside_all[3])
        total = total + weight * coupling * (beside_all[:3] - unit)
    return total / saturation

def cross(first, second):
    return jnp.stack([first[1] * second[2] - first[2] * second[1], first[2] * second[0] - first[0] * second[2], first[0] * second[1] - first[1] * second[0]])

def predictor(unit, field):
    twist = cross(unit, field)
    torque = -(twist + damping * cross(unit, twist)) / (1.0 + damping * damping)
    moved = unit + time_step * torque
    return moved / jnp.sqrt(lax.optimization_barrier(jnp.sum(moved * moved, 0)))

def reference(theta, phi, labels, ms_region, aex_region, kernel):
    unit = directions(theta, phi)
    saturation = ms_region[labels]
    stiffness = aex_region[labels]
    padded = jnp.pad(jnp.concatenate([unit, stiffness[None]]), ((0, 0), (1, 1), (1, 1), (1, 1)))
    field_exchange = exchange_term(padded, unit, stiffness, saturation)
    moment = unit * saturation
    depth, height, width = theta.shape
    grid = jnp.zeros((3, 2 * depth, 2 * height, 2 * width), moment.dtype)
    grid = grid.at[:, :depth, :height, :width].set(moment)
    spectrum = jnp.fft.fftn(grid, axes=(1, 2, 3))
    tensor = jnp.transpose(kernel.astype(moment.dtype), (0, 1, 3, 2))
    image = -jnp.stack([tensor[0] * spectrum[0] + tensor[3] * spectrum[1] + tensor[4] * spectrum[2], tensor[3] * spectrum[0] + tensor[1] * spectrum[1] + tensor[5] * spectrum[2], tensor[4] * spectrum[0] + tensor[5] * spectrum[1] + tensor[2] * spectrum[2]])
    field_demag = jnp.real(jnp.fft.ifftn(image, axes=(1, 2, 3)))[:, :depth, :height, :width]
    field = field_exchange + field_demag.astype(moment.dtype)
    return (field, predictor(unit, field))
```

```python
import functools
import math

import jax
import jax.numpy as jnp
import ml_dtypes
import numpy as np
from jax import lax
from jax.experimental import pallas as pl
from jax.experimental.pallas import tpu as pltpu
from jax.sharding import PartitionSpec as P

damping = 0.5
time_step = 0.2
side_weight = 0.25
layer_weight = 0.5
root_half = math.sqrt(0.5)
constant_limit = 20 << 20


def split_high(value):
    high = value.astype(jnp.bfloat16)
    low = (value - high.astype(jnp.float32)).astype(jnp.bfloat16)
    return high, low


def split_table(table):
    high = table.astype(np.float32).astype(ml_dtypes.bfloat16)
    low = (table - high.astype(np.float64)).astype(np.float32).astype(ml_dtypes.bfloat16)
    return high, low


def dot(left, right, contract=((1,), (0,))):
    return lax.dot_general(left, right, (contract, ((), ())), preferred_element_type=jnp.float32)


def line_table(count_x, count_y, width, rows):
    cells = count_x * width
    if count_x * 2 * cells * count_y * 2 * rows * 2 > constant_limit:
        return None
    place = np.arange(cells)[None, :, None, None]
    wave = (
        np.arange(count_x)[:, None, None, None] * (count_y * rows)
        + np.arange(count_y)[None, None, :, None] * rows
        + np.arange(rows)[None, None, None, :]
    )
    angle = (place * wave % (2 * cells)) * (2.0 * math.pi / (2 * cells))
    table = np.stack([np.cos(angle), -np.sin(angle)], 3)
    table = table.reshape(count_x, cells, count_y * 2 * rows)
    high, low = split_table(table)
    return np.stack([high, low], 1)


def line_table_here(count_x, count_y, width, rows):
    cells = count_x * width
    place = jnp.arange(cells, dtype=jnp.int32)[:, None, None]
    wave = (
        lax.axis_index("gx") * (count_y * rows)
        + jnp.arange(count_y, dtype=jnp.int32)[None, :, None] * rows
        + jnp.arange(rows, dtype=jnp.int32)[None, None, :]
    )
    angle = (place * wave % (2 * cells)).astype(jnp.float32) * (math.pi / cells)
    table = jnp.stack([jnp.cos(angle), -jnp.sin(angle)], 2).reshape(cells, count_y * 2 * rows)
    return jnp.stack(split_high(table))


def column_tables(height):
    angle = (np.arange(2 * height)[:, None] * np.arange(height)[None, :] % (2 * height)) * (
        math.pi / height
    )
    high, low = split_table(np.concatenate([np.cos(angle), np.sin(angle)], 1))
    forward = np.concatenate([high, high, low], 1)
    high, low = split_table(np.concatenate([np.cos(angle.T), np.sin(angle.T)], 0))
    inverse = np.concatenate([high, high, low], 1)
    return forward, inverse


def sine_cosine(angle):
    turns = jnp.floor(angle * (2.0 / math.pi) + 0.5)
    rest = angle - turns * 1.5703125
    rest = rest - turns * 4.8351287841796875e-4
    rest = rest - turns * 3.1385570764541626e-7
    square = rest * rest
    sine = rest + rest * square * (
        -1.6666654611e-1 + square * (8.3321608736e-3 - square * 1.9515295891e-4)
    )
    cosine = (
        1.0
        - 0.5 * square
        + square * square * (4.166664568298827e-2 + square * (-1.388731625493765e-3 + square * 2.443315711809948e-5))
    )
    quarter = turns.astype(jnp.int32)
    odd = (quarter & 1) == 1
    out_sine = jnp.where(odd, cosine, sine)
    out_cosine = jnp.where(odd, sine, cosine)
    out_sine = jnp.where((quarter & 2) == 2, -out_sine, out_sine)
    out_cosine = jnp.where(((quarter + 1) & 2) == 2, -out_cosine, out_cosine)
    return out_sine, out_cosine


def directions(theta, phi):
    lateral, axial = sine_cosine(theta)
    sine, cosine = sine_cosine(phi)
    return [lateral * cosine, lateral * sine, axial]


def looked_up(labels, region):
    result = jnp.zeros_like(labels) + region[0]
    for index in range(1, region.shape[0]):
        result = jnp.where(labels == float(index), region[index], result)
    return result


def lines_body(raw, region, table_high, table_low):
    blocks = []
    for theta, phi, labels in raw:
        unit = directions(theta, phi)
        saturation = looked_up(labels, region)
        rows = theta.shape[0] * theta.shape[1]
        blocks.append(
            jnp.concatenate([(part * saturation).reshape(rows, -1) for part in unit], 0)
        )
    moment = jnp.concatenate(blocks, 1)
    high, low = split_high(moment)
    both = dot(jnp.concatenate([high, low], 0), table_high)
    lines = moment.shape[0]
    return both[:lines] + both[lines:] + dot(high, table_low)


def lines_kernel(raw_ref, region_ref, table_ref, out_ref):
    raw = [[raw_ref[g, f] for f in range(3)] for g in range(raw_ref.shape[0])]
    result = lines_body(raw, region_ref, table_ref[0], table_ref[1])
    lanes = out_ref.shape[2]
    for index in range(out_ref.shape[0]):
        out_ref[index] = result[:, index * lanes : (index + 1) * lanes]


def back_lines_body(spectrum, table_high, table_low, groups):
    high, low = split_high(spectrum)
    both = jnp.concatenate([high, low], 0)
    lines = spectrum.shape[0]
    width = table_high.shape[0] // groups
    result = []
    for index in range(groups):
        rows = slice(index * width, (index + 1) * width)
        wide = dot(both, table_high[rows], ((1,), (1,)))
        result.append(
            wide[:lines] + wide[lines:] + dot(high, table_low[rows], ((1,), (1,)))
        )
    return result


def back_lines_kernel(spectrum_ref, table_ref, out_ref):
    spectrum = jnp.concatenate([spectrum_ref[g] for g in range(spectrum_ref.shape[0])], 1)
    parts = back_lines_body(spectrum, table_ref[0], table_ref[1], out_ref.shape[0])
    for index, part in enumerate(parts):
        out_ref[index] = part


def tensor_kernel(kernel_ref, twice_ref, out_ref):
    twice = twice_ref[...]

    def step(index, carry):
        turned = dot(kernel_ref[index], twice, ((0,), (0,)))
        out_ref[index] = turned.astype(jnp.bfloat16)
        return carry

    lax.fori_loop(0, kernel_ref.shape[0], step, 0)


def turn(value, sign):
    lanes = value.shape[-1]
    if lanes == 128:
        return pltpu.roll(value, lanes // 2, value.ndim - 1) * sign
    return jnp.concatenate([value[..., lanes // 2 :], value[..., : lanes // 2]], -1) * sign


def layers_forward(layer, sign):
    d0, d1, d2, d3 = layer
    r2 = turn(d2, sign)
    near, far = d1 + d3, d1 - d3
    far_turned = turn(far, sign)
    near_turned = turn(near, sign)
    even, odd = d0 + d2, d0 - d2
    out = [None] * 8
    out[0], out[4] = even + near, even - near
    out[2], out[6] = odd + far_turned, odd - far_turned
    plus, minus = d0 + r2, d0 - r2
    first = (far + near_turned) * root_half
    second = (near_turned - far) * root_half
    out[1], out[5] = plus + first, plus - first
    out[3], out[7] = minus + second, minus - second
    return out


def layers_inverse(wave, sign):
    a, b = wave[0] + wave[4], wave[0] - wave[4]
    e, f = wave[2] + wave[6], turn(wave[2] - wave[6], sign)
    p, q = wave[1] + wave[5], wave[1] - wave[5]
    s, t = wave[3] + wave[7], turn(wave[3] - wave[7], sign)
    o0, o1, o2, o3 = p + s, q - t, p - s, q + t
    return [
        a + e + o0,
        b - f + (o1 - turn(o1, sign)) * root_half,
        a - e - turn(o2, sign),
        b + f - (o3 + turn(o3, sign)) * root_half,
    ]


def apply_tensor(tensor, wave):
    out = [[], [], []]
    for level in range(8):
        xx, yy, zz, xy, xz, yz = [tensor[part][level] for part in range(6)]
        x, y, z = wave[0][level], wave[1][level], wave[2][level]
        out[0].append(xx * x + xy * y + xz * z)
        out[1].append(xy * x + yy * y + yz * z)
        out[2].append(xz * x + yz * y + zz * z)
    return out


def waves_kernel(scale, spec_ref, tensor_ref, forward_ref, inverse_ref, out_ref, wave_ref, back_ref):
    count_y, lines, lanes = spec_ref.shape
    local = 8
    planes = lines // local
    height = count_y * local
    sign = jnp.where(
        lax.broadcasted_iota(jnp.int32, (1, lanes), 1) < lanes // 2, 1.0, -1.0
    ).astype(jnp.float32)
    columns = []
    for plane in range(planes):
        value = spec_ref[:, plane * local : (plane + 1) * local, :].reshape(height, lanes)
        value = jnp.concatenate([value, turn(value, sign)], 0)
        high, low = split_high(value)
        columns.append(jnp.concatenate([high, low, high], 0))
    wave_ref[...] = dot(forward_ref[...], jnp.concatenate(columns, 1))

    chunk = 16
    depth = planes // 3
    double = 2 * height

    def step(index, carry):
        rows = pl.ds(pl.multiple_of(index * chunk, chunk), chunk)
        wave = []
        for part in range(3):
            layer = [
                wave_ref[rows, (part * depth + z) * lanes : (part * depth + z + 1) * lanes]
                for z in range(depth)
            ]
            wave.append(layers_forward(layer, sign))
        tensor = [
            [tensor_ref[part * 8 + level, rows, :].astype(jnp.float32) for level in range(8)]
            for part in range(6)
        ]
        image = apply_tensor(tensor, wave)
        for part in range(3):
            layer = layers_inverse(image[part], sign)
            for z in range(depth):
                place = slice((part * depth + z) * lanes, (part * depth + z + 1) * lanes)
                high, low = split_high(layer[z] * scale)
                back_ref[rows, place] = high
                back_ref[pl.ds(pl.multiple_of(double + index * chunk, chunk), chunk), place] = low
                back_ref[pl.ds(pl.multiple_of(2 * double + index * chunk, chunk), chunk), place] = high
        return carry

    lax.fori_loop(0, double // chunk, step, 0)
    back = dot(inverse_ref[...], back_ref[...])
    for plane in range(planes):
        place = slice(plane * lanes, (plane + 1) * lanes)
        value = back[:height, place] - turn(back[height:, place], sign)
        out_ref[:, plane * local : (plane + 1) * local, :] = value.reshape(count_y, local, lanes)


def exchange_kernel(raw_ref, rows_ref, place_ref, ms_ref, aex_ref, exchange_ref, unit_ref):
    count_x = raw_ref.shape[0]
    depth, height, width = raw_ref.shape[2:]
    gx, gy, count_y = place_ref[0], place_ref[1], place_ref[2]
    left, right = jnp.maximum(gx - 1, 0), jnp.minimum(gx + 1, count_x - 1)
    shape = (depth, height, width)
    lane = lax.broadcasted_iota(jnp.int32, shape, 2)
    row = lax.broadcasted_iota(jnp.int32, shape, 1)

    def quantities(values):
        return directions(values[0], values[1]) + [looked_up(values[2], aex_ref)]

    raw = [raw_ref[gx, f] for f in range(3)]
    here = quantities(raw)
    side = quantities([jnp.where(lane == 0, raw_ref[right, f], raw_ref[left, f]) for f in range(3)])
    above = quantities(
        [
            jnp.where(
                row == 0,
                jnp.broadcast_to(rows_ref[1, f][:, None, :], shape),
                jnp.broadcast_to(rows_ref[0, f][:, None, :], shape),
            )
            for f in range(3)
        ]
    )
    saturation = looked_up(raw[2], ms_ref)
    total = [jnp.zeros(shape, jnp.float32) for _ in range(3)]

    def add(total, beside, weight):
        coupling = 2.0 * here[3] * beside[3] / (here[3] + beside[3]) * weight
        return [total[c] + coupling * (beside[c] - here[c]) for c in range(3)]

    one = jnp.float32(1.0)
    zero = jnp.float32(0.0)
    for shift, edge, there in ((1, 0, gx > 0), (width - 1, width - 1, gx < count_x - 1)):
        beside = [
            jnp.where(lane == edge, pltpu.roll(s, shift, 2), pltpu.roll(h, shift, 2))
            for s, h in zip(side, here)
        ]
        weight = jnp.where(lane == edge, jnp.where(there, one, zero), one) * side_weight
        total = add(total, beside, weight)
    for shift, edge, there in ((1, 0, gy > 0), (height - 1, height - 1, gy < count_y - 1)):
        beside = [
            jnp.where(row == edge, pltpu.roll(s, shift, 1), pltpu.roll(h, shift, 1))
            for s, h in zip(above, here)
        ]
        weight = jnp.where(row == edge, jnp.where(there, one, zero), one) * side_weight
        total = add(total, beside, weight)
    for part in range(3):
        unit_ref[part] = here[part]
    for z in range(depth):
        out = [total[c][z] for c in range(3)]
        for other in (z - 1, z + 1):
            if 0 <= other < depth:
                a, b = here[3][z], here[3][other]
                coupling = 2.0 * a * b / (a + b) * layer_weight
                out = [out[c] + coupling * (here[c][other] - here[c][z]) for c in range(3)]
        for c in range(3):
            exchange_ref[c, z] = out[c] / saturation[z]


def cross(first, second):
    return [
        first[1] * second[2] - first[2] * second[1],
        first[2] * second[0] - first[0] * second[2],
        first[0] * second[1] - first[1] * second[0],
    ]


def final_kernel(parts_ref, exchange_ref, unit_ref, field_ref, predicted_ref):
    depth, height, width = unit_ref.shape[1:]
    rows = depth * height
    unit, field = [], []
    for c in range(3):
        place = slice(c * rows, (c + 1) * rows)
        total = parts_ref[0, place]
        for index in range(1, parts_ref.shape[0]):
            total = total + parts_ref[index, place]
        field.append(exchange_ref[c] + total.reshape(depth, height, width))
        unit.append(unit_ref[c])
        field_ref[c] = field[c]
    twist = cross(unit, field)
    second = cross(unit, twist)
    moved = [
        unit[c] - (time_step / (1.0 + damping * damping)) * (twist[c] + damping * second[c])
        for c in range(3)
    ]
    length = jnp.sqrt(moved[0] * moved[0] + moved[1] * moved[1] + moved[2] * moved[2])
    for c in range(3):
        predicted_ref[c] = moved[c] / length


vmem = pl.BlockSpec(memory_space=pltpu.VMEM)
smem = pl.BlockSpec(memory_space=pltpu.SMEM)


def call(body, out, ins, operands, scratch=(), flops=0, name=None):
    size = sum(math.prod(o.shape) * o.dtype.itemsize for o in operands)
    outs = out if isinstance(out, (list, tuple)) else [out]
    size += sum(math.prod(o.shape) * o.dtype.itemsize for o in outs)
    return pl.pallas_call(
        body,
        out_shape=out,
        in_specs=ins,
        out_specs=jax.tree.map(lambda _: vmem, out),
        scratch_shapes=list(scratch),
        compiler_params=pltpu.CompilerParams(vmem_limit_bytes=40 << 20),
        cost_estimate=pl.CostEstimate(flops=flops, bytes_accessed=size, transcendentals=0),
        name=name,
    )(*operands)


def f32(*shape):
    return jax.ShapeDtypeStruct(shape, jnp.float32)


def per_device(theta, phi, labels, ms_region, aex_region, kernel):
    count_x, count_y = lax.axis_size("gx"), lax.axis_size("gy")
    gx, gy = lax.axis_index("gx"), lax.axis_index("gy")
    depth, height, width = theta.shape
    rows = kernel.shape[2]
    lanes = 2 * rows
    lines = 3 * depth * height
    whole_y = count_y * height

    raw = jnp.stack([theta, phi, labels.astype(jnp.float32)])
    gathered = lax.all_gather(raw, "gx")
    up = [(i, i + 1) for i in range(count_y - 1)]
    down = [(j, i) for i, j in up]
    before = lax.ppermute(raw[:, :, height - 1], "gy", up)
    after = lax.ppermute(raw[:, :, 0], "gy", down)

    table = line_table(count_x, count_y, width, rows)
    if table is None:
        table = line_table_here(count_x, count_y, width, rows)
    else:
        table = lax.dynamic_index_in_dim(jnp.asarray(table), gx, 0, keepdims=False)
    forward, inverse = column_tables(whole_y)

    twice = np.concatenate([np.eye(rows), np.eye(rows)], 1).astype(ml_dtypes.bfloat16)
    tensor = call(
        tensor_kernel,
        jax.ShapeDtypeStruct((48, 2 * whole_y, lanes), jnp.bfloat16),
        [vmem, vmem],
        (kernel.reshape(48, rows, 2 * whole_y), jnp.asarray(twice)),
        flops=48 * 2 * rows * lanes * 2 * whole_y,
        name="tensor",
    )
    spectrum = call(
        lines_kernel,
        f32(count_y, lines, lanes),
        [vmem, smem, vmem],
        (gathered, ms_region, table),
        flops=6 * lines * count_x * width * count_y * lanes,
        name="lines",
    )
    columns = lax.all_to_all(spectrum, "gy", split_axis=0, concat_axis=0, tiled=True)
    scale = -1.0 / (8.0 * depth * 0 + 2 * depth * 2 * whole_y * 2 * count_x * width)
    waves = call(
        functools.partial(waves_kernel, scale),
        f32(count_y, lines, lanes),
        [vmem] * 4,
        (columns, tensor, jnp.asarray(forward), jnp.asarray(inverse)),
        scratch=(
            pltpu.VMEM((2 * whole_y, 3 * depth * lanes), jnp.float32),
            pltpu.VMEM((6 * whole_y, 3 * depth * lanes), jnp.bfloat16),
        ),
        flops=20 * whole_y * whole_y * 3 * depth * lanes,
        name="waves",
    )
    returned = lax.all_to_all(waves, "gy", split_axis=0, concat_axis=0, tiled=True)
    partial = call(
        back_lines_kernel,
        f32(count_x, lines, width),
        [vmem, vmem],
        (returned, table),
        flops=6 * lines * count_x * width * count_y * lanes,
        name="back_lines",
    )
    parts = lax.all_to_all(partial, "gx", split_axis=0, concat_axis=0, tiled=True)
    place = jnp.stack([gx, gy, jnp.int32(count_y)]).astype(jnp.int32)
    exchange, unit = call(
        exchange_kernel,
        [f32(3, depth, height, width), f32(3, depth, height, width)],
        [vmem, vmem, smem, smem, smem],
        (gathered, jnp.stack([before, after]), place, ms_region, aex_region),
        flops=300 * depth * height * width,
        name="exchange",
    )
    field, predicted = call(
        final_kernel,
        [f32(3, depth, height, width), f32(3, depth, height, width)],
        [vmem] * 3,
        (parts, exchange, unit),
        flops=60 * depth * height * width,
        name="predict",
    )
    return field, predicted


def solution(mesh):
    in_specs = (
        P(None, "gy", "gx"),
        P(None, "gy", "gx"),
        P(None, "gy", "gx"),
        P(),
        P(),
        P(None, None, ("gx", "gy"), None),
    )
    out_specs = (P(None, None, "gy", "gx"), P(None, None, "gy", "gx"))
    return jax.shard_map(
        per_device, mesh=mesh, in_specs=in_specs, out_specs=out_specs, check_vma=False
    )
```

```python
import functools
import math

import jax
import jax.numpy as jnp
import ml_dtypes
import numpy as np
from jax import lax
from jax.experimental import pallas as pl
from jax.experimental.pallas import tpu as pltpu
from jax.sharding import PartitionSpec as P

damping = 0.5
time_step = 0.2
side_weight = 0.25
layer_weight = 0.5
root_half = math.sqrt(0.5)
constant_limit = 20 << 20


def split_high(value):
    high = value.astype(jnp.bfloat16)
    low = (value - high.astype(jnp.float32)).astype(jnp.bfloat16)
    return high, low


def split_table(table):
    high = table.astype(np.float32).astype(ml_dtypes.bfloat16)
    low = (table - high.astype(np.float64)).astype(np.float32).astype(ml_dtypes.bfloat16)
    return high, low


def dot(left, right, contract=((1,), (0,))):
    return lax.dot_general(left, right, (contract, ((), ())), preferred_element_type=jnp.float32)


def line_table(count_x, count_y, width, rows):
    cells = count_x * width
    if count_x * 2 * cells * count_y * 2 * rows * 2 > constant_limit:
        return None
    place = np.arange(cells)[None, :, None, None]
    wave = (
        np.arange(count_x)[:, None, None, None] * (count_y * rows)
        + np.arange(count_y)[None, None, :, None] * rows
        + np.arange(rows)[None, None, None, :]
    )
    angle = (place * wave % (2 * cells)) * (2.0 * math.pi / (2 * cells))
    table = np.stack([np.cos(angle), -np.sin(angle)], 3)
    table = table.reshape(count_x, cells, count_y * 2 * rows)
    high, low = split_table(table)
    return np.stack([high, low], 1)


def line_table_here(count_x, count_y, width, rows):
    cells = count_x * width
    place = jnp.arange(cells, dtype=jnp.int32)[:, None, None]
    wave = (
        lax.axis_index("gx") * (count_y * rows)
        + jnp.arange(count_y, dtype=jnp.int32)[None, :, None] * rows
        + jnp.arange(rows, dtype=jnp.int32)[None, None, :]
    )
    angle = (place * wave % (2 * cells)).astype(jnp.float32) * (math.pi / cells)
    table = jnp.stack([jnp.cos(angle), -jnp.sin(angle)], 2).reshape(cells, count_y * 2 * rows)
    return jnp.stack(split_high(table))


def column_tables(height):
    angle = (np.arange(2 * height)[:, None] * np.arange(height)[None, :] % (2 * height)) * (
        math.pi / height
    )
    high, low = split_table(np.concatenate([np.cos(angle), np.sin(angle)], 1))
    forward = np.concatenate([high, high, low], 1)
    high, low = split_table(np.concatenate([np.cos(angle.T), np.sin(angle.T)], 0))
    inverse = np.concatenate([high, high, low], 1)
    return forward, inverse


def sine_cosine(angle):
    turns = jnp.floor(angle * (2.0 / math.pi) + 0.5)
    rest = angle - turns * 1.5703125
    rest = rest - turns * 4.8351287841796875e-4
    rest = rest - turns * 3.1385570764541626e-7
    square = rest * rest
    sine = rest + rest * square * (
        -1.6666654611e-1 + square * (8.3321608736e-3 - square * 1.9515295891e-4)
    )
    cosine = (
        1.0
        - 0.5 * square
        + square * square * (4.166664568298827e-2 + square * (-1.388731625493765e-3 + square * 2.443315711809948e-5))
    )
    quarter = turns.astype(jnp.int32)
    odd = (quarter & 1) == 1
    out_sine = jnp.where(odd, cosine, sine)
    out_cosine = jnp.where(odd, sine, cosine)
    out_sine = jnp.where((quarter & 2) == 2, -out_sine, out_sine)
    out_cosine = jnp.where(((quarter + 1) & 2) == 2, -out_cosine, out_cosine)
    return out_sine, out_cosine


def directions(theta, phi):
    lateral, axial = sine_cosine(theta)
    sine, cosine = sine_cosine(phi)
    return [lateral * cosine, lateral * sine, axial]


def looked_up(labels, region):
    result = jnp.zeros_like(labels) + region[0]
    for index in range(1, region.shape[0]):
        result = jnp.where(labels == float(index), region[index], result)
    return result


def pack_kernel(theta_ref, phi_ref, labels_ref, raw_ref, first_ref, last_ref):
    height = theta_ref.shape[1]
    values = [theta_ref[...], phi_ref[...], labels_ref[...].astype(jnp.float32)]
    for index, value in enumerate(values):
        for copy in range(raw_ref.shape[0]):
            raw_ref[copy, index] = value
        first_ref[index] = value[:, 0]
        last_ref[index] = value[:, height - 1]


def lines_body(raw, region, table_high, table_low):
    blocks = []
    for theta, phi, labels in raw:
        unit = directions(theta, phi)
        saturation = looked_up(labels, region)
        rows = theta.shape[0] * theta.shape[1]
        blocks.append(
            jnp.concatenate([(part * saturation).reshape(rows, -1) for part in unit], 0)
        )
    moment = jnp.concatenate(blocks, 1)
    high, low = split_high(moment)
    both = dot(jnp.concatenate([high, low], 0), table_high)
    lines = moment.shape[0]
    return both[:lines] + both[lines:] + dot(high, table_low)


def lines_kernel(raw_ref, region_ref, table_ref, out_ref):
    raw = [[raw_ref[g, f] for f in range(3)] for g in range(raw_ref.shape[0])]
    result = lines_body(raw, region_ref, table_ref[0], table_ref[1])
    lanes = out_ref.shape[2]
    for index in range(out_ref.shape[0]):
        out_ref[index] = result[:, index * lanes : (index + 1) * lanes]


def back_lines_body(spectrum, table_high, table_low, groups):
    high, low = split_high(spectrum)
    both = jnp.concatenate([high, low], 0)
    lines = spectrum.shape[0]
    width = table_high.shape[0] // groups
    result = []
    for index in range(groups):
        rows = slice(index * width, (index + 1) * width)
        wide = dot(both, table_high[rows], ((1,), (1,)))
        result.append(
            wide[:lines] + wide[lines:] + dot(high, table_low[rows], ((1,), (1,)))
        )
    return result


def back_lines_kernel(spectrum_ref, table_ref, out_ref):
    spectrum = jnp.concatenate([spectrum_ref[g] for g in range(spectrum_ref.shape[0])], 1)
    parts = back_lines_body(spectrum, table_ref[0], table_ref[1], out_ref.shape[0])
    for index, part in enumerate(parts):
        out_ref[index] = part


def tensor_kernel(kernel_ref, twice_ref, out_ref):
    twice = twice_ref[...]

    unroll = 8

    def step(index, carry):
        for offset in range(unroll):
            turned = dot(kernel_ref[index * unroll + offset], twice, ((0,), (0,)))
            out_ref[index * unroll + offset] = turned.astype(jnp.bfloat16)
        return carry

    lax.fori_loop(0, kernel_ref.shape[0] // unroll, step, 0)


def turn(value, sign):
    lanes = value.shape[-1]
    if lanes == 128:
        return pltpu.roll(value, lanes // 2, value.ndim - 1) * sign
    return jnp.concatenate([value[..., lanes // 2 :], value[..., : lanes // 2]], -1) * sign


def layers_forward(layer, sign):
    d0, d1, d2, d3 = layer
    r2 = turn(d2, sign)
    near, far = d1 + d3, d1 - d3
    far_turned = turn(far, sign)
    near_turned = turn(near, sign)
    even, odd = d0 + d2, d0 - d2
    out = [None] * 8
    out[0], out[4] = even + near, even - near
    out[2], out[6] = odd + far_turned, odd - far_turned
    plus, minus = d0 + r2, d0 - r2
    first = (far + near_turned) * root_half
    second = (near_turned - far) * root_half
    out[1], out[5] = plus + first, plus - first
    out[3], out[7] = minus + second, minus - second
    return out


def layers_inverse(wave, sign):
    a, b = wave[0] + wave[4], wave[0] - wave[4]
    e, f = wave[2] + wave[6], turn(wave[2] - wave[6], sign)
    p, q = wave[1] + wave[5], wave[1] - wave[5]
    s, t = wave[3] + wave[7], turn(wave[3] - wave[7], sign)
    o0, o1, o2, o3 = p + s, q - t, p - s, q + t
    return [
        a + e + o0,
        b - f + (o1 - turn(o1, sign)) * root_half,
        a - e - turn(o2, sign),
        b + f - (o3 + turn(o3, sign)) * root_half,
    ]


def apply_tensor(tensor, wave):
    out = [[], [], []]
    for level in range(8):
        xx, yy, zz, xy, xz, yz = [tensor[part][level] for part in range(6)]
        x, y, z = wave[0][level], wave[1][level], wave[2][level]
        out[0].append(xx * x + xy * y + xz * z)
        out[1].append(xy * x + yy * y + yz * z)
        out[2].append(xz * x + yz * y + zz * z)
    return out


def waves_kernel(scale, spec_ref, tensor_ref, forward_ref, inverse_ref, out_ref, wave_ref, back_ref):
    count_y, lines, lanes = spec_ref.shape
    local = 8
    planes = lines // local
    height = count_y * local
    sign = jnp.where(
        lax.broadcasted_iota(jnp.int32, (1, lanes), 1) < lanes // 2, 1.0, -1.0
    ).astype(jnp.float32)
    columns = []
    for plane in range(planes):
        value = spec_ref[:, plane * local : (plane + 1) * local, :].reshape(height, lanes)
        value = jnp.concatenate([value, turn(value, sign)], 0)
        high, low = split_high(value)
        columns.append(jnp.concatenate([high, low, high], 0))
    wave_ref[...] = dot(forward_ref[...], jnp.concatenate(columns, 1))

    chunk = 16
    depth = planes // 3
    double = 2 * height

    def step(index, carry):
        rows = pl.ds(pl.multiple_of(index * chunk, chunk), chunk)
        wave = []
        for part in range(3):
            layer = [
                wave_ref[rows, (part * depth + z) * lanes : (part * depth + z + 1) * lanes]
                for z in range(depth)
            ]
            wave.append(layers_forward(layer, sign))
        tensor = [
            [tensor_ref[part * 8 + level, rows, :].astype(jnp.float32) for level in range(8)]
            for part in range(6)
        ]
        image = apply_tensor(tensor, wave)
        for part in range(3):
            layer = layers_inverse(image[part], sign)
            for z in range(depth):
                place = slice((part * depth + z) * lanes, (part * depth + z + 1) * lanes)
                high, low = split_high(layer[z] * scale)
                back_ref[rows, place] = high
                back_ref[pl.ds(pl.multiple_of(double + index * chunk, chunk), chunk), place] = low
                back_ref[pl.ds(pl.multiple_of(2 * double + index * chunk, chunk), chunk), place] = high
        return carry

    lax.fori_loop(0, double // chunk, step, 0)
    back = dot(inverse_ref[...], back_ref[...])
    for plane in range(planes):
        place = slice(plane * lanes, (plane + 1) * lanes)
        value = back[:height, place] - turn(back[height:, place], sign)
        out_ref[:, plane * local : (plane + 1) * local, :] = value.reshape(count_y, local, lanes)


def exchange_kernel(raw_ref, before_ref, after_ref, place_ref, ms_ref, aex_ref, exchange_ref, unit_ref):
    count_x = raw_ref.shape[0]
    depth, height, width = raw_ref.shape[2:]
    gx, gy, count_y = place_ref[0], place_ref[1], place_ref[2]
    left, right = jnp.maximum(gx - 1, 0), jnp.minimum(gx + 1, count_x - 1)
    shape = (depth, height, width)
    lane = lax.broadcasted_iota(jnp.int32, shape, 2)
    row = lax.broadcasted_iota(jnp.int32, shape, 1)

    def quantities(values):
        return directions(values[0], values[1]) + [looked_up(values[2], aex_ref)]

    raw = [raw_ref[gx, f] for f in range(3)]
    here = quantities(raw)
    side = quantities([jnp.where(lane == 0, raw_ref[right, f], raw_ref[left, f]) for f in range(3)])
    above = quantities(
        [
            jnp.where(
                row == 0,
                jnp.broadcast_to(after_ref[f][:, None, :], shape),
                jnp.broadcast_to(before_ref[f][:, None, :], shape),
            )
            for f in range(3)
        ]
    )
    saturation = looked_up(raw[2], ms_ref)
    total = [jnp.zeros(shape, jnp.float32) for _ in range(3)]

    def add(total, beside, weight):
        coupling = 2.0 * here[3] * beside[3] / (here[3] + beside[3]) * weight
        return [total[c] + coupling * (beside[c] - here[c]) for c in range(3)]

    one = jnp.float32(1.0)
    zero = jnp.float32(0.0)
    for shift, edge, there in ((1, 0, gx > 0), (width - 1, width - 1, gx < count_x - 1)):
        beside = [
            jnp.where(lane == edge, pltpu.roll(s, shift, 2), pltpu.roll(h, shift, 2))
            for s, h in zip(side, here)
        ]
        weight = jnp.where(lane == edge, jnp.where(there, one, zero), one) * side_weight
        total = add(total, beside, weight)
    for shift, edge, there in ((1, 0, gy > 0), (height - 1, height - 1, gy < count_y - 1)):
        beside = [
            jnp.where(row == edge, pltpu.roll(s, shift, 1), pltpu.roll(h, shift, 1))
            for s, h in zip(above, here)
        ]
        weight = jnp.where(row == edge, jnp.where(there, one, zero), one) * side_weight
        total = add(total, beside, weight)
    for part in range(3):
        unit_ref[part] = here[part]
    for z in range(depth):
        out = [total[c][z] for c in range(3)]
        for other in (z - 1, z + 1):
            if 0 <= other < depth:
                a, b = here[3][z], here[3][other]
                coupling = 2.0 * a * b / (a + b) * layer_weight
                out = [out[c] + coupling * (here[c][other] - here[c][z]) for c in range(3)]
        for c in range(3):
            exchange_ref[c, z] = out[c] / saturation[z]


def cross(first, second):
    return [
        first[1] * second[2] - first[2] * second[1],
        first[2] * second[0] - first[0] * second[2],
        first[0] * second[1] - first[1] * second[0],
    ]


def final_kernel(parts_ref, exchange_ref, unit_ref, field_ref, predicted_ref):
    depth, height, width = unit_ref.shape[1:]
    rows = depth * height
    unit, field = [], []
    for c in range(3):
        place = slice(c * rows, (c + 1) * rows)
        total = parts_ref[0, place]
        for index in range(1, parts_ref.shape[0]):
            total = total + parts_ref[index, place]
        field.append(exchange_ref[c] + total.reshape(depth, height, width))
        unit.append(unit_ref[c])
        field_ref[c] = field[c]
    twist = cross(unit, field)
    second = cross(unit, twist)
    moved = [
        unit[c] - (time_step / (1.0 + damping * damping)) * (twist[c] + damping * second[c])
        for c in range(3)
    ]
    length = jnp.sqrt(moved[0] * moved[0] + moved[1] * moved[1] + moved[2] * moved[2])
    for c in range(3):
        predicted_ref[c] = moved[c] / length


vmem = pl.BlockSpec(memory_space=pltpu.VMEM)
smem = pl.BlockSpec(memory_space=pltpu.SMEM)


def call(body, out, ins, operands, scratch=(), flops=0, name=None):
    size = sum(math.prod(o.shape) * o.dtype.itemsize for o in operands)
    outs = out if isinstance(out, (list, tuple)) else [out]
    size += sum(math.prod(o.shape) * o.dtype.itemsize for o in outs)
    return pl.pallas_call(
        body,
        out_shape=out,
        in_specs=ins,
        out_specs=jax.tree.map(lambda _: vmem, out),
        scratch_shapes=list(scratch),
        compiler_params=pltpu.CompilerParams(vmem_limit_bytes=16 << 20),
        cost_estimate=pl.CostEstimate(flops=flops, bytes_accessed=size, transcendentals=0),
        name=name,
    )(*operands)


def f32(*shape):
    return jax.ShapeDtypeStruct(shape, jnp.float32)


def per_device(theta, phi, labels, ms_region, aex_region, kernel):
    count_x, count_y = lax.axis_size("gx"), lax.axis_size("gy")
    gx, gy = lax.axis_index("gx"), lax.axis_index("gy")
    depth, height, width = theta.shape
    rows = kernel.shape[2]
    lanes = 2 * rows
    lines = 3 * depth * height
    whole_y = count_y * height

    packed, first, last = call(
        pack_kernel,
        [f32(count_x, 3, depth, height, width), f32(3, depth, width), f32(3, depth, width)],
        [vmem] * 3,
        (theta, phi, labels),
        name="pack",
    )
    gathered = lax.all_to_all(packed, "gx", split_axis=0, concat_axis=0, tiled=True)
    up = [(i, i + 1) for i in range(count_y - 1)]
    down = [(j, i) for i, j in up]
    before = lax.ppermute(last, "gy", up)
    after = lax.ppermute(first, "gy", down)

    table = line_table(count_x, count_y, width, rows)
    if table is None:
        table = line_table_here(count_x, count_y, width, rows)
    else:
        table = lax.dynamic_index_in_dim(jnp.asarray(table), gx, 0, keepdims=False)
    forward, inverse = column_tables(whole_y)

    twice = np.concatenate([np.eye(rows), np.eye(rows)], 1).astype(ml_dtypes.bfloat16)
    tensor = call(
        tensor_kernel,
        jax.ShapeDtypeStruct((48, 2 * whole_y, lanes), jnp.bfloat16),
        [vmem, vmem],
        (kernel.reshape(48, rows, 2 * whole_y), jnp.asarray(twice)),
        flops=48 * 2 * rows * lanes * 2 * whole_y,
        name="tensor",
    )
    spectrum = call(
        lines_kernel,
        f32(count_y, lines, lanes),
        [vmem, smem, vmem],
        (gathered, ms_region, table),
        flops=6 * lines * count_x * width * count_y * lanes,
        name="lines",
    )
    columns = lax.all_to_all(spectrum, "gy", split_axis=0, concat_axis=0, tiled=True)
    scale = -1.0 / (2 * depth * 2 * whole_y * 2 * count_x * width)
    waves = call(
        functools.partial(waves_kernel, scale),
        f32(count_y, lines, lanes),
        [vmem] * 4,
        (columns, tensor, jnp.asarray(forward), jnp.asarray(inverse)),
        scratch=(
            pltpu.VMEM((2 * whole_y, 3 * depth * lanes), jnp.float32),
            pltpu.VMEM((6 * whole_y, 3 * depth * lanes), jnp.bfloat16),
        ),
        flops=20 * whole_y * whole_y * 3 * depth * lanes,
        name="waves",
    )
    returned = lax.all_to_all(waves, "gy", split_axis=0, concat_axis=0, tiled=True)
    place = jnp.stack([gx, gy, jnp.int32(count_y)]).astype(jnp.int32)
    exchange, unit = call(
        exchange_kernel,
        [f32(3, depth, height, width), f32(3, depth, height, width)],
        [vmem, vmem, vmem, smem, smem, smem],
        (gathered, before, after, place, ms_region, aex_region),
        flops=300 * depth * height * width,
        name="exchange",
    )
    returned, exchange, unit = lax.optimization_barrier((returned, exchange, unit))
    partial = call(
        back_lines_kernel,
        f32(count_x, lines, width),
        [vmem, vmem],
        (returned, table),
        flops=6 * lines * count_x * width * count_y * lanes,
        name="back_lines",
    )
    parts = lax.all_to_all(partial, "gx", split_axis=0, concat_axis=0, tiled=True)
    field, predicted = call(
        final_kernel,
        [f32(3, depth, height, width), f32(3, depth, height, width)],
        [vmem] * 3,
        (parts, exchange, unit),
        flops=60 * depth * height * width,
        name="predict",
    )
    return field, predicted


def solution(mesh):
    in_specs = (
        P(None, "gy", "gx"),
        P(None, "gy", "gx"),
        P(None, "gy", "gx"),
        P(),
        P(),
        P(None, None, ("gx", "gy"), None),
    )
    out_specs = (P(None, None, "gy", "gx"), P(None, None, "gy", "gx"))
    return jax.shard_map(
        per_device, mesh=mesh, in_specs=in_specs, out_specs=out_specs, check_vma=False
    )
```

```python
import functools
import math

import jax
import jax.numpy as jnp
import ml_dtypes
import numpy as np
from jax import lax
from jax.experimental import pallas as pl
from jax.experimental.pallas import tpu as pltpu
from jax.sharding import PartitionSpec as P

damping = 0.5
time_step = 0.2
side_weight = 0.25
layer_weight = 0.5
root_half = math.sqrt(0.5)
constant_limit = 20 << 20


def split_high(value):
    high = value.astype(jnp.bfloat16)
    low = (value - high.astype(jnp.float32)).astype(jnp.bfloat16)
    return high, low


def split_table(table):
    high = table.astype(np.float32).astype(ml_dtypes.bfloat16)
    low = (table - high.astype(np.float64)).astype(np.float32).astype(ml_dtypes.bfloat16)
    return high, low


def dot(left, right, contract=((1,), (0,))):
    return lax.dot_general(left, right, (contract, ((), ())), preferred_element_type=jnp.float32)


def line_table(count_x, count_y, width, rows):
    cells = count_x * width
    if count_x * 2 * cells * count_y * 2 * rows * 2 > constant_limit:
        return None
    place = np.arange(cells)[None, :, None, None]
    wave = (
        np.arange(count_x)[:, None, None, None] * (count_y * rows)
        + np.arange(count_y)[None, None, :, None] * rows
        + np.arange(rows)[None, None, None, :]
    )
    angle = (place * wave % (2 * cells)) * (2.0 * math.pi / (2 * cells))
    table = np.stack([np.cos(angle), -np.sin(angle)], 3)
    table = table.reshape(count_x, count_x, width, count_y * 2 * rows)
    high, low = split_table(table)
    return np.stack([high, low], 1)


def line_table_here(count_x, count_y, width, rows):
    cells = count_x * width
    place = jnp.arange(cells, dtype=jnp.int32)[:, None, None]
    wave = (
        lax.axis_index("gx") * (count_y * rows)
        + jnp.arange(count_y, dtype=jnp.int32)[None, :, None] * rows
        + jnp.arange(rows, dtype=jnp.int32)[None, None, :]
    )
    angle = (place * wave % (2 * cells)).astype(jnp.float32) * (math.pi / cells)
    table = jnp.stack([jnp.cos(angle), -jnp.sin(angle)], 2).reshape(cells, count_y * 2 * rows)
    return jnp.stack(split_high(table)).reshape(1, 2, count_x, width, count_y * 2 * rows)


def column_tables(height):
    angle = (np.arange(2 * height)[:, None] * np.arange(height)[None, :] % (2 * height)) * (
        math.pi / height
    )
    high, low = split_table(np.concatenate([np.cos(angle), np.sin(angle)], 1))
    forward = np.concatenate([high, high, low], 1)
    high, low = split_table(np.concatenate([np.cos(angle.T), np.sin(angle.T)], 0))
    inverse = np.concatenate([high, high, low], 1)
    return forward, inverse


def sine_cosine(angle):
    turns = jnp.floor(angle * (2.0 / math.pi) + 0.5)
    rest = angle - turns * 1.5703125
    rest = rest - turns * 4.8351287841796875e-4
    rest = rest - turns * 3.1385570764541626e-7
    square = rest * rest
    sine = rest + rest * square * (
        -1.6666654611e-1 + square * (8.3321608736e-3 - square * 1.9515295891e-4)
    )
    cosine = (
        1.0
        - 0.5 * square
        + square * square * (4.166664568298827e-2 + square * (-1.388731625493765e-3 + square * 2.443315711809948e-5))
    )
    quarter = turns.astype(jnp.int32)
    odd = (quarter & 1) == 1
    out_sine = jnp.where(odd, cosine, sine)
    out_cosine = jnp.where(odd, sine, cosine)
    out_sine = jnp.where((quarter & 2) == 2, -out_sine, out_sine)
    out_cosine = jnp.where(((quarter + 1) & 2) == 2, -out_cosine, out_cosine)
    return out_sine, out_cosine


def directions(theta, phi):
    lateral, axial = sine_cosine(theta)
    sine, cosine = sine_cosine(phi)
    return [lateral * cosine, lateral * sine, axial]


def looked_up(labels, region):
    result = jnp.zeros_like(labels) + region[0]
    for index in range(1, region.shape[0]):
        result = jnp.where(labels == float(index), region[index], result)
    return result


def pack_kernel(theta_ref, phi_ref, labels_ref, raw_ref, first_ref, last_ref, angle, label, sems):
    height = theta_ref.shape[1]
    copies = [
        pltpu.make_async_copy(theta_ref, angle.at[0], sems.at[0]),
        pltpu.make_async_copy(phi_ref, angle.at[1], sems.at[1]),
        pltpu.make_async_copy(labels_ref, label, sems.at[2]),
    ]
    for copy in copies:
        copy.start()
    for copy in copies:
        copy.wait()
    for index, value in enumerate((angle[0], angle[1], label[...].astype(jnp.float32))):
        raw_ref[index] = value
        first_ref[index] = value[:, 0]
        last_ref[index] = value[:, height - 1]


def table_copies(table_ref, table, sems, gx):
    mine = gx if table_ref.shape[0] > 1 else 0
    copies = []
    for number in range(table_ref.shape[2]):
        block = lax.bitwise_xor(gx, number)
        copies.append(
            pltpu.make_async_copy(table_ref.at[mine, :, block], table.at[number], sems.at[number])
        )
    for copy in copies:
        copy.start()
    return copies


def lines_kernel(count_x, count_y, *refs):
    raw_refs, (region, place, table_ref) = refs[:count_x], refs[count_x : count_x + 3]
    out_refs = refs[count_x + 3 : count_x + 3 + count_y]
    table, ordered, sems = refs[count_x + 3 + count_y :]
    gx, gy = place[0], place[1]
    copies = table_copies(table_ref, table, sems, gx)
    halves = []
    for raw_ref in raw_refs:
        unit = directions(raw_ref[0], raw_ref[1])
        saturation = looked_up(raw_ref[2], region)
        rows = saturation.shape[0] * saturation.shape[1]
        block = jnp.concatenate([(part * saturation).reshape(rows, -1) for part in unit], 0)
        halves.append(split_high(block))
    lines = 3 * rows
    total = None
    for (high, low), copy, number in zip(halves, copies, range(count_x)):
        copy.wait()
        both = dot(jnp.concatenate([high, low], 0), table[number, 0])
        part = both[:lines] + both[lines:] + dot(high, table[number, 1])
        total = part if total is None else total + part
    lanes = ordered.shape[2]
    for index in range(count_y):
        ordered[index] = total[:, index * lanes : (index + 1) * lanes]
    for number in range(count_y):
        out_refs[number][...] = ordered[lax.bitwise_xor(gy, number)]


def back_lines_kernel(count_x, count_y, *refs):
    in_refs, (place, table_ref) = refs[:count_y], refs[count_y : count_y + 2]
    out_refs = refs[count_y + 2 : count_y + 2 + count_x]
    table, ordered, sems = refs[count_y + 2 + count_x :]
    gx, gy = place[0], place[1]
    copies = table_copies(table_ref, table, sems, gx)
    for number in range(count_y):
        ordered[lax.bitwise_xor(gy, number)] = in_refs[number][...]
    high, low = split_high(jnp.concatenate([ordered[g] for g in range(count_y)], 1))
    both = jnp.concatenate([high, low], 0)
    lines = high.shape[0]
    for number in range(count_x):
        copies[number].wait()
        wide = dot(both, table[number, 0], ((1,), (1,)))
        out_refs[number][...] = (
            wide[:lines] + wide[lines:] + dot(high, table[number, 1], ((1,), (1,)))
        )


def tensor_kernel(kernel_ref, twice_ref, out_ref):
    twice = twice_ref[...]

    unroll = 8

    def step(index, carry):
        for offset in range(unroll):
            turned = dot(kernel_ref[index * unroll + offset], twice, ((0,), (0,)))
            out_ref[index * unroll + offset] = turned.astype(jnp.bfloat16)
        return carry

    lax.fori_loop(0, kernel_ref.shape[0] // unroll, step, 0)


def turn(value, sign):
    lanes = value.shape[-1]
    if lanes == 128:
        return pltpu.roll(value, lanes // 2, value.ndim - 1) * sign
    return jnp.concatenate([value[..., lanes // 2 :], value[..., : lanes // 2]], -1) * sign


def layers_forward(layer, sign):
    d0, d1, d2, d3 = layer
    r2 = turn(d2, sign)
    near, far = d1 + d3, d1 - d3
    far_turned = turn(far, sign)
    near_turned = turn(near, sign)
    even, odd = d0 + d2, d0 - d2
    out = [None] * 8
    out[0], out[4] = even + near, even - near
    out[2], out[6] = odd + far_turned, odd - far_turned
    plus, minus = d0 + r2, d0 - r2
    first = (far + near_turned) * root_half
    second = (near_turned - far) * root_half
    out[1], out[5] = plus + first, plus - first
    out[3], out[7] = minus + second, minus - second
    return out


def layers_inverse(wave, sign):
    a, b = wave[0] + wave[4], wave[0] - wave[4]
    e, f = wave[2] + wave[6], turn(wave[2] - wave[6], sign)
    p, q = wave[1] + wave[5], wave[1] - wave[5]
    s, t = wave[3] + wave[7], turn(wave[3] - wave[7], sign)
    o0, o1, o2, o3 = p + s, q - t, p - s, q + t
    return [
        a + e + o0,
        b - f + (o1 - turn(o1, sign)) * root_half,
        a - e - turn(o2, sign),
        b + f - (o3 + turn(o3, sign)) * root_half,
    ]


def apply_tensor(tensor, wave):
    out = [[], [], []]
    for level in range(8):
        xx, yy, zz, xy, xz, yz = [tensor[part][level] for part in range(6)]
        x, y, z = wave[0][level], wave[1][level], wave[2][level]
        out[0].append(xx * x + xy * y + xz * z)
        out[1].append(xy * x + yy * y + yz * z)
        out[2].append(xz * x + yz * y + zz * z)
    return out


def waves_kernel(scale, count_y, *refs):
    spec_refs, (place, tensor_ref, forward_ref, inverse_ref) = refs[:count_y], refs[count_y : count_y + 4]
    out_refs = refs[count_y + 4 : 2 * count_y + 4]
    ordered, wave_ref, back_ref = refs[2 * count_y + 4 :]
    gy = place[1]
    lines, lanes = spec_refs[0].shape
    for number in range(count_y):
        ordered[lax.bitwise_xor(gy, number)] = spec_refs[number][...]
    local = 8
    planes = lines // local
    height = count_y * local
    sign = jnp.where(
        lax.broadcasted_iota(jnp.int32, (1, lanes), 1) < lanes // 2, 1.0, -1.0
    ).astype(jnp.float32)
    columns = []
    for plane in range(planes):
        value = ordered[:, plane * local : (plane + 1) * local, :].reshape(height, lanes)
        value = jnp.concatenate([value, turn(value, sign)], 0)
        high, low = split_high(value)
        columns.append(jnp.concatenate([high, low, high], 0))
    wave_ref[...] = dot(forward_ref[...], jnp.concatenate(columns, 1))

    chunk = 16
    depth = planes // 3
    double = 2 * height

    def step(index, carry):
        rows = pl.ds(pl.multiple_of(index * chunk, chunk), chunk)
        wave = []
        for part in range(3):
            layer = [
                wave_ref[rows, (part * depth + z) * lanes : (part * depth + z + 1) * lanes]
                for z in range(depth)
            ]
            wave.append(layers_forward(layer, sign))
        tensor = [
            [tensor_ref[part * 8 + level, rows, :].astype(jnp.float32) for level in range(8)]
            for part in range(6)
        ]
        image = apply_tensor(tensor, wave)
        for part in range(3):
            layer = layers_inverse(image[part], sign)
            for z in range(depth):
                spot = slice((part * depth + z) * lanes, (part * depth + z + 1) * lanes)
                high, low = split_high(layer[z] * scale)
                back_ref[rows, spot] = high
                back_ref[pl.ds(pl.multiple_of(double + index * chunk, chunk), chunk), spot] = low
                back_ref[pl.ds(pl.multiple_of(2 * double + index * chunk, chunk), chunk), spot] = high
        return carry

    lax.fori_loop(0, double // chunk, step, 0)
    back = dot(inverse_ref[...], back_ref[...])
    for plane in range(planes):
        part = slice(plane * lanes, (plane + 1) * lanes)
        value = back[:height, part] - turn(back[height:, part], sign)
        ordered[:, plane * local : (plane + 1) * local, :] = value.reshape(count_y, local, lanes)
    for number in range(count_y):
        out_refs[number][...] = ordered[lax.bitwise_xor(gy, number)]


def exchange_kernel(count_x, count_y, *refs):
    raw_refs, (before_ref, after_ref, place, ms_ref, aex_ref) = refs[:count_x], refs[count_x : count_x + 5]
    exchange_ref, unit_ref, raw_ref = refs[count_x + 5 :]
    depth, height, width = raw_ref.shape[2:]
    gx, gy = place[0], place[1]
    for number in range(count_x):
        raw_ref[lax.bitwise_xor(gx, number)] = raw_refs[number][...]
    left, right = jnp.maximum(gx - 1, 0), jnp.minimum(gx + 1, count_x - 1)
    shape = (depth, height, width)
    lane = lax.broadcasted_iota(jnp.int32, shape, 2)
    row = lax.broadcasted_iota(jnp.int32, shape, 1)

    def quantities(values):
        return directions(values[0], values[1]) + [looked_up(values[2], aex_ref)]

    raw = [raw_refs[0][f] for f in range(3)]
    here = quantities(raw)
    side = quantities([jnp.where(lane == 0, raw_ref[right, f], raw_ref[left, f]) for f in range(3)])
    above = quantities(
        [
            jnp.where(
                row == 0,
                jnp.broadcast_to(after_ref[f][:, None, :], shape),
                jnp.broadcast_to(before_ref[f][:, None, :], shape),
            )
            for f in range(3)
        ]
    )
    saturation = looked_up(raw[2], ms_ref)
    total = [jnp.zeros(shape, jnp.float32) for _ in range(3)]

    def add(total, beside, weight):
        coupling = 2.0 * here[3] * beside[3] / (here[3] + beside[3]) * weight
        return [total[c] + coupling * (beside[c] - here[c]) for c in range(3)]

    one = jnp.float32(1.0)
    zero = jnp.float32(0.0)
    for shift, edge, there in ((1, 0, gx > 0), (width - 1, width - 1, gx < count_x - 1)):
        beside = [
            jnp.where(lane == edge, pltpu.roll(s, shift, 2), pltpu.roll(h, shift, 2))
            for s, h in zip(side, here)
        ]
        weight = jnp.where(lane == edge, jnp.where(there, one, zero), one) * side_weight
        total = add(total, beside, weight)
    for shift, edge, there in ((1, 0, gy > 0), (height - 1, height - 1, gy < count_y - 1)):
        beside = [
            jnp.where(row == edge, pltpu.roll(s, shift, 1), pltpu.roll(h, shift, 1))
            for s, h in zip(above, here)
        ]
        weight = jnp.where(row == edge, jnp.where(there, one, zero), one) * side_weight
        total = add(total, beside, weight)
    for part in range(3):
        unit_ref[part] = here[part]
    for z in range(depth):
        out = [total[c][z] for c in range(3)]
        for other in (z - 1, z + 1):
            if 0 <= other < depth:
                a, b = here[3][z], here[3][other]
                coupling = 2.0 * a * b / (a + b) * layer_weight
                out = [out[c] + coupling * (here[c][other] - here[c][z]) for c in range(3)]
        for c in range(3):
            exchange_ref[c, z] = out[c] / saturation[z]


def cross(first, second):
    return [
        first[1] * second[2] - first[2] * second[1],
        first[2] * second[0] - first[0] * second[2],
        first[0] * second[1] - first[1] * second[0],
    ]


def final_kernel(count_x, *refs):
    part_refs, (exchange_ref, unit_ref, field_ref, predicted_ref) = refs[:count_x], refs[count_x:]
    depth, height, width = unit_ref.shape[1:]
    rows = depth * height
    unit, field = [], []
    for c in range(3):
        place = slice(c * rows, (c + 1) * rows)
        total = part_refs[0][place]
        for part_ref in part_refs[1:]:
            total = total + part_ref[place]
        field.append(exchange_ref[c] + total.reshape(depth, height, width))
        unit.append(unit_ref[c])
        field_ref[c] = field[c]
    twist = cross(unit, field)
    second = cross(unit, twist)
    moved = [
        unit[c] - (time_step / (1.0 + damping * damping)) * (twist[c] + damping * second[c])
        for c in range(3)
    ]
    length = jnp.sqrt(moved[0] * moved[0] + moved[1] * moved[1] + moved[2] * moved[2])
    for c in range(3):
        predicted_ref[c] = moved[c] / length


vmem = pl.BlockSpec(memory_space=pltpu.VMEM)
smem = pl.BlockSpec(memory_space=pltpu.SMEM)
hbm = pl.BlockSpec(memory_space=pltpu.HBM)


def call(body, out, ins, operands, scratch=(), flops=0, name=None, grant=16 << 20):
    operands = [
        pltpu.with_memory_space_constraint(o, pltpu.HBM) if i is hbm else o
        for i, o in zip(ins, operands)
    ]
    size = sum(math.prod(o.shape) * o.dtype.itemsize for o in operands)
    outs = out if isinstance(out, (list, tuple)) else [out]
    size += sum(math.prod(o.shape) * o.dtype.itemsize for o in outs)
    return pl.pallas_call(
        body,
        out_shape=out,
        in_specs=ins,
        out_specs=jax.tree.map(lambda _: vmem, out),
        scratch_shapes=list(scratch),
        compiler_params=pltpu.CompilerParams(vmem_limit_bytes=grant),
        cost_estimate=pl.CostEstimate(flops=flops, bytes_accessed=size, transcendentals=0),
        name=name,
    )(*operands)


def f32(*shape):
    return jax.ShapeDtypeStruct(shape, jnp.float32)


def exchanged(chunks, axis):
    devices = lax.axis_size(axis)
    out = [chunks[0]] + [None] * (devices - 1)
    for number in reversed(range(1, devices)):
        pairs = [(i, i ^ number) for i in range(devices)]
        out[number] = lax.ppermute(chunks[number], axis, pairs)
    return out


def per_device(theta, phi, labels, ms_region, aex_region, kernel):
    count_x, count_y = lax.axis_size("gx"), lax.axis_size("gy")
    gx, gy = lax.axis_index("gx"), lax.axis_index("gy")
    depth, height, width = theta.shape
    rows = kernel.shape[2]
    lanes = 2 * rows
    lines = 3 * depth * height
    whole_y = count_y * height

    place = jnp.stack([gx, gy]).astype(jnp.int32)
    cells = f32(3, depth, height, width)
    table = line_table(count_x, count_y, width, rows)
    if table is None:
        table = line_table_here(count_x, count_y, width, rows)
    table = jnp.asarray(table)
    forward, inverse = column_tables(whole_y)
    twice = np.concatenate([np.eye(rows), np.eye(rows)], 1).astype(ml_dtypes.bfloat16)
    table_scratch = pltpu.VMEM((count_x, 2, width, count_y * lanes), jnp.bfloat16)
    ordered = pltpu.VMEM((count_y, lines, lanes), jnp.float32)
    table_grant = (12 << 20) + 5 * math.prod(table_scratch.shape)
    table_sems = pltpu.SemaphoreType.DMA((count_x,))
    transform_flops = 6 * lines * count_x * width * count_y * lanes

    packed, first, last = call(
        pack_kernel,
        [cells, f32(3, depth, width), f32(3, depth, width)],
        [hbm] * 3,
        (theta, phi, labels),
        scratch=(
            pltpu.VMEM((2, depth, height, width), jnp.float32),
            pltpu.VMEM((depth, height, width), jnp.int32),
            pltpu.SemaphoreType.DMA((3,)),
        ),
        name="pack",
    )
    gathered = exchanged([packed] * count_x, "gx")
    up = [(i, i + 1) for i in range(count_y - 1)]
    down = [(j, i) for i, j in up]
    before = lax.ppermute(last, "gy", up)
    after = lax.ppermute(first, "gy", down)

    tensor = call(
        tensor_kernel,
        jax.ShapeDtypeStruct((48, 2 * whole_y, lanes), jnp.bfloat16),
        [vmem, vmem],
        (kernel.reshape(48, rows, 2 * whole_y), jnp.asarray(twice)),
        flops=48 * 2 * rows * lanes * 2 * whole_y,
        name="tensor",
    )
    spectrum = call(
        functools.partial(lines_kernel, count_x, count_y),
        [f32(lines, lanes)] * count_y,
        [vmem] * count_x + [smem, smem, hbm],
        (*gathered, ms_region, place, table),
        scratch=(table_scratch, ordered, table_sems),
        grant=table_grant,
        flops=transform_flops,
        name="lines",
    )
    columns = exchanged(spectrum, "gy")
    exchange, unit = call(
        functools.partial(exchange_kernel, count_x, count_y),
        [cells, cells],
        [vmem] * (count_x + 2) + [smem] * 3,
        (*gathered, before, after, place, ms_region, aex_region),
        scratch=(pltpu.VMEM((count_x, 3, depth, height, width), jnp.float32),),
        flops=300 * depth * height * width,
        name="exchange",
    )
    columns, exchange, unit = lax.optimization_barrier((columns, exchange, unit))
    scale = -1.0 / (2 * depth * 2 * whole_y * 2 * count_x * width)
    waves = call(
        functools.partial(waves_kernel, scale, count_y),
        [f32(lines, lanes)] * count_y,
        [vmem] * count_y + [smem] + [vmem] * 3,
        (*columns, place, tensor, jnp.asarray(forward), jnp.asarray(inverse)),
        scratch=(
            ordered,
            pltpu.VMEM((2 * whole_y, 3 * depth * lanes), jnp.float32),
            pltpu.VMEM((6 * whole_y, 3 * depth * lanes), jnp.bfloat16),
        ),
        flops=20 * whole_y * whole_y * 3 * depth * lanes,
        name="waves",
    )
    returned = exchanged(waves, "gy")
    partial = call(
        functools.partial(back_lines_kernel, count_x, count_y),
        [f32(lines, width)] * count_x,
        [vmem] * count_y + [smem, hbm],
        (*returned, place, table),
        scratch=(table_scratch, ordered, table_sems),
        grant=table_grant,
        flops=transform_flops,
        name="back_lines",
    )
    parts = exchanged(partial, "gx")
    field, predicted = call(
        functools.partial(final_kernel, count_x),
        [cells, cells],
        [vmem] * (count_x + 2),
        (*parts, exchange, unit),
        flops=60 * depth * height * width,
        name="predict",
    )
    return field, predicted


def solution(mesh):
    in_specs = (
        P(None, "gy", "gx"),
        P(None, "gy", "gx"),
        P(None, "gy", "gx"),
        P(),
        P(),
        P(None, None, ("gx", "gy"), None),
    )
    out_specs = (P(None, None, "gy", "gx"), P(None, None, "gy", "gx"))
    return jax.shard_map(
        per_device, mesh=mesh, in_specs=in_specs, out_specs=out_specs, check_vma=False
    )
```

```python
import functools
import math

import jax
import jax.numpy as jnp
import ml_dtypes
import numpy as np
from jax import lax
from jax.experimental import pallas as pl
from jax.experimental.pallas import tpu as pltpu
from jax.sharding import PartitionSpec as P

damping = 0.5
time_step = 0.2
side_weight = 0.25
layer_weight = 0.5
root_half = math.sqrt(0.5)
constant_limit = 20 << 20


def split_high(value):
    high = value.astype(jnp.bfloat16)
    low = (value - high.astype(jnp.float32)).astype(jnp.bfloat16)
    return high, low


def split_table(table):
    high = table.astype(np.float32).astype(ml_dtypes.bfloat16)
    low = (table - high.astype(np.float64)).astype(np.float32).astype(ml_dtypes.bfloat16)
    return high, low


def dot(left, right, contract=((1,), (0,))):
    return lax.dot_general(left, right, (contract, ((), ())), preferred_element_type=jnp.float32)


def line_table(count_x, count_y, width, rows):
    cells = count_x * width
    if count_x * 2 * cells * count_y * 2 * rows * 2 > constant_limit:
        return None
    place = np.arange(cells)[None, None, :, None]
    wave = (
        np.arange(count_x)[:, None, None, None] * (count_y * rows)
        + np.arange(count_y)[None, :, None, None] * rows
        + np.arange(rows)[None, None, None, :]
    )
    angle = (place * wave % (2 * cells)) * (2.0 * math.pi / (2 * cells))
    table = np.concatenate([np.cos(angle), -np.sin(angle)], 3)
    table = table.reshape(count_x, count_y, count_x, width, 2 * rows)
    high, low = split_table(table)
    return np.stack([high, low], 2)


def line_table_here(count_x, width, rows, order):
    cells = count_x * width
    count_y = len(order)
    place = jnp.arange(cells, dtype=jnp.int32)[:, None, None]
    block = lax.bitwise_xor(lax.axis_index("gy"), jnp.array(order, jnp.int32))
    wave = (
        lax.axis_index("gx") * (count_y * rows)
        + block[None, :, None] * rows
        + jnp.arange(rows, dtype=jnp.int32)[None, None, :]
    )
    angle = (place * wave % (2 * cells)).astype(jnp.float32) * (math.pi / cells)
    table = jnp.concatenate([jnp.cos(angle), -jnp.sin(angle)], 2)
    table = table.reshape(1, 1, count_x, width, count_y * 2 * rows)
    return jnp.stack(split_high(table), 2)


def column_tables(count_y, local, order):
    height = count_y * local
    wave = np.arange(2 * height)
    block = np.arange(count_y)[:, None] ^ np.array(order)[None, :]
    place = (block[:, :, None] * local + np.arange(local)).reshape(count_y, height)
    angle = (wave[None, :, None] * place[:, None, :] % (2 * height)) * (math.pi / height)
    high, low = split_table(np.concatenate([np.cos(angle), np.sin(angle)], 2))
    forward = np.concatenate([high, high, low], 2)
    angle = angle.transpose(0, 2, 1)
    high, low = split_table(np.concatenate([np.cos(angle), np.sin(angle)], 1))
    inverse = np.concatenate([high, high, low], 2)
    return forward, inverse


def column_tables_here(count_y, local, order):
    height = count_y * local
    wave = jnp.arange(2 * height, dtype=jnp.int32)
    block = lax.bitwise_xor(lax.axis_index("gy"), jnp.array(order, jnp.int32))
    place = (block[:, None] * local + jnp.arange(local, dtype=jnp.int32)).reshape(height)
    angle = (wave[:, None] * place % (2 * height)).astype(jnp.float32) * (math.pi / height)
    high, low = split_high(jnp.concatenate([jnp.cos(angle), jnp.sin(angle)], 1))
    forward = jnp.concatenate([high, high, low], 1)
    high, low = split_high(jnp.concatenate([jnp.cos(angle.T), jnp.sin(angle.T)], 0))
    inverse = jnp.concatenate([high, high, low], 1)
    return forward[None], inverse[None]


def load_kernel(order_x, order_y, place, *refs):
    table_ref, forward_ref, inverse_ref, table, forward, inverse, sem = refs
    gx, gy = place[0], place[1]
    mine_x = gx if table_ref.shape[0] > 1 else 0
    mine_y = gy if forward_ref.shape[0] > 1 else 0
    lanes = table_ref.shape[5]
    copies = [
        pltpu.make_async_copy(forward_ref.at[mine_y], forward, sem.at[0]),
        pltpu.make_async_copy(inverse_ref.at[mine_y], inverse, sem.at[1]),
    ]
    for spot_x, number_x in enumerate(order_x):
        block_x = lax.bitwise_xor(gx, number_x)
        for spot_y in range(table_ref.shape[1]):
            block_y = lax.bitwise_xor(gy, order_y[spot_y]) if table_ref.shape[1] > 1 else 0
            columns = slice(spot_y * lanes, (spot_y + 1) * lanes)
            copies.append(
                pltpu.make_async_copy(
                    table_ref.at[mine_x, block_y, :, block_x],
                    table.at[:, spot_x, :, columns],
                    sem.at[len(copies)],
                )
            )
    for copy in copies:
        copy.start()
    for copy in copies:
        copy.wait()


def sine_cosine(angle):
    turns = jnp.floor(angle * (2.0 / math.pi) + 0.5)
    rest = angle - turns * 1.5703125
    rest = rest - turns * 4.8351287841796875e-4
    rest = rest - turns * 3.1385570764541626e-7
    square = rest * rest
    sine = rest + rest * square * (
        -1.6666654611e-1 + square * (8.3321608736e-3 - square * 1.9515295891e-4)
    )
    cosine = (
        1.0
        - 0.5 * square
        + square * square * (4.166664568298827e-2 + square * (-1.388731625493765e-3 + square * 2.443315711809948e-5))
    )
    quarter = turns.astype(jnp.int32)
    odd = (quarter & 1) == 1
    out_sine = jnp.where(odd, cosine, sine)
    out_cosine = jnp.where(odd, sine, cosine)
    out_sine = jnp.where((quarter & 2) == 2, -out_sine, out_sine)
    out_cosine = jnp.where(((quarter + 1) & 2) == 2, -out_cosine, out_cosine)
    return out_sine, out_cosine


def directions(theta, phi):
    lateral, axial = sine_cosine(theta)
    sine, cosine = sine_cosine(phi)
    return [lateral * cosine, lateral * sine, axial]


def looked_up(labels, region):
    result = jnp.zeros_like(labels) + region[0]
    for index in range(1, region.shape[0]):
        result = jnp.where(labels == float(index), region[index], result)
    return result


def pack_kernel(theta_ref, phi_ref, labels_ref, raw_ref, first_ref, last_ref, angle, label, sems):
    height = theta_ref.shape[1]
    copies = [
        pltpu.make_async_copy(theta_ref, angle.at[0], sems.at[0]),
        pltpu.make_async_copy(phi_ref, angle.at[1], sems.at[1]),
        pltpu.make_async_copy(labels_ref, label, sems.at[2]),
    ]
    for copy in copies:
        copy.start()
    for copy in copies:
        copy.wait()
    for index, value in enumerate((angle[0], angle[1], label[...].astype(jnp.float32))):
        raw_ref[index] = value
        first_ref[index] = value[:, 0]
        last_ref[index] = value[:, height - 1]


def lines_kernel(count_x, count_y, *refs):
    raw_refs, (region_ref, table) = refs[:count_x], refs[count_x : count_x + 2]
    out_refs, (region, sem) = refs[count_x + 2 : -2], refs[-2:]
    fetch = pltpu.make_async_copy(region_ref, region, sem)
    fetch.start()
    units = [directions(raw_ref[0], raw_ref[1]) for raw_ref in raw_refs]
    fetch.wait()
    total = None
    for number in range(count_x):
        saturation = looked_up(raw_refs[number][2], region)
        rows = saturation.shape[0] * saturation.shape[1]
        block = [(part * saturation).reshape(rows, -1) for part in units[number]]
        high, low = split_high(jnp.concatenate(block, 0))
        both = dot(jnp.concatenate([high, low], 0), table[0, number])
        part = both[: 3 * rows] + both[3 * rows :] + dot(high, table[1, number])
        total = part if total is None else total + part
    lanes = out_refs[0].shape[1]
    for number in range(count_y):
        out_refs[number][...] = total[:, number * lanes : (number + 1) * lanes]


def back_lines_kernel(count_x, count_y, *refs):
    in_refs, table, out_refs = refs[:count_y], refs[count_y], refs[count_y + 1 :]
    high, low = split_high(jnp.concatenate([ref[...] for ref in in_refs], 1))
    both = jnp.concatenate([high, low], 0)
    lines = high.shape[0]
    for number in range(count_x):
        wide = dot(both, table[0, number], ((1,), (1,)))
        out_refs[number][...] = (
            wide[:lines] + wide[lines:] + dot(high, table[1, number], ((1,), (1,)))
        )


def tensor_kernel(kernel_ref, twice_ref, out_ref):
    twice = twice_ref[...]

    unroll = 8

    def step(index, carry):
        for offset in range(unroll):
            turned = dot(kernel_ref[index * unroll + offset], twice, ((0,), (0,)))
            out_ref[index * unroll + offset] = turned.astype(jnp.bfloat16)
        return carry

    lax.fori_loop(0, kernel_ref.shape[0] // unroll, step, 0)


def turn(value, sign):
    lanes = value.shape[-1]
    if lanes == 128:
        return pltpu.roll(value, lanes // 2, value.ndim - 1) * sign
    return jnp.concatenate([value[..., lanes // 2 :], value[..., : lanes // 2]], -1) * sign


def layers_forward(layer, sign):
    d0, d1, d2, d3 = layer
    r2 = turn(d2, sign)
    near, far = d1 + d3, d1 - d3
    far_turned = turn(far, sign)
    near_turned = turn(near, sign)
    even, odd = d0 + d2, d0 - d2
    out = [None] * 8
    out[0], out[4] = even + near, even - near
    out[2], out[6] = odd + far_turned, odd - far_turned
    plus, minus = d0 + r2, d0 - r2
    first = (far + near_turned) * root_half
    second = (near_turned - far) * root_half
    out[1], out[5] = plus + first, plus - first
    out[3], out[7] = minus + second, minus - second
    return out


def layers_inverse(wave, sign):
    a, b = wave[0] + wave[4], wave[0] - wave[4]
    e, f = wave[2] + wave[6], turn(wave[2] - wave[6], sign)
    p, q = wave[1] + wave[5], wave[1] - wave[5]
    s, t = wave[3] + wave[7], turn(wave[3] - wave[7], sign)
    o0, o1, o2, o3 = p + s, q - t, p - s, q + t
    return [
        a + e + o0,
        b - f + (o1 - turn(o1, sign)) * root_half,
        a - e - turn(o2, sign),
        b + f - (o3 + turn(o3, sign)) * root_half,
    ]


def apply_tensor(tensor, wave):
    out = [[], [], []]
    for level in range(8):
        xx, yy, zz, xy, xz, yz = [tensor[part][level] for part in range(6)]
        x, y, z = wave[0][level], wave[1][level], wave[2][level]
        out[0].append(xx * x + xy * y + xz * z)
        out[1].append(xy * x + yy * y + yz * z)
        out[2].append(xz * x + yz * y + zz * z)
    return out


def waves_kernel(scale, count_y, *refs):
    spec_refs, (tensor_ref, forward_ref, inverse_ref) = refs[:count_y], refs[count_y : count_y + 3]
    out_refs, (wave_ref, back_ref) = refs[count_y + 3 : -2], refs[-2:]
    lines, lanes = spec_refs[0].shape
    local = 8
    planes = lines // local
    height = count_y * local
    sign = jnp.where(
        lax.broadcasted_iota(jnp.int32, (1, lanes), 1) < lanes // 2, 1.0, -1.0
    ).astype(jnp.float32)
    columns = []
    for plane in range(planes):
        value = jnp.concatenate(
            [ref[plane * local : (plane + 1) * local] for ref in spec_refs], 0
        )
        value = jnp.concatenate([value, turn(value, sign)], 0)
        high, low = split_high(value)
        columns.append(jnp.concatenate([high, low, high], 0))
    wave_ref[...] = dot(forward_ref[...], jnp.concatenate(columns, 1))

    chunk = 16
    depth = planes // 3
    double = 2 * height

    def step(index, carry):
        rows = pl.ds(pl.multiple_of(index * chunk, chunk), chunk)
        wave = []
        for part in range(3):
            layer = [
                wave_ref[rows, (part * depth + z) * lanes : (part * depth + z + 1) * lanes]
                for z in range(depth)
            ]
            wave.append(layers_forward(layer, sign))
        tensor = [
            [tensor_ref[part * 8 + level, rows, :].astype(jnp.float32) for level in range(8)]
            for part in range(6)
        ]
        image = apply_tensor(tensor, wave)
        for part in range(3):
            layer = layers_inverse(image[part], sign)
            for z in range(depth):
                spot = slice((part * depth + z) * lanes, (part * depth + z + 1) * lanes)
                high, low = split_high(layer[z] * scale)
                back_ref[rows, spot] = high
                back_ref[pl.ds(pl.multiple_of(double + index * chunk, chunk), chunk), spot] = low
                back_ref[pl.ds(pl.multiple_of(2 * double + index * chunk, chunk), chunk), spot] = high
        return carry

    lax.fori_loop(0, double // chunk, step, 0)
    back = dot(inverse_ref[...], back_ref[...])
    for plane in range(planes):
        part = slice(plane * lanes, (plane + 1) * lanes)
        value = back[:height, part] - turn(back[height:, part], sign)
        for number in range(count_y):
            out_refs[number][plane * local : (plane + 1) * local] = value[
                number * local : (number + 1) * local
            ]


def exchange_kernel(order_x, count_y, *refs):
    count_x = len(order_x)
    raw_refs, (before_ref, after_ref, place, ms_ref, aex_ref) = refs[:count_x], refs[count_x : count_x + 5]
    exchange_ref, unit_ref, raw_ref = refs[count_x + 5 :]
    depth, height, width = raw_ref.shape[2:]
    gx, gy = place[0], place[1]
    for spot, number in enumerate(order_x):
        raw_ref[lax.bitwise_xor(gx, number)] = raw_refs[spot][...]
    left, right = jnp.maximum(gx - 1, 0), jnp.minimum(gx + 1, count_x - 1)
    shape = (depth, height, width)
    lane = lax.broadcasted_iota(jnp.int32, shape, 2)
    row = lax.broadcasted_iota(jnp.int32, shape, 1)

    def quantities(values):
        return directions(values[0], values[1]) + [looked_up(values[2], aex_ref)]

    raw = [raw_refs[0][f] for f in range(3)]
    here = quantities(raw)
    side = quantities([jnp.where(lane == 0, raw_ref[right, f], raw_ref[left, f]) for f in range(3)])
    above = quantities(
        [
            jnp.where(
                row == 0,
                jnp.broadcast_to(after_ref[f][:, None, :], shape),
                jnp.broadcast_to(before_ref[f][:, None, :], shape),
            )
            for f in range(3)
        ]
    )
    saturation = looked_up(raw[2], ms_ref)
    total = [jnp.zeros(shape, jnp.float32) for _ in range(3)]

    def add(total, beside, weight):
        coupling = 2.0 * here[3] * beside[3] / (here[3] + beside[3]) * weight
        return [total[c] + coupling * (beside[c] - here[c]) for c in range(3)]

    one = jnp.float32(1.0)
    zero = jnp.float32(0.0)
    for shift, edge, there in ((1, 0, gx > 0), (width - 1, width - 1, gx < count_x - 1)):
        beside = [
            jnp.where(lane == edge, pltpu.roll(s, shift, 2), pltpu.roll(h, shift, 2))
            for s, h in zip(side, here)
        ]
        weight = jnp.where(lane == edge, jnp.where(there, one, zero), one) * side_weight
        total = add(total, beside, weight)
    for shift, edge, there in ((1, 0, gy > 0), (height - 1, height - 1, gy < count_y - 1)):
        beside = [
            jnp.where(row == edge, pltpu.roll(s, shift, 1), pltpu.roll(h, shift, 1))
            for s, h in zip(above, here)
        ]
        weight = jnp.where(row == edge, jnp.where(there, one, zero), one) * side_weight
        total = add(total, beside, weight)
    for part in range(3):
        unit_ref[part] = here[part]
    for z in range(depth):
        out = [total[c][z] for c in range(3)]
        for other in (z - 1, z + 1):
            if 0 <= other < depth:
                a, b = here[3][z], here[3][other]
                coupling = 2.0 * a * b / (a + b) * layer_weight
                out = [out[c] + coupling * (here[c][other] - here[c][z]) for c in range(3)]
        for c in range(3):
            exchange_ref[c, z] = out[c] / saturation[z]


def cross(first, second):
    return [
        first[1] * second[2] - first[2] * second[1],
        first[2] * second[0] - first[0] * second[2],
        first[0] * second[1] - first[1] * second[0],
    ]


def final_kernel(count_x, *refs):
    part_refs, (exchange_ref, unit_ref, field_ref, predicted_ref) = refs[:count_x], refs[count_x:]
    depth, height, width = unit_ref.shape[1:]
    rows = depth * height
    unit, field = [], []
    for c in range(3):
        place = slice(c * rows, (c + 1) * rows)
        total = part_refs[0][place]
        for part_ref in part_refs[1:]:
            total = total + part_ref[place]
        field.append(exchange_ref[c] + total.reshape(depth, height, width))
        unit.append(unit_ref[c])
        field_ref[c] = field[c]
    twist = cross(unit, field)
    second = cross(unit, twist)
    moved = [
        unit[c] - (time_step / (1.0 + damping * damping)) * (twist[c] + damping * second[c])
        for c in range(3)
    ]
    length = jnp.sqrt(moved[0] * moved[0] + moved[1] * moved[1] + moved[2] * moved[2])
    for c in range(3):
        predicted_ref[c] = moved[c] / length


vmem = pl.BlockSpec(memory_space=pltpu.VMEM)
smem = pl.BlockSpec(memory_space=pltpu.SMEM)
hbm = pl.BlockSpec(memory_space=pltpu.HBM)


def call(body, out, ins, operands, scratch=(), flops=0, name=None, grant=16 << 20):
    operands = [
        pltpu.with_memory_space_constraint(o, pltpu.HBM) if i is hbm else o
        for i, o in zip(ins, operands)
    ]
    size = sum(math.prod(o.shape) * o.dtype.itemsize for o in operands)
    outs = out if isinstance(out, (list, tuple)) else [out]
    size += sum(math.prod(o.shape) * jnp.dtype(o.dtype).itemsize for o in outs)
    return pl.pallas_call(
        body,
        out_shape=out,
        in_specs=ins,
        out_specs=[vmem] * len(outs) if outs is out else vmem,
        scratch_shapes=list(scratch),
        compiler_params=pltpu.CompilerParams(vmem_limit_bytes=grant),
        cost_estimate=pl.CostEstimate(flops=flops, bytes_accessed=size, transcendentals=0),
        name=name,
    )(*operands)


def f32(*shape):
    return jax.ShapeDtypeStruct(shape, jnp.float32)


def exchanged(chunks, axis, order):
    devices = len(order)
    out = [chunks[0]] + [None] * (devices - 1)
    for spot, number in enumerate(order[1:]):
        pairs = [(i, i ^ number) for i in range(devices)]
        out[spot + 1] = lax.ppermute(chunks[spot + 1], axis, pairs)
    return out


def partners(devices):
    return [0] + list(range(devices - 1, 0, -1))


def per_device(theta, phi, labels, ms_region, aex_region, kernel):
    count_x, count_y = lax.axis_size("gx"), lax.axis_size("gy")
    gx, gy = lax.axis_index("gx"), lax.axis_index("gy")
    depth, height, width = theta.shape
    rows = kernel.shape[2]
    lanes = 2 * rows
    lines = 3 * depth * height
    whole_y = count_y * height

    place = jnp.stack([gx, gy]).astype(jnp.int32)
    cells = f32(3, depth, height, width)
    order_x, order_y = partners(count_x), partners(count_y)
    table = line_table(count_x, count_y, width, rows)
    if table is None:
        table = line_table_here(count_x, width, rows, order_y)
        columns_tables = column_tables_here(count_y, height, order_y)
    else:
        columns_tables = column_tables(count_y, height, order_y)
    sources = [jnp.asarray(t) for t in (table, *columns_tables)]
    twice = np.concatenate([np.eye(rows), np.eye(rows)], 1).astype(ml_dtypes.bfloat16)
    transform_flops = 6 * lines * count_x * width * count_y * lanes

    packed, first, last = call(
        pack_kernel,
        [cells, f32(3, depth, width), f32(3, depth, width)],
        [hbm] * 3,
        (theta, phi, labels),
        scratch=(
            pltpu.VMEM((2, depth, height, width), jnp.float32),
            pltpu.VMEM((depth, height, width), jnp.int32),
            pltpu.SemaphoreType.DMA((3,)),
        ),
        name="pack",
    )
    gathered = exchanged([packed] * count_x, "gx", order_x)
    up = [(i, i + 1) for i in range(count_y - 1)]
    down = [(j, i) for i, j in up]
    before = lax.ppermute(last, "gy", up)
    after = lax.ppermute(first, "gy", down)
    gathered, before, after = lax.optimization_barrier((gathered, before, after))
    table, forward, inverse = call(
        functools.partial(load_kernel, order_x, order_y),
        [
            pltpu.VMEM((2, count_x, width, count_y * lanes), jnp.bfloat16),
            pltpu.VMEM(sources[1].shape[1:], jnp.bfloat16),
            pltpu.VMEM(sources[2].shape[1:], jnp.bfloat16),
        ],
        [smem] + [hbm] * 3,
        (place, *sources),
        scratch=(pltpu.SemaphoreType.DMA((2 + count_x * count_y,)),),
        name="load",
    )

    tensor = call(
        tensor_kernel,
        jax.ShapeDtypeStruct((48, 2 * whole_y, lanes), jnp.bfloat16),
        [vmem, vmem],
        (kernel.reshape(48, rows, 2 * whole_y), jnp.asarray(twice)),
        flops=48 * 2 * rows * lanes * 2 * whole_y,
        name="tensor",
    )
    spectrum = call(
        functools.partial(lines_kernel, count_x, count_y),
        [f32(lines, lanes)] * count_y,
        [vmem] * count_x + [hbm, vmem],
        (*gathered, ms_region, table),
        scratch=(pltpu.SMEM(ms_region.shape, jnp.float32), pltpu.SemaphoreType.DMA),
        flops=transform_flops,
        name="lines",
    )
    columns = exchanged(spectrum, "gy", order_y)
    exchange, unit = call(
        functools.partial(exchange_kernel, order_x, count_y),
        [cells, cells],
        [vmem] * (count_x + 2) + [smem] * 3,
        (*gathered, before, after, place, ms_region, aex_region),
        scratch=(pltpu.VMEM((count_x, 3, depth, height, width), jnp.float32),),
        flops=300 * depth * height * width,
        name="exchange",
    )
    columns, exchange, unit = lax.optimization_barrier((columns, exchange, unit))
    scale = -1.0 / (2 * depth * 2 * whole_y * 2 * count_x * width)
    waves = call(
        functools.partial(waves_kernel, scale, count_y),
        [f32(lines, lanes)] * count_y,
        [vmem] * (count_y + 3),
        (*columns, tensor, forward, inverse),
        scratch=(
            pltpu.VMEM((2 * whole_y, 3 * depth * lanes), jnp.float32),
            pltpu.VMEM((6 * whole_y, 3 * depth * lanes), jnp.bfloat16),
        ),
        flops=20 * whole_y * whole_y * 3 * depth * lanes,
        name="waves",
    )
    returned = exchanged(waves, "gy", order_y)
    partial = call(
        functools.partial(back_lines_kernel, count_x, count_y),
        [f32(lines, width)] * count_x,
        [vmem] * (count_y + 1),
        (*returned, table),
        flops=transform_flops,
        name="back_lines",
    )
    parts = exchanged(partial, "gx", order_x)
    field, predicted = call(
        functools.partial(final_kernel, count_x),
        [cells, cells],
        [vmem] * (count_x + 2),
        (*parts, exchange, unit),
        flops=60 * depth * height * width,
        name="predict",
    )
    return field, predicted


def solution(mesh):
    in_specs = (
        P(None, "gy", "gx"),
        P(None, "gy", "gx"),
        P(None, "gy", "gx"),
        P(),
        P(),
        P(None, None, ("gx", "gy"), None),
    )
    out_specs = (P(None, None, "gy", "gx"), P(None, None, "gy", "gx"))
    return jax.shard_map(
        per_device, mesh=mesh, in_specs=in_specs, out_specs=out_specs, check_vma=False
    )
```

```python
import functools
import math

import jax
import jax.numpy as jnp
import ml_dtypes
import numpy as np
from jax import lax
from jax.experimental import pallas as pl
from jax.experimental.pallas import tpu as pltpu
from jax.sharding import PartitionSpec as P

damping = 0.5
time_step = 0.2
side_weight = 0.25
layer_weight = 0.5
root_half = math.sqrt(0.5)
constant_limit = 20 << 20


def split_high(value):
    high = value.astype(jnp.bfloat16)
    low = (value - high.astype(jnp.float32)).astype(jnp.bfloat16)
    return high, low


def split_table(table):
    high = table.astype(np.float32).astype(ml_dtypes.bfloat16)
    low = (table - high.astype(np.float64)).astype(np.float32).astype(ml_dtypes.bfloat16)
    return high, low


def dot(left, right, contract=((1,), (0,))):
    return lax.dot_general(left, right, (contract, ((), ())), preferred_element_type=jnp.float32)


def line_table(count_x, count_y, width, rows):
    cells = count_x * width
    if count_x * 2 * cells * count_y * 2 * rows * 2 > constant_limit:
        return None
    place = np.arange(cells)[None, None, :, None]
    wave = (
        np.arange(count_x)[:, None, None, None] * (count_y * rows)
        + np.arange(count_y)[None, :, None, None] * rows
        + np.arange(rows)[None, None, None, :]
    )
    angle = (place * wave % (2 * cells)) * (2.0 * math.pi / (2 * cells))
    table = np.concatenate([np.cos(angle), -np.sin(angle)], 3)
    table = table.reshape(count_x, count_y, count_x, width, 2 * rows)
    high, low = split_table(table)
    return np.stack([high, low], 2)


def line_table_here(count_x, width, rows, order):
    cells = count_x * width
    count_y = len(order)
    place = jnp.arange(cells, dtype=jnp.int32)[:, None, None]
    block = lax.bitwise_xor(lax.axis_index("gy"), jnp.array(order, jnp.int32))
    wave = (
        lax.axis_index("gx") * (count_y * rows)
        + block[None, :, None] * rows
        + jnp.arange(rows, dtype=jnp.int32)[None, None, :]
    )
    angle = (place * wave % (2 * cells)).astype(jnp.float32) * (math.pi / cells)
    table = jnp.concatenate([jnp.cos(angle), -jnp.sin(angle)], 2)
    table = table.reshape(1, 1, count_x, width, count_y * 2 * rows)
    return jnp.stack(split_high(table), 2)


def column_tables(count_y, local, order):
    height = count_y * local
    wave = np.arange(2 * height)
    block = np.arange(count_y)[:, None] ^ np.array(order)[None, :]
    place = (block[:, :, None] * local + np.arange(local)).reshape(count_y, height)
    angle = (wave[None, :, None] * place[:, None, :] % (2 * height)) * (math.pi / height)
    high, low = split_table(np.concatenate([np.cos(angle), np.sin(angle)], 2))
    forward = np.concatenate([high, high, low], 2)
    angle = angle.transpose(0, 2, 1)
    high, low = split_table(np.concatenate([np.cos(angle), np.sin(angle)], 1))
    inverse = np.concatenate([high, high, low], 2)
    return forward, inverse


def column_tables_here(count_y, local, order):
    height = count_y * local
    wave = jnp.arange(2 * height, dtype=jnp.int32)
    block = lax.bitwise_xor(lax.axis_index("gy"), jnp.array(order, jnp.int32))
    place = (block[:, None] * local + jnp.arange(local, dtype=jnp.int32)).reshape(height)
    angle = (wave[:, None] * place % (2 * height)).astype(jnp.float32) * (math.pi / height)
    high, low = split_high(jnp.concatenate([jnp.cos(angle), jnp.sin(angle)], 1))
    forward = jnp.concatenate([high, high, low], 1)
    high, low = split_high(jnp.concatenate([jnp.cos(angle.T), jnp.sin(angle.T)], 0))
    inverse = jnp.concatenate([high, high, low], 1)
    return forward[None], inverse[None]


def load_kernel(order_x, order_y, place, *refs):
    table_ref, forward_ref, inverse_ref, table, forward, inverse, sem = refs
    gx, gy = place[0], place[1]
    mine_x = gx if table_ref.shape[0] > 1 else 0
    mine_y = gy if forward_ref.shape[0] > 1 else 0
    lanes = table_ref.shape[5]
    copies = [
        pltpu.make_async_copy(forward_ref.at[mine_y], forward, sem.at[0]),
        pltpu.make_async_copy(inverse_ref.at[mine_y], inverse, sem.at[1]),
    ]
    for spot_x, number_x in enumerate(order_x):
        block_x = lax.bitwise_xor(gx, number_x)
        for spot_y in range(table_ref.shape[1]):
            block_y = lax.bitwise_xor(gy, order_y[spot_y]) if table_ref.shape[1] > 1 else 0
            columns = slice(spot_y * lanes, (spot_y + 1) * lanes)
            copies.append(
                pltpu.make_async_copy(
                    table_ref.at[mine_x, block_y, :, block_x],
                    table.at[:, spot_x, :, columns],
                    sem.at[len(copies)],
                )
            )
    for copy in copies:
        copy.start()
    for copy in copies:
        copy.wait()


def sine_cosine(angle):
    turns = jnp.floor(angle * (2.0 / math.pi) + 0.5)
    rest = angle - turns * 1.5703125
    rest = rest - turns * 4.8351287841796875e-4
    rest = rest - turns * 3.1385570764541626e-7
    square = rest * rest
    sine = rest + rest * square * (
        -1.6666654611e-1 + square * (8.3321608736e-3 - square * 1.9515295891e-4)
    )
    cosine = (
        1.0
        - 0.5 * square
        + square * square * (4.166664568298827e-2 + square * (-1.388731625493765e-3 + square * 2.443315711809948e-5))
    )
    quarter = turns.astype(jnp.int32)
    odd = (quarter & 1) == 1
    out_sine = jnp.where(odd, cosine, sine)
    out_cosine = jnp.where(odd, sine, cosine)
    out_sine = jnp.where((quarter & 2) == 2, -out_sine, out_sine)
    out_cosine = jnp.where(((quarter + 1) & 2) == 2, -out_cosine, out_cosine)
    return out_sine, out_cosine


def directions(theta, phi):
    lateral, axial = sine_cosine(theta)
    sine, cosine = sine_cosine(phi)
    return [lateral * cosine, lateral * sine, axial]


def looked_up(labels, region):
    result = jnp.zeros_like(labels) + region[0]
    for index in range(1, region.shape[0]):
        result = jnp.where(labels == float(index), region[index], result)
    return result


def pack_kernel(theta_ref, phi_ref, labels_ref, raw_ref, angle, label, sems):
    copies = [
        pltpu.make_async_copy(theta_ref, angle.at[0], sems.at[0]),
        pltpu.make_async_copy(phi_ref, angle.at[1], sems.at[1]),
        pltpu.make_async_copy(labels_ref, label, sems.at[2]),
    ]
    for copy in copies:
        copy.start()
    for copy in copies:
        copy.wait()
    for index, value in enumerate((angle[0], angle[1], label[...].astype(jnp.float32))):
        raw_ref[index] = value


def lines_kernel(count_x, order_y, *refs):
    raw_refs, (region_ref, place, table) = refs[:count_x], refs[count_x : count_x + 3]
    out_refs, (region, sem) = refs[count_x + 3 : -2], refs[-2:]
    gy = place[1]
    fetch = pltpu.make_async_copy(region_ref, region, sem)
    fetch.start()
    units = [directions(raw_ref[0], raw_ref[1]) for raw_ref in raw_refs]
    fetch.wait()
    total = None
    for number in range(count_x):
        saturation = looked_up(raw_refs[number][2], region)
        rows = saturation.shape[0] * saturation.shape[1]
        block = [(part * saturation).reshape(rows, -1) for part in units[number]]
        high, low = split_high(jnp.concatenate(block, 0))
        both = dot(jnp.concatenate([high, low], 0), table[0, number])
        part = both[: 3 * rows] + both[3 * rows :] + dot(high, table[1, number])
        total = part if total is None else total + part
    lanes = out_refs[0].shape[1]
    last_row = raw_refs[0].shape[2] - 1
    for spot, number in enumerate(order_y):
        out_refs[spot][: 3 * rows] = total[:, spot * lanes : (spot + 1) * lanes]
        if number in meeting(len(order_y)):
            up = lax.bitwise_xor(gy, number) > gy
            for field in range(3):
                value = raw_refs[0][field]
                edge = jnp.where(up, value[:, last_row], value[:, 0])
                put_edge(out_refs[spot], 3 * rows, field, edge)


def meeting(devices):
    return [number for number in range(1, devices) if (number & (number + 1)) == 0]


def edge_spots(depth, width, lanes, start, field):
    pieces = width // lanes
    return [start + (field * pieces + piece) * depth for piece in range(pieces)]


def put_edge(ref, start, field, edge):
    lanes = ref.shape[1]
    for piece, row in enumerate(edge_spots(*edge.shape, lanes, start, field)):
        ref[row : row + edge.shape[0]] = edge[:, piece * lanes : (piece + 1) * lanes]


def get_edge(ref, depth, width, start, field):
    spots = edge_spots(depth, width, ref.shape[1], start, field)
    return jnp.concatenate([ref[row : row + depth] for row in spots], 1)


def back_lines_kernel(count_x, count_y, *refs):
    in_refs, table, out_refs = refs[:count_y], refs[count_y], refs[count_y + 1 :]
    high, low = split_high(jnp.concatenate([ref[...] for ref in in_refs], 1))
    both = jnp.concatenate([high, low], 0)
    lines = high.shape[0]
    for number in range(count_x):
        wide = dot(both, table[0, number], ((1,), (1,)))
        out_refs[number][...] = (
            wide[:lines] + wide[lines:] + dot(high, table[1, number], ((1,), (1,)))
        )


def tensor_kernel(kernel_ref, twice_ref, out_ref):
    twice = twice_ref[...]

    unroll = 8

    def step(index, carry):
        for offset in range(unroll):
            turned = dot(kernel_ref[index * unroll + offset], twice, ((0,), (0,)))
            out_ref[index * unroll + offset] = turned.astype(jnp.bfloat16)
        return carry

    lax.fori_loop(0, kernel_ref.shape[0] // unroll, step, 0)


def turn(value, sign):
    lanes = value.shape[-1]
    if lanes == 128:
        return pltpu.roll(value, lanes // 2, value.ndim - 1) * sign
    return jnp.concatenate([value[..., lanes // 2 :], value[..., : lanes // 2]], -1) * sign


def layers_forward(layer, sign):
    d0, d1, d2, d3 = layer
    r2 = turn(d2, sign)
    near, far = d1 + d3, d1 - d3
    far_turned = turn(far, sign)
    near_turned = turn(near, sign)
    even, odd = d0 + d2, d0 - d2
    out = [None] * 8
    out[0], out[4] = even + near, even - near
    out[2], out[6] = odd + far_turned, odd - far_turned
    plus, minus = d0 + r2, d0 - r2
    first = (far + near_turned) * root_half
    second = (near_turned - far) * root_half
    out[1], out[5] = plus + first, plus - first
    out[3], out[7] = minus + second, minus - second
    return out


def layers_inverse(wave, sign):
    a, b = wave[0] + wave[4], wave[0] - wave[4]
    e, f = wave[2] + wave[6], turn(wave[2] - wave[6], sign)
    p, q = wave[1] + wave[5], wave[1] - wave[5]
    s, t = wave[3] + wave[7], turn(wave[3] - wave[7], sign)
    o0, o1, o2, o3 = p + s, q - t, p - s, q + t
    return [
        a + e + o0,
        b - f + (o1 - turn(o1, sign)) * root_half,
        a - e - turn(o2, sign),
        b + f - (o3 + turn(o3, sign)) * root_half,
    ]


def apply_tensor(tensor, wave):
    out = [[], [], []]
    for level in range(8):
        xx, yy, zz, xy, xz, yz = [tensor[part][level] for part in range(6)]
        x, y, z = wave[0][level], wave[1][level], wave[2][level]
        out[0].append(xx * x + xy * y + xz * z)
        out[1].append(xy * x + yy * y + yz * z)
        out[2].append(xz * x + yz * y + zz * z)
    return out


def waves_kernel(scale, count_y, *refs):
    spec_refs, (tensor_ref, forward_ref, inverse_ref) = refs[:count_y], refs[count_y : count_y + 3]
    out_refs, (wave_ref, back_ref) = refs[count_y + 3 : -2], refs[-2:]
    lines, lanes = spec_refs[0].shape
    local = 8
    planes = lines // local
    height = count_y * local
    sign = jnp.where(
        lax.broadcasted_iota(jnp.int32, (1, lanes), 1) < lanes // 2, 1.0, -1.0
    ).astype(jnp.float32)
    columns = []
    for plane in range(planes):
        value = jnp.concatenate(
            [spec_ref[plane * local : (plane + 1) * local] for spec_ref in spec_refs], 0
        )
        value = jnp.concatenate([value, turn(value, sign)], 0)
        high, low = split_high(value)
        columns.append(jnp.concatenate([high, low, high], 0))
    wave_ref[...] = dot(forward_ref[...], jnp.concatenate(columns, 1))

    chunk = 16
    depth = planes // 3
    double = 2 * height

    def step(index, carry):
        rows = pl.ds(pl.multiple_of(index * chunk, chunk), chunk)
        wave = []
        for part in range(3):
            layer = [
                wave_ref[rows, (part * depth + z) * lanes : (part * depth + z + 1) * lanes]
                for z in range(depth)
            ]
            wave.append(layers_forward(layer, sign))
        tensor = [
            [tensor_ref[part * 8 + level, rows, :].astype(jnp.float32) for level in range(8)]
            for part in range(6)
        ]
        image = apply_tensor(tensor, wave)
        for part in range(3):
            layer = layers_inverse(image[part], sign)
            for z in range(depth):
                spot = slice((part * depth + z) * lanes, (part * depth + z + 1) * lanes)
                high, low = split_high(layer[z] * scale)
                back_ref[rows, spot] = high
                back_ref[pl.ds(pl.multiple_of(double + index * chunk, chunk), chunk), spot] = low
                back_ref[pl.ds(pl.multiple_of(2 * double + index * chunk, chunk), chunk), spot] = high
        return carry

    lax.fori_loop(0, double // chunk, step, 0)
    back = dot(inverse_ref[...], back_ref[...])
    for plane in range(planes):
        part = slice(plane * lanes, (plane + 1) * lanes)
        value = back[:height, part] - turn(back[height:, part], sign)
        for number in range(count_y):
            out_refs[number][plane * local : (plane + 1) * local] = value[
                number * local : (number + 1) * local
            ]


def exchange_kernel(order_x, count_y, *refs):
    count_x, numbers = len(order_x), meeting(count_y)
    raw_refs, edge_refs, (place, ms_ref, aex_ref) = refs[:count_x], refs[count_x:-6], refs[-6:-3]
    exchange_ref, unit_ref, raw_ref = refs[-3:]
    depth, height, width = raw_ref.shape[2:]
    gx, gy = place[0], place[1]

    def row_meeting(field, other):
        value = None
        for number, edge_ref in zip(numbers, edge_refs):
            edge = get_edge(edge_ref, depth, width, 3 * depth * height, field)
            match = lax.bitwise_xor(gy, number) == other
            value = edge if value is None else jnp.where(match, edge, value)
        return jnp.broadcast_to(value[:, None, :], (depth, height, width))

    for spot, number in enumerate(order_x):
        raw_ref[lax.bitwise_xor(gx, number)] = raw_refs[spot][...]
    left, right = jnp.maximum(gx - 1, 0), jnp.minimum(gx + 1, count_x - 1)
    shape = (depth, height, width)
    lane = lax.broadcasted_iota(jnp.int32, shape, 2)
    row = lax.broadcasted_iota(jnp.int32, shape, 1)

    def quantities(values):
        return directions(values[0], values[1]) + [looked_up(values[2], aex_ref)]

    raw = [raw_refs[0][f] for f in range(3)]
    here = quantities(raw)
    side = quantities([jnp.where(lane == 0, raw_ref[right, f], raw_ref[left, f]) for f in range(3)])
    above = quantities(
        [jnp.where(row == 0, row_meeting(f, gy + 1), row_meeting(f, gy - 1)) for f in range(3)]
    )
    saturation = looked_up(raw[2], ms_ref)
    total = [jnp.zeros(shape, jnp.float32) for _ in range(3)]

    def add(total, beside, weight):
        coupling = 2.0 * here[3] * beside[3] / (here[3] + beside[3]) * weight
        return [total[c] + coupling * (beside[c] - here[c]) for c in range(3)]

    one = jnp.float32(1.0)
    zero = jnp.float32(0.0)
    for shift, edge, there in ((1, 0, gx > 0), (width - 1, width - 1, gx < count_x - 1)):
        beside = [
            jnp.where(lane == edge, pltpu.roll(s, shift, 2), pltpu.roll(h, shift, 2))
            for s, h in zip(side, here)
        ]
        weight = jnp.where(lane == edge, jnp.where(there, one, zero), one) * side_weight
        total = add(total, beside, weight)
    for shift, edge, there in ((1, 0, gy > 0), (height - 1, height - 1, gy < count_y - 1)):
        beside = [
            jnp.where(row == edge, pltpu.roll(s, shift, 1), pltpu.roll(h, shift, 1))
            for s, h in zip(above, here)
        ]
        weight = jnp.where(row == edge, jnp.where(there, one, zero), one) * side_weight
        total = add(total, beside, weight)
    for part in range(3):
        unit_ref[part] = here[part]
    for z in range(depth):
        out = [total[c][z] for c in range(3)]
        for other in (z - 1, z + 1):
            if 0 <= other < depth:
                a, b = here[3][z], here[3][other]
                coupling = 2.0 * a * b / (a + b) * layer_weight
                out = [out[c] + coupling * (here[c][other] - here[c][z]) for c in range(3)]
        for c in range(3):
            exchange_ref[c, z] = out[c] / saturation[z]


def cross(first, second):
    return [
        first[1] * second[2] - first[2] * second[1],
        first[2] * second[0] - first[0] * second[2],
        first[0] * second[1] - first[1] * second[0],
    ]


def final_kernel(count_x, *refs):
    part_refs, (exchange_ref, unit_ref, field_ref, predicted_ref) = refs[:count_x], refs[count_x:]
    depth, height, width = unit_ref.shape[1:]
    rows = depth * height
    unit, field = [], []
    for c in range(3):
        place = slice(c * rows, (c + 1) * rows)
        total = part_refs[0][place]
        for part_ref in part_refs[1:]:
            total = total + part_ref[place]
        field.append(exchange_ref[c] + total.reshape(depth, height, width))
        unit.append(unit_ref[c])
        field_ref[c] = field[c]
    twist = cross(unit, field)
    second = cross(unit, twist)
    moved = [
        unit[c] - (time_step / (1.0 + damping * damping)) * (twist[c] + damping * second[c])
        for c in range(3)
    ]
    length = jnp.sqrt(moved[0] * moved[0] + moved[1] * moved[1] + moved[2] * moved[2])
    for c in range(3):
        predicted_ref[c] = moved[c] / length


vmem = pl.BlockSpec(memory_space=pltpu.VMEM)
smem = pl.BlockSpec(memory_space=pltpu.SMEM)
hbm = pl.BlockSpec(memory_space=pltpu.HBM)


def call(body, out, ins, operands, scratch=(), flops=0, name=None, grant=16 << 20):
    operands = [
        pltpu.with_memory_space_constraint(o, pltpu.HBM) if i is hbm else o
        for i, o in zip(ins, operands)
    ]
    size = sum(math.prod(o.shape) * o.dtype.itemsize for o in operands)
    outs = out if isinstance(out, (list, tuple)) else [out]
    size += sum(math.prod(o.shape) * jnp.dtype(o.dtype).itemsize for o in outs)
    return pl.pallas_call(
        body,
        out_shape=out,
        in_specs=ins,
        out_specs=[vmem] * len(outs) if outs is out else vmem,
        scratch_shapes=list(scratch),
        compiler_params=pltpu.CompilerParams(vmem_limit_bytes=grant),
        cost_estimate=pl.CostEstimate(flops=flops, bytes_accessed=size, transcendentals=0),
        name=name,
    )(*operands)


def f32(*shape):
    return jax.ShapeDtypeStruct(shape, jnp.float32)


def exchanged(chunks, axis, order):
    devices = len(order)
    out = [chunks[0]] + [None] * (devices - 1)
    for spot, number in enumerate(order[1:]):
        pairs = [(i, i ^ number) for i in range(devices)]
        out[spot + 1] = lax.ppermute(chunks[spot + 1], axis, pairs)
    return out


def partners(devices):
    return [0] + list(range(devices - 1, 0, -1))


def per_device(theta, phi, labels, ms_region, aex_region, kernel):
    count_x, count_y = lax.axis_size("gx"), lax.axis_size("gy")
    gx, gy = lax.axis_index("gx"), lax.axis_index("gy")
    depth, height, width = theta.shape
    rows = kernel.shape[2]
    lanes = 2 * rows
    lines = 3 * depth * height
    whole_y = count_y * height

    place = jnp.stack([gx, gy]).astype(jnp.int32)
    cells = f32(3, depth, height, width)
    order_x, order_y = partners(count_x), partners(count_y)
    table = line_table(count_x, count_y, width, rows)
    if table is None:
        table = line_table_here(count_x, width, rows, order_y)
        columns_tables = column_tables_here(count_y, height, order_y)
    else:
        columns_tables = column_tables(count_y, height, order_y)
    sources = [jnp.asarray(t) for t in (table, *columns_tables)]
    twice = np.concatenate([np.eye(rows), np.eye(rows)], 1).astype(ml_dtypes.bfloat16)
    transform_flops = 6 * lines * count_x * width * count_y * lanes

    packed = call(
        pack_kernel,
        cells,
        [hbm] * 3,
        (theta, phi, labels),
        scratch=(
            pltpu.VMEM((2, depth, height, width), jnp.float32),
            pltpu.VMEM((depth, height, width), jnp.int32),
            pltpu.SemaphoreType.DMA((3,)),
        ),
        name="pack",
    )
    gathered = exchanged([packed] * count_x, "gx", order_x)
    table, forward, inverse = call(
        functools.partial(load_kernel, order_x, order_y),
        [
            pltpu.VMEM((2, count_x, width, count_y * lanes), jnp.bfloat16),
            pltpu.VMEM(sources[1].shape[1:], jnp.bfloat16),
            pltpu.VMEM(sources[2].shape[1:], jnp.bfloat16),
        ],
        [smem] + [hbm] * 3,
        (place, *sources),
        scratch=(pltpu.SemaphoreType.DMA((2 + count_x * count_y,)),),
        name="load",
    )

    tensor = call(
        tensor_kernel,
        jax.ShapeDtypeStruct((48, 2 * whole_y, lanes), jnp.bfloat16),
        [vmem, vmem],
        (kernel.reshape(48, rows, 2 * whole_y), jnp.asarray(twice)),
        flops=48 * 2 * rows * lanes * 2 * whole_y,
        name="tensor",
    )
    gathered, tensor = lax.optimization_barrier((gathered, tensor))
    edge_rows = 3 * depth * width // lanes
    spectrum = call(
        functools.partial(lines_kernel, count_x, order_y),
        [f32(lines + (edge_rows if n in meeting(count_y) else 0), lanes) for n in order_y],
        [vmem] * count_x + [hbm, smem, vmem],
        (*gathered, ms_region, place, table),
        scratch=(pltpu.SMEM(ms_region.shape, jnp.float32), pltpu.SemaphoreType.DMA),
        flops=transform_flops,
        name="lines",
    )
    columns = exchanged(spectrum, "gy", order_y)
    scale = -1.0 / (2 * depth * 2 * whole_y * 2 * count_x * width)
    waves = call(
        functools.partial(waves_kernel, scale, count_y),
        [f32(lines, lanes)] * count_y,
        [vmem] * (count_y + 3),
        (*columns, tensor, forward, inverse),
        scratch=(
            pltpu.VMEM((2 * whole_y, 3 * depth * lanes), jnp.float32),
            pltpu.VMEM((6 * whole_y, 3 * depth * lanes), jnp.bfloat16),
        ),
        flops=20 * whole_y * whole_y * 3 * depth * lanes,
        name="waves",
    )
    returned = exchanged(waves, "gy", order_y)
    partial = call(
        functools.partial(back_lines_kernel, count_x, count_y),
        [f32(lines, width)] * count_x,
        [vmem] * (count_y + 1),
        (*returned, table),
        flops=transform_flops,
        name="back_lines",
    )
    edges = [columns[order_y.index(number)] for number in meeting(count_y)]
    edges, partial = lax.optimization_barrier((edges, partial))
    exchange, unit = call(
        functools.partial(exchange_kernel, order_x, count_y),
        [cells, cells],
        [vmem] * (count_x + len(edges)) + [smem] * 3,
        (*gathered, *edges, place, ms_region, aex_region),
        scratch=(pltpu.VMEM((count_x, 3, depth, height, width), jnp.float32),),
        flops=300 * depth * height * width,
        name="exchange",
    )
    parts = exchanged(partial, "gx", order_x)
    field, predicted = call(
        functools.partial(final_kernel, count_x),
        [cells, cells],
        [vmem] * (count_x + 2),
        (*parts, exchange, unit),
        flops=60 * depth * height * width,
        name="predict",
    )
    return field, predicted


def solution(mesh):
    in_specs = (
        P(None, "gy", "gx"),
        P(None, "gy", "gx"),
        P(None, "gy", "gx"),
        P(),
        P(),
        P(None, None, ("gx", "gy"), None),
    )
    out_specs = (P(None, None, "gy", "gx"), P(None, None, "gy", "gx"))
    return jax.shard_map(
        per_device, mesh=mesh, in_specs=in_specs, out_specs=out_specs, check_vma=False
    )
```

```python
import functools
import math

import jax
import jax.numpy as jnp
import ml_dtypes
import numpy as np
from jax import lax
from jax.experimental import pallas as pl
from jax.experimental.pallas import tpu as pltpu
from jax.sharding import PartitionSpec as P

damping = 0.5
time_step = 0.2
side_weight = 0.25
layer_weight = 0.5
root_half = math.sqrt(0.5)
constant_limit = 20 << 20


def split_high(value):
    high = value.astype(jnp.bfloat16)
    low = (value - high.astype(jnp.float32)).astype(jnp.bfloat16)
    return high, low


def split_table(table):
    high = table.astype(np.float32).astype(ml_dtypes.bfloat16)
    low = (table - high.astype(np.float64)).astype(np.float32).astype(ml_dtypes.bfloat16)
    return high, low


def dot(left, right, contract=((1,), (0,))):
    return lax.dot_general(left, right, (contract, ((), ())), preferred_element_type=jnp.float32)


def line_table(count_x, count_y, width, rows):
    cells = count_x * width
    if count_x * 2 * cells * count_y * 2 * rows * 2 > constant_limit:
        return None
    place = np.arange(cells)[None, None, :, None]
    wave = (
        np.arange(count_x)[:, None, None, None] * (count_y * rows)
        + np.arange(count_y)[None, :, None, None] * rows
        + np.arange(rows)[None, None, None, :]
    )
    angle = (place * wave % (2 * cells)) * (2.0 * math.pi / (2 * cells))
    table = np.concatenate([np.cos(angle), -np.sin(angle)], 3)
    table = table.reshape(count_x, count_y, count_x, width, 2 * rows)
    high, low = split_table(table)
    return np.stack([high, low], 2)


def line_table_here(count_x, width, rows, order):
    cells = count_x * width
    count_y = len(order)
    place = jnp.arange(cells, dtype=jnp.int32)[:, None, None]
    block = lax.bitwise_xor(lax.axis_index("gy"), jnp.array(order, jnp.int32))
    wave = (
        lax.axis_index("gx") * (count_y * rows)
        + block[None, :, None] * rows
        + jnp.arange(rows, dtype=jnp.int32)[None, None, :]
    )
    angle = (place * wave % (2 * cells)).astype(jnp.float32) * (math.pi / cells)
    table = jnp.concatenate([jnp.cos(angle), -jnp.sin(angle)], 2)
    table = table.reshape(1, 1, count_x, width, count_y * 2 * rows)
    return jnp.stack(split_high(table), 2)


def column_tables(count_y, local, order):
    height = count_y * local
    wave = np.arange(2 * height)
    block = np.arange(count_y)[:, None] ^ np.array(order)[None, :]
    place = (block[:, :, None] * local + np.arange(local)).reshape(count_y, height)
    angle = (wave[None, :, None] * place[:, None, :] % (2 * height)) * (math.pi / height)
    high, low = split_table(np.concatenate([np.cos(angle), np.sin(angle)], 2))
    forward = np.concatenate([high, high, low], 2)
    angle = angle.transpose(0, 2, 1)
    high, low = split_table(np.concatenate([np.cos(angle), np.sin(angle)], 1))
    inverse = np.concatenate([high, high, low], 2)
    return forward, inverse


def column_tables_here(count_y, local, order):
    height = count_y * local
    wave = jnp.arange(2 * height, dtype=jnp.int32)
    block = lax.bitwise_xor(lax.axis_index("gy"), jnp.array(order, jnp.int32))
    place = (block[:, None] * local + jnp.arange(local, dtype=jnp.int32)).reshape(height)
    angle = (wave[:, None] * place % (2 * height)).astype(jnp.float32) * (math.pi / height)
    high, low = split_high(jnp.concatenate([jnp.cos(angle), jnp.sin(angle)], 1))
    forward = jnp.concatenate([high, high, low], 1)
    high, low = split_high(jnp.concatenate([jnp.cos(angle.T), jnp.sin(angle.T)], 0))
    inverse = jnp.concatenate([high, high, low], 1)
    return forward[None], inverse[None]


def load_kernel(order_x, order_y, place, *refs):
    table_ref, forward_ref, inverse_ref, table, forward, inverse, sem = refs
    gx, gy = place[0], place[1]
    mine_x = gx if table_ref.shape[0] > 1 else 0
    mine_y = gy if forward_ref.shape[0] > 1 else 0
    lanes = table_ref.shape[5]
    copies = [
        pltpu.make_async_copy(forward_ref.at[mine_y], forward, sem.at[0]),
        pltpu.make_async_copy(inverse_ref.at[mine_y], inverse, sem.at[1]),
    ]
    for spot_x, number_x in enumerate(order_x):
        block_x = lax.bitwise_xor(gx, number_x)
        for spot_y in range(table_ref.shape[1]):
            block_y = lax.bitwise_xor(gy, order_y[spot_y]) if table_ref.shape[1] > 1 else 0
            columns = slice(spot_y * lanes, (spot_y + 1) * lanes)
            copies.append(
                pltpu.make_async_copy(
                    table_ref.at[mine_x, block_y, :, block_x],
                    table.at[:, spot_x, :, columns],
                    sem.at[len(copies)],
                )
            )
    for copy in copies:
        copy.start()
    for copy in copies:
        copy.wait()


def sine_cosine(angle):
    turns = jnp.floor(angle * (2.0 / math.pi) + 0.5)
    rest = angle - turns * 1.5703125
    rest = rest - turns * 4.8351287841796875e-4
    rest = rest - turns * 3.1385570764541626e-7
    square = rest * rest
    sine = rest + rest * square * (
        -1.6666654611e-1 + square * (8.3321608736e-3 - square * 1.9515295891e-4)
    )
    cosine = (
        1.0
        - 0.5 * square
        + square * square * (4.166664568298827e-2 + square * (-1.388731625493765e-3 + square * 2.443315711809948e-5))
    )
    quarter = turns.astype(jnp.int32)
    odd = (quarter & 1) == 1
    out_sine = jnp.where(odd, cosine, sine)
    out_cosine = jnp.where(odd, sine, cosine)
    out_sine = jnp.where((quarter & 2) == 2, -out_sine, out_sine)
    out_cosine = jnp.where(((quarter + 1) & 2) == 2, -out_cosine, out_cosine)
    return out_sine, out_cosine


def directions(theta, phi):
    lateral, axial = sine_cosine(theta)
    sine, cosine = sine_cosine(phi)
    return [lateral * cosine, lateral * sine, axial]


def looked_up(labels, region):
    result = jnp.zeros_like(labels) + region[0]
    for index in range(1, region.shape[0]):
        result = jnp.where(labels == float(index), region[index], result)
    return result


def pack_kernel(theta_ref, phi_ref, labels_ref, raw_ref, angle, label, sems):
    copies = [
        pltpu.make_async_copy(theta_ref, angle.at[0], sems.at[0]),
        pltpu.make_async_copy(phi_ref, angle.at[1], sems.at[1]),
        pltpu.make_async_copy(labels_ref, label, sems.at[2]),
    ]
    for copy in copies:
        copy.start()
    for copy in copies:
        copy.wait()
    for index, value in enumerate((angle[0], angle[1], label[...].astype(jnp.float32))):
        raw_ref[index] = value


def lines_kernel(count_x, order_y, *refs):
    raw_refs, (region_ref, place, table) = refs[:count_x], refs[count_x : count_x + 3]
    out_refs, (region, sem) = refs[count_x + 3 : -2], refs[-2:]
    gy = place[1]
    fetch = pltpu.make_async_copy(region_ref, region, sem)
    fetch.start()
    units = [directions(raw_ref[0], raw_ref[1]) for raw_ref in raw_refs]
    fetch.wait()
    total = None
    for number in range(count_x):
        saturation = looked_up(raw_refs[number][2], region)
        rows = saturation.shape[0] * saturation.shape[1]
        block = [(part * saturation).reshape(rows, -1) for part in units[number]]
        high, low = split_high(jnp.concatenate(block, 0))
        both = dot(jnp.concatenate([high, low], 0), table[0, number])
        part = both[: 3 * rows] + both[3 * rows :] + dot(high, table[1, number])
        total = part if total is None else total + part
    lanes = out_refs[0].shape[1]
    last_row = raw_refs[0].shape[2] - 1
    for spot, number in enumerate(order_y):
        out_refs[spot][: 3 * rows] = total[:, spot * lanes : (spot + 1) * lanes]
        if number in meeting(len(order_y)):
            up = lax.bitwise_xor(gy, number) > gy
            for field in range(3):
                value = raw_refs[0][field]
                edge = jnp.where(up, value[:, last_row], value[:, 0])
                put_edge(out_refs[spot], 3 * rows, field, edge)


def meeting(devices):
    return [number for number in range(1, devices) if (number & (number + 1)) == 0]


def edge_spots(depth, width, lanes, start, field):
    pieces = width // lanes
    return [start + (field * pieces + piece) * depth for piece in range(pieces)]


def put_edge(ref, start, field, edge):
    lanes = ref.shape[1]
    for piece, row in enumerate(edge_spots(*edge.shape, lanes, start, field)):
        ref[row : row + edge.shape[0]] = edge[:, piece * lanes : (piece + 1) * lanes]


def get_edge(ref, depth, width, start, field):
    spots = edge_spots(depth, width, ref.shape[1], start, field)
    return jnp.concatenate([ref[row : row + depth] for row in spots], 1)


def back_lines_kernel(count_x, count_y, *refs):
    in_refs, table, out_refs = refs[:count_y], refs[count_y], refs[count_y + 1 :]
    high, low = split_high(jnp.concatenate([ref[...] for ref in in_refs], 1))
    both = jnp.concatenate([high, low], 0)
    lines = high.shape[0]
    for number in range(count_x):
        wide = dot(both, table[0, number], ((1,), (1,)))
        out_refs[number][...] = (
            wide[:lines] + wide[lines:] + dot(high, table[1, number], ((1,), (1,)))
        )


def tensor_kernel(kernel_ref, twice_ref, out_ref):
    twice = twice_ref[...]

    unroll = 8

    def step(index, carry):
        for offset in range(unroll):
            turned = dot(kernel_ref[index * unroll + offset], twice, ((0,), (0,)))
            out_ref[index * unroll + offset] = turned.astype(jnp.bfloat16)
        return carry

    lax.fori_loop(0, kernel_ref.shape[0] // unroll, step, 0)


def turn(value, sign):
    lanes = value.shape[-1]
    if lanes == 128:
        return pltpu.roll(value, lanes // 2, value.ndim - 1) * sign
    return jnp.concatenate([value[..., lanes // 2 :], value[..., : lanes // 2]], -1) * sign


def layers_forward(layer, sign):
    d0, d1, d2, d3 = layer
    r2 = turn(d2, sign)
    near, far = d1 + d3, d1 - d3
    far_turned = turn(far, sign)
    near_turned = turn(near, sign)
    even, odd = d0 + d2, d0 - d2
    out = [None] * 8
    out[0], out[4] = even + near, even - near
    out[2], out[6] = odd + far_turned, odd - far_turned
    plus, minus = d0 + r2, d0 - r2
    first = (far + near_turned) * root_half
    second = (near_turned - far) * root_half
    out[1], out[5] = plus + first, plus - first
    out[3], out[7] = minus + second, minus - second
    return out


def layers_inverse(wave, sign):
    a, b = wave[0] + wave[4], wave[0] - wave[4]
    e, f = wave[2] + wave[6], turn(wave[2] - wave[6], sign)
    p, q = wave[1] + wave[5], wave[1] - wave[5]
    s, t = wave[3] + wave[7], turn(wave[3] - wave[7], sign)
    o0, o1, o2, o3 = p + s, q - t, p - s, q + t
    return [
        a + e + o0,
        b - f + (o1 - turn(o1, sign)) * root_half,
        a - e - turn(o2, sign),
        b + f - (o3 + turn(o3, sign)) * root_half,
    ]


def apply_tensor(tensor, wave):
    out = [[], [], []]
    for level in range(8):
        xx, yy, zz, xy, xz, yz = [tensor[part][level] for part in range(6)]
        x, y, z = wave[0][level], wave[1][level], wave[2][level]
        out[0].append(xx * x + xy * y + xz * z)
        out[1].append(xy * x + yy * y + yz * z)
        out[2].append(xz * x + yz * y + zz * z)
    return out


def waves_kernel(scale, count_y, *refs):
    spec_refs, tables = refs[:count_y], refs[count_y : count_y + 3]
    out_refs, scratch = refs[count_y + 3 : -2], refs[-2:]
    lines, lanes = spec_refs[0].shape
    local = 8

    def read(plane):
        rows = slice(plane * local, (plane + 1) * local)
        return jnp.concatenate([spec_ref[rows] for spec_ref in spec_refs], 0)

    def write(plane, value):
        for number in range(count_y):
            out_refs[number][plane * local : (plane + 1) * local] = value[
                number * local : (number + 1) * local
            ]

    waves(scale, count_y * local, lines // local, lanes, read, write, tables, scratch)


def waves(scale, height, planes, lanes, read, write, tables, scratch):
    (tensor_ref, forward_ref, inverse_ref), (wave_ref, back_ref) = tables, scratch
    sign = jnp.where(
        lax.broadcasted_iota(jnp.int32, (1, lanes), 1) < lanes // 2, 1.0, -1.0
    ).astype(jnp.float32)
    columns = []
    for plane in range(planes):
        value = read(plane)
        value = jnp.concatenate([value, turn(value, sign)], 0)
        high, low = split_high(value)
        columns.append(jnp.concatenate([high, low, high], 0))
    wave_ref[...] = dot(forward_ref[...], jnp.concatenate(columns, 1))

    chunk = 16
    depth = planes // 3
    double = 2 * height

    def step(index, carry):
        rows = pl.ds(pl.multiple_of(index * chunk, chunk), chunk)
        wave = []
        for part in range(3):
            layer = [
                wave_ref[rows, (part * depth + z) * lanes : (part * depth + z + 1) * lanes]
                for z in range(depth)
            ]
            wave.append(layers_forward(layer, sign))
        tensor = [
            [tensor_ref[part * 8 + level, rows, :].astype(jnp.float32) for level in range(8)]
            for part in range(6)
        ]
        image = apply_tensor(tensor, wave)
        for part in range(3):
            layer = layers_inverse(image[part], sign)
            for z in range(depth):
                spot = slice((part * depth + z) * lanes, (part * depth + z + 1) * lanes)
                high, low = split_high(layer[z] * scale)
                back_ref[rows, spot] = high
                back_ref[pl.ds(pl.multiple_of(double + index * chunk, chunk), chunk), spot] = low
                back_ref[pl.ds(pl.multiple_of(2 * double + index * chunk, chunk), chunk), spot] = high
        return carry

    lax.fori_loop(0, double // chunk, step, 0)
    back = dot(inverse_ref[...], back_ref[...])
    for plane in range(planes):
        part = slice(plane * lanes, (plane + 1) * lanes)
        value = back[:height, part] - turn(back[height:, part], sign)
        write(plane, value)


def exchange_kernel(order_x, count_y, *refs):
    count_x, numbers = len(order_x), meeting(count_y)
    raw_refs, edge_refs, (place, ms_ref, aex_ref) = refs[:count_x], refs[count_x:-6], refs[-6:-3]
    exchange_ref, unit_ref, raw_ref = refs[-3:]
    depth, height, width = shape = raw_ref.shape[2:]
    gx, gy = place[0], place[1]

    def row_meeting(field, other):
        value = None
        for number, edge_ref in zip(numbers, edge_refs):
            edge = get_edge(edge_ref, depth, width, 3 * depth * height, field)
            match = lax.bitwise_xor(gy, number) == other
            value = edge if value is None else jnp.where(match, edge, value)
        return jnp.broadcast_to(value[:, None, :], shape)

    for spot, number in enumerate(order_x):
        raw_ref[lax.bitwise_xor(gx, number)] = raw_refs[spot][...]
    left, right = jnp.maximum(gx - 1, 0), jnp.minimum(gx + 1, count_x - 1)
    lane = lax.broadcasted_iota(jnp.int32, shape, 2)
    row = lax.broadcasted_iota(jnp.int32, shape, 1)
    raw = [raw_refs[0][f] for f in range(3)]
    side = [jnp.where(lane == 0, raw_ref[right, f], raw_ref[left, f]) for f in range(3)]
    above = [
        jnp.where(row == 0, row_meeting(f, gy + 1), row_meeting(f, gy - 1)) for f in range(3)
    ]
    exchange(raw, side, above, (gx, count_x, gy, count_y), ms_ref, aex_ref, exchange_ref, unit_ref)


def exchange(raw, side, above, spots, ms_ref, aex_ref, exchange_ref, unit_ref):
    depth, height, width = shape = raw[0].shape
    gx, count_x, gy, count_y = spots
    lane = lax.broadcasted_iota(jnp.int32, shape, 2)
    row = lax.broadcasted_iota(jnp.int32, shape, 1)

    def quantities(values):
        return directions(values[0], values[1]) + [looked_up(values[2], aex_ref)]

    here, side, above = quantities(raw), quantities(side), quantities(above)
    saturation = looked_up(raw[2], ms_ref)
    total = [jnp.zeros(shape, jnp.float32) for _ in range(3)]

    def add(total, beside, weight):
        coupling = 2.0 * here[3] * beside[3] / (here[3] + beside[3]) * weight
        return [total[c] + coupling * (beside[c] - here[c]) for c in range(3)]

    one = jnp.float32(1.0)
    zero = jnp.float32(0.0)
    for shift, edge, there in ((1, 0, gx > 0), (width - 1, width - 1, gx < count_x - 1)):
        beside = [
            jnp.where(lane == edge, pltpu.roll(s, shift, 2), pltpu.roll(h, shift, 2))
            for s, h in zip(side, here)
        ]
        weight = jnp.where(lane == edge, jnp.where(there, one, zero), one) * side_weight
        total = add(total, beside, weight)
    for shift, edge, there in ((1, 0, gy > 0), (height - 1, height - 1, gy < count_y - 1)):
        beside = [
            jnp.where(row == edge, pltpu.roll(s, shift, 1), pltpu.roll(h, shift, 1))
            for s, h in zip(above, here)
        ]
        weight = jnp.where(row == edge, jnp.where(there, one, zero), one) * side_weight
        total = add(total, beside, weight)
    for part in range(3):
        unit_ref[part] = here[part]
    for z in range(depth):
        out = [total[c][z] for c in range(3)]
        for other in (z - 1, z + 1):
            if 0 <= other < depth:
                a, b = here[3][z], here[3][other]
                coupling = 2.0 * a * b / (a + b) * layer_weight
                out = [out[c] + coupling * (here[c][other] - here[c][z]) for c in range(3)]
        for c in range(3):
            exchange_ref[c, z] = out[c] / saturation[z]


def cross(first, second):
    return [
        first[1] * second[2] - first[2] * second[1],
        first[2] * second[0] - first[0] * second[2],
        first[0] * second[1] - first[1] * second[0],
    ]


def final_kernel(count_x, *refs):
    part_refs, (exchange_ref, unit_ref, field_ref, predicted_ref) = refs[:count_x], refs[count_x:]
    rows = unit_ref.shape[1] * unit_ref.shape[2]
    demag = []
    for c in range(3):
        place = slice(c * rows, (c + 1) * rows)
        total = part_refs[0][place]
        for part_ref in part_refs[1:]:
            total = total + part_ref[place]
        demag.append(total)
    predict(demag, exchange_ref, unit_ref, field_ref, predicted_ref)


def predict(demag, exchange_ref, unit_ref, field_ref, predicted_ref):
    depth, height, width = unit_ref.shape[1:]
    unit, field = [], []
    for c in range(3):
        field.append(exchange_ref[c] + demag[c].reshape(depth, height, width))
        unit.append(unit_ref[c])
        field_ref[c] = field[c]
    twist = cross(unit, field)
    second = cross(unit, twist)
    moved = [
        unit[c] - (time_step / (1.0 + damping * damping)) * (twist[c] + damping * second[c])
        for c in range(3)
    ]
    length = jnp.sqrt(moved[0] * moved[0] + moved[1] * moved[1] + moved[2] * moved[2])
    for c in range(3):
        predicted_ref[c] = moved[c] / length


def sorted_table(count_x, count_y, width, rows):
    place = sorted_cells(width).reshape(2, 1, width // 2)
    place = (place + np.arange(count_x)[None, :, None] * width)[..., None, None, None]
    wave = np.arange(count_y)[:, None, None] * rows + np.arange(rows)[None, None, :]
    length = 2 * count_x * width
    angle = (place * wave % length) * (2.0 * math.pi / length)
    table = np.concatenate([np.cos(angle), -np.sin(angle)], -2)
    return np.stack(split_table(table.reshape(2, count_x, width // 2, count_y * 2 * rows)))


def sorted_cells(width):
    return (np.array([0, 2, 1, 3])[:, None] + 4 * np.arange(width // 4)[None, :]).reshape(width)


def sorting_kernel(order_x, *refs):
    theta_ref, phi_ref, labels_ref, region_ref, place, sort_ref = refs[:6]
    out_refs, (first_ref, last_ref) = refs[6:-8], refs[-8:-6]
    angle, label, region, sort, layers, sems = refs[-6:]
    copies = [
        pltpu.make_async_copy(theta_ref, angle.at[0], sems.at[0]),
        pltpu.make_async_copy(phi_ref, angle.at[1], sems.at[1]),
        pltpu.make_async_copy(labels_ref, label, sems.at[2]),
        pltpu.make_async_copy(region_ref, region, sems.at[3]),
        pltpu.make_async_copy(sort_ref, sort, sems.at[4]),
    ]
    for copy in copies:
        copy.start()
    for copy in copies:
        copy.wait()
    gx = place[0]
    depth, height, width = label.shape
    raw = [angle[0], angle[1], label[...].astype(jnp.float32)]
    saturation = looked_up(raw[2], region)
    rows = depth * height
    moment = [(part * saturation).reshape(rows, width) for part in directions(raw[0], raw[1])]
    high, low = split_high(jnp.concatenate(moment, 0))
    both = dot(jnp.concatenate([high, low], 0), sort[...])
    moment = both[: 3 * rows] + both[3 * rows :]
    for c in range(3):
        layers[:, c * height : (c + 1) * height] = moment[c * rows : (c + 1) * rows].reshape(
            depth, height, width
        )
    lane = lax.broadcasted_iota(jnp.int32, (height, width), 1)
    sides = []
    for column in (0, width - 1):
        side = jnp.zeros((height, width), jnp.float32)
        for field in range(3):
            for z in range(depth):
                value = raw[field][z][:, column : column + 1]
                side = jnp.where(lane == field * depth + z, value, side)
        sides.append(side)
    for spot, number in enumerate(order_x):
        other = lax.bitwise_xor(gx, number)
        out_refs[spot][: 3 * height] = layers[other]
        out_refs[spot][3 * height :] = jnp.where(other > gx, sides[1], sides[0])
    for field in range(3):
        first_ref[field] = raw[field][:, 0]
        last_ref[field] = raw[field][:, height - 1]


def fetch_kernel(table_ref, table, sems):
    copies = [
        pltpu.make_async_copy(table_ref.at[half, parity], table.at[half, parity], sems.at[half, parity])
        for half in range(2)
        for parity in range(2)
    ]
    for copy in copies:
        copy.start()
    for copy in copies:
        copy.wait()


def pair_sign(lanes):
    spot = lax.broadcasted_iota(jnp.int32, (1, lanes), 1)
    return jnp.where((spot & 64) == 0, 1.0, -1.0).astype(jnp.float32)


def turn_all(value, sign):
    lanes = value.shape[1]
    return jnp.concatenate([turn(value[:, i : i + 128], sign) for i in range(0, lanes, 128)], 1)


def layer_lines_kernel(order_x, *refs):
    count_x = len(order_x)
    chunk_refs, (place, table, out_ref, blocks) = refs[:count_x], refs[count_x:]
    gx = place[0]
    rows = blocks.shape[1]
    for spot, number in enumerate(order_x):
        blocks[lax.bitwise_xor(gx, number)] = chunk_refs[spot][:rows]
    sums = []
    for parity in range(2):
        value = jnp.concatenate(
            [blocks[g, :, parity * 128 : (parity + 1) * 128] for g in range(count_x)], 1
        )
        flipped = value * pair_sign(value.shape[1])
        high, low = split_high(jnp.concatenate([value, flipped], 0))
        wide = table[0, parity].reshape(value.shape[1], -1)
        fine = table[1, parity].reshape(value.shape[1], -1)
        both = dot(jnp.concatenate([high, low], 0), wide)
        sums.append(both[: 2 * rows] + both[2 * rows :] + dot(high, fine))
    sign = pair_sign(128)
    even, even_flipped = sums[0][:rows], sums[0][rows:]
    odd, odd_turned = sums[1][:rows], turn_all(sums[1][rows:], sign)
    waves = [even + odd, even_flipped + odd_turned, even - odd, even_flipped - odd_turned]
    count_y = out_ref.shape[0] // count_x
    for g in range(count_x):
        for y in range(count_y):
            out_ref[g * count_y + y] = waves[g][:, y * 128 : (y + 1) * 128]


def layer_back_kernel(order_x, *refs):
    count_x = len(order_x)
    (spec_ref, place, table), out_refs, blocks = refs[:3], refs[3:-1], refs[-1]
    gx = place[0]
    rows = spec_ref.shape[1]
    count_y = spec_ref.shape[0] // count_x
    w0, w1, w2, w3 = [
        jnp.concatenate([spec_ref[g * count_y + y] for y in range(count_y)], 1)
        for g in range(count_x)
    ]
    sign = pair_sign(128)
    even, odd = w0 + w2, w1 + w3
    cross_even, cross_odd = w0 - w2, turn_all(w1 - w3, sign)
    pairs = [(even + odd, even - odd), (cross_even - cross_odd, cross_even + cross_odd)]
    for parity in range(2):
        high, low = split_high(jnp.concatenate(pairs[parity], 0))
        wide = table[0, parity].reshape(count_x * 128, -1)
        fine = table[1, parity].reshape(count_x * 128, -1)
        both = dot(jnp.concatenate([high, low], 0), wide, ((1,), (1,)))
        both = both[: 2 * rows] + both[2 * rows :] + dot(high, fine, ((1,), (1,)))
        value = jnp.where(pair_sign(both.shape[1]) > 0.0, both[:rows], both[rows:])
        for g in range(count_x):
            blocks[g, :, parity * 128 : (parity + 1) * 128] = value[:, g * 128 : (g + 1) * 128]
    for spot, number in enumerate(order_x):
        out_refs[spot][...] = blocks[lax.bitwise_xor(gx, number)]


def layer_waves_kernel(scale, count_y, spec_ref, *refs):
    tables, out_ref, scratch = refs[:3], refs[3], refs[4:]
    count, lines, lanes = spec_ref.shape
    depth, local = count // count_y, lines // 3

    def place(plane):
        c, z = divmod(plane, depth)
        return slice(z * count_y, (z + 1) * count_y), slice(c * local, (c + 1) * local)

    def read(plane):
        blocks, rows = place(plane)
        return spec_ref[blocks, rows].reshape(count_y * local, lanes)

    def write(plane, value):
        blocks, rows = place(plane)
        out_ref[blocks, rows] = value.reshape(count_y, local, lanes)

    waves(scale, count_y * local, 3 * depth, lanes, read, write, tables, scratch)


def layer_exchange_kernel(order_x, count_y, *refs):
    count_x = len(order_x)
    theta_ref, phi_ref, labels_ref, before_ref, after_ref = refs[:5]
    chunk_refs, (place, ms_ref, aex_ref, exchange_ref, unit_ref) = refs[5:-5], refs[-5:]
    depth, height, width = shape = theta_ref.shape
    gx, gy = place[0], place[1]
    lane = lax.broadcasted_iota(jnp.int32, shape, 2)
    row = lax.broadcasted_iota(jnp.int32, shape, 1)

    def side_tile(other):
        value = None
        for spot, number in enumerate(order_x[1:]):
            tile = chunk_refs[spot][3 * height :]
            match = lax.bitwise_xor(gx, number) == other
            value = tile if value is None else jnp.where(match, tile, value)
        return value

    def spread(tile, field):
        columns = [tile[:, field * depth + z : field * depth + z + 1] for z in range(depth)]
        return jnp.stack([jnp.broadcast_to(c, (height, width)) for c in columns])

    left, right = side_tile(gx - 1), side_tile(gx + 1)
    raw = [theta_ref[...], phi_ref[...], labels_ref[...].astype(jnp.float32)]
    side = [jnp.where(lane == 0, spread(right, f), spread(left, f)) for f in range(3)]
    above = [
        jnp.where(
            row == 0,
            jnp.broadcast_to(after_ref[f][:, None, :], shape),
            jnp.broadcast_to(before_ref[f][:, None, :], shape),
        )
        for f in range(3)
    ]
    exchange(raw, side, above, (gx, count_x, gy, count_y), ms_ref, aex_ref, exchange_ref, unit_ref)


def layer_final_kernel(order_x, *refs):
    count_x = len(order_x)
    part_refs, (place, unsort, exchange_ref, unit_ref) = refs[:count_x], refs[count_x : count_x + 4]
    field_ref, predicted_ref, layers = refs[count_x + 4 :]
    gx = place[0]
    depth, height, width = unit_ref.shape[1:]
    for spot, number in enumerate(order_x):
        layers[lax.bitwise_xor(gx, number)] = part_refs[spot][...]
    value = jnp.concatenate(
        [layers[:, c * height : (c + 1) * height].reshape(depth * height, width) for c in range(3)], 0
    )
    high = value.astype(jnp.bfloat16)
    rest = value - high.astype(jnp.float32)
    middle, low = split_high(rest)
    rows = value.shape[0]
    sorted_back = dot(jnp.concatenate([high, middle, low], 0), unsort[...])
    value = sorted_back[:rows] + (sorted_back[rows : 2 * rows] + sorted_back[2 * rows :])
    size = depth * height
    predict(
        [value[c * size : (c + 1) * size] for c in range(3)],
        exchange_ref,
        unit_ref,
        field_ref,
        predicted_ref,
    )


vmem = pl.BlockSpec(memory_space=pltpu.VMEM)
smem = pl.BlockSpec(memory_space=pltpu.SMEM)
hbm = pl.BlockSpec(memory_space=pltpu.HBM)


def call(body, out, ins, operands, scratch=(), flops=0, name=None, grant=16 << 20):
    operands = [
        pltpu.with_memory_space_constraint(o, pltpu.HBM) if i is hbm else o
        for i, o in zip(ins, operands)
    ]
    size = sum(math.prod(o.shape) * o.dtype.itemsize for o in operands)
    outs = out if isinstance(out, (list, tuple)) else [out]
    size += sum(math.prod(o.shape) * jnp.dtype(o.dtype).itemsize for o in outs)
    return pl.pallas_call(
        body,
        out_shape=out,
        in_specs=ins,
        out_specs=[vmem] * len(outs) if outs is out else vmem,
        scratch_shapes=list(scratch),
        compiler_params=pltpu.CompilerParams(vmem_limit_bytes=grant),
        cost_estimate=pl.CostEstimate(flops=flops, bytes_accessed=size, transcendentals=0),
        name=name,
    )(*operands)


def f32(*shape):
    return jax.ShapeDtypeStruct(shape, jnp.float32)


def exchanged(chunks, axis, order):
    devices = len(order)
    out = [chunks[0]] + [None] * (devices - 1)
    for spot, number in enumerate(order[1:]):
        pairs = [(i, i ^ number) for i in range(devices)]
        out[spot + 1] = lax.ppermute(chunks[spot + 1], axis, pairs)
    return out


def partners(devices):
    return [0] + list(range(devices - 1, 0, -1))


def tensor_here(kernel):
    rows, columns = kernel.shape[2:]
    twice = np.concatenate([np.eye(rows), np.eye(rows)], 1).astype(ml_dtypes.bfloat16)
    return call(
        tensor_kernel,
        jax.ShapeDtypeStruct((48, columns, 2 * rows), jnp.bfloat16),
        [vmem, vmem],
        (kernel.reshape(48, rows, columns), jnp.asarray(twice)),
        flops=48 * 4 * rows * rows * columns,
        name="tensor",
    )


def per_layer(theta, phi, labels, ms_region, aex_region, kernel):
    count_x, count_y = lax.axis_size("gx"), lax.axis_size("gy")
    depth, height, width = theta.shape
    rows = kernel.shape[2]
    lanes = 2 * rows
    whole_y = count_y * height
    lines = 3 * height
    cells, edge = f32(3, depth, height, width), f32(3, depth, width)
    order_x = partners(count_x)
    place = jnp.stack([lax.axis_index("gx"), lax.axis_index("gy")]).astype(jnp.int32)
    sort = np.eye(width)[:, sorted_cells(width)]
    table = jnp.asarray(sorted_table(count_x, count_y, width, rows))
    forward, inverse = [jnp.asarray(t[0]) for t in column_tables(count_y, height, range(count_y))]
    transform_flops = 6 * lines * count_x * width * count_y * lanes

    *chunks, first, last = call(
        functools.partial(sorting_kernel, order_x),
        [f32(lines + height, width)] * count_x + [edge, edge],
        [hbm] * 4 + [smem, hbm],
        (theta, phi, labels, ms_region, place, jnp.asarray(sort.astype(ml_dtypes.bfloat16))),
        scratch=(
            pltpu.VMEM((2, depth, height, width), jnp.float32),
            pltpu.VMEM((depth, height, width), jnp.int32),
            pltpu.SMEM(ms_region.shape, jnp.float32),
            pltpu.VMEM((width, width), jnp.bfloat16),
            pltpu.VMEM((depth, lines, width), jnp.float32),
            pltpu.SemaphoreType.DMA((5,)),
        ),
        name="sort",
    )
    chunks = exchanged(chunks, "gx", order_x)
    table = call(
        fetch_kernel,
        [pltpu.VMEM(table.shape, jnp.bfloat16)],
        [hbm],
        (table,),
        scratch=(pltpu.SemaphoreType.DMA((2, 2)),),
        name="fetch",
    )[0]
    tensor = tensor_here(kernel)
    spectrum = call(
        functools.partial(layer_lines_kernel, order_x),
        f32(count_x * count_y, lines, lanes),
        [vmem] * count_x + [smem, vmem],
        (*chunks, place, table),
        scratch=(pltpu.VMEM((count_x, lines, width), jnp.float32),),
        flops=transform_flops,
        name="lines",
    )
    spectrum, first, last = lax.optimization_barrier((spectrum, first, last))
    axes = ("gx", "gy")
    columns = lax.all_to_all(spectrum, axes, split_axis=0, concat_axis=0, tiled=True)
    scale = -1.0 / (2 * depth * 2 * whole_y * 2 * count_x * width)
    images = call(
        functools.partial(layer_waves_kernel, scale, count_y),
        f32(count_x * count_y, lines, lanes),
        [vmem] * 4,
        (columns, tensor, forward, inverse),
        scratch=(
            pltpu.VMEM((2 * whole_y, 3 * depth * lanes), jnp.float32),
            pltpu.VMEM((6 * whole_y, 3 * depth * lanes), jnp.bfloat16),
        ),
        flops=20 * whole_y * whole_y * 3 * depth * lanes,
        name="waves",
    )
    returned = lax.all_to_all(images, axes, split_axis=0, concat_axis=0, tiled=True)
    up = [(i, i + 1) for i in range(count_y - 1)]
    before = lax.ppermute(last, "gy", up)
    after = lax.ppermute(first, "gy", [(j, i) for i, j in up])
    exchange_field, unit = call(
        functools.partial(layer_exchange_kernel, order_x, count_y),
        [cells, cells],
        [vmem] * (4 + count_x) + [smem] * 3,
        (theta, phi, labels, before, after, *chunks[1:], place, ms_region, aex_region),
        flops=300 * depth * height * width,
        name="exchange",
    )
    returned, exchange_field, unit = lax.optimization_barrier((returned, exchange_field, unit))
    partial = call(
        functools.partial(layer_back_kernel, order_x),
        [f32(lines, width)] * count_x,
        [vmem, smem, vmem],
        (returned, place, table),
        scratch=(pltpu.VMEM((count_x, lines, width), jnp.float32),),
        flops=transform_flops,
        name="back_lines",
    )
    parts = exchanged(partial, "gx", order_x)
    return call(
        functools.partial(layer_final_kernel, order_x),
        [cells, cells],
        [vmem] * count_x + [smem] + [vmem] * 3,
        (*parts, place, jnp.asarray(sort.T.astype(ml_dtypes.bfloat16)), exchange_field, unit),
        scratch=(pltpu.VMEM((depth, lines, width), jnp.float32),),
        flops=60 * depth * height * width,
        name="predict",
    )


def per_device(theta, phi, labels, ms_region, aex_region, kernel):
    count_x, count_y = lax.axis_size("gx"), lax.axis_size("gy")
    gx, gy = lax.axis_index("gx"), lax.axis_index("gy")
    depth, height, width = theta.shape
    rows = kernel.shape[2]
    lanes = 2 * rows
    if count_x == depth == 4 and lanes == 128 and width == 256 and height == 8:
        return tuple(per_layer(theta, phi, labels, ms_region, aex_region, kernel))
    lines = 3 * depth * height
    whole_y = count_y * height

    place = jnp.stack([gx, gy]).astype(jnp.int32)
    cells = f32(3, depth, height, width)
    order_x, order_y = partners(count_x), partners(count_y)
    table = line_table(count_x, count_y, width, rows)
    if table is None:
        table = line_table_here(count_x, width, rows, order_y)
        columns_tables = column_tables_here(count_y, height, order_y)
    else:
        columns_tables = column_tables(count_y, height, order_y)
    sources = [jnp.asarray(t) for t in (table, *columns_tables)]
    transform_flops = 6 * lines * count_x * width * count_y * lanes

    packed = call(
        pack_kernel,
        cells,
        [hbm] * 3,
        (theta, phi, labels),
        scratch=(
            pltpu.VMEM((2, depth, height, width), jnp.float32),
            pltpu.VMEM((depth, height, width), jnp.int32),
            pltpu.SemaphoreType.DMA((3,)),
        ),
        name="pack",
    )
    gathered = exchanged([packed] * count_x, "gx", order_x)
    table, forward, inverse = call(
        functools.partial(load_kernel, order_x, order_y),
        [
            pltpu.VMEM((2, count_x, width, count_y * lanes), jnp.bfloat16),
            pltpu.VMEM(sources[1].shape[1:], jnp.bfloat16),
            pltpu.VMEM(sources[2].shape[1:], jnp.bfloat16),
        ],
        [smem] + [hbm] * 3,
        (place, *sources),
        scratch=(pltpu.SemaphoreType.DMA((2 + count_x * count_y,)),),
        name="load",
    )

    tensor = tensor_here(kernel)
    gathered, tensor = lax.optimization_barrier((gathered, tensor))
    edge_rows = 3 * depth * width // lanes
    spectrum = call(
        functools.partial(lines_kernel, count_x, order_y),
        [f32(lines + (edge_rows if n in meeting(count_y) else 0), lanes) for n in order_y],
        [vmem] * count_x + [hbm, smem, vmem],
        (*gathered, ms_region, place, table),
        scratch=(pltpu.SMEM(ms_region.shape, jnp.float32), pltpu.SemaphoreType.DMA),
        flops=transform_flops,
        name="lines",
    )
    columns = exchanged(spectrum, "gy", order_y)
    scale = -1.0 / (2 * depth * 2 * whole_y * 2 * count_x * width)
    waves = call(
        functools.partial(waves_kernel, scale, count_y),
        [f32(lines, lanes)] * count_y,
        [vmem] * (count_y + 3),
        (*columns, tensor, forward, inverse),
        scratch=(
            pltpu.VMEM((2 * whole_y, 3 * depth * lanes), jnp.float32),
            pltpu.VMEM((6 * whole_y, 3 * depth * lanes), jnp.bfloat16),
        ),
        flops=20 * whole_y * whole_y * 3 * depth * lanes,
        name="waves",
    )
    returned = exchanged(waves, "gy", order_y)
    partial = call(
        functools.partial(back_lines_kernel, count_x, count_y),
        [f32(lines, width)] * count_x,
        [vmem] * (count_y + 1),
        (*returned, table),
        flops=transform_flops,
        name="back_lines",
    )
    edges = [columns[order_y.index(number)] for number in meeting(count_y)]
    edges, partial = lax.optimization_barrier((edges, partial))
    exchange_field, unit = call(
        functools.partial(exchange_kernel, order_x, count_y),
        [cells, cells],
        [vmem] * (count_x + len(edges)) + [smem] * 3,
        (*gathered, *edges, place, ms_region, aex_region),
        scratch=(pltpu.VMEM((count_x, 3, depth, height, width), jnp.float32),),
        flops=300 * depth * height * width,
        name="exchange",
    )
    parts = exchanged(partial, "gx", order_x)
    field, predicted = call(
        functools.partial(final_kernel, count_x),
        [cells, cells],
        [vmem] * (count_x + 2),
        (*parts, exchange_field, unit),
        flops=60 * depth * height * width,
        name="predict",
    )
    return field, predicted


def solution(mesh):
    in_specs = (
        P(None, "gy", "gx"),
        P(None, "gy", "gx"),
        P(None, "gy", "gx"),
        P(),
        P(),
        P(None, None, ("gx", "gy"), None),
    )
    out_specs = (P(None, None, "gy", "gx"), P(None, None, "gy", "gx"))
    return jax.shard_map(
        per_device, mesh=mesh, in_specs=in_specs, out_specs=out_specs, check_vma=False
    )
```

```python
import functools
import math

import jax
import jax.numpy as jnp
import ml_dtypes
import numpy as np
from jax import lax
from jax.experimental import pallas as pl
from jax.experimental.pallas import tpu as pltpu
from jax.sharding import PartitionSpec as P

damping = 0.5
time_step = 0.2
side_weight = 0.25
layer_weight = 0.5
root_half = math.sqrt(0.5)
constant_limit = 20 << 20


def split_high(value):
    high = value.astype(jnp.bfloat16)
    low = (value - high.astype(jnp.float32)).astype(jnp.bfloat16)
    return high, low


def split_table(table):
    high = table.astype(np.float32).astype(ml_dtypes.bfloat16)
    low = (table - high.astype(np.float64)).astype(np.float32).astype(ml_dtypes.bfloat16)
    return high, low


def dot(left, right, contract=((1,), (0,))):
    return lax.dot_general(left, right, (contract, ((), ())), preferred_element_type=jnp.float32)


def line_table(count_x, count_y, width, rows):
    cells = count_x * width
    if count_x * 2 * cells * count_y * 2 * rows * 2 > constant_limit:
        return None
    place = np.arange(cells)[None, None, :, None]
    wave = (
        np.arange(count_x)[:, None, None, None] * (count_y * rows)
        + np.arange(count_y)[None, :, None, None] * rows
        + np.arange(rows)[None, None, None, :]
    )
    angle = (place * wave % (2 * cells)) * (2.0 * math.pi / (2 * cells))
    table = np.concatenate([np.cos(angle), -np.sin(angle)], 3)
    table = table.reshape(count_x, count_y, count_x, width, 2 * rows)
    high, low = split_table(table)
    return np.stack([high, low], 2)


def line_table_here(count_x, width, rows, order):
    cells = count_x * width
    count_y = len(order)
    place = jnp.arange(cells, dtype=jnp.int32)[:, None, None]
    block = lax.bitwise_xor(lax.axis_index("gy"), jnp.array(order, jnp.int32))
    wave = (
        lax.axis_index("gx") * (count_y * rows)
        + block[None, :, None] * rows
        + jnp.arange(rows, dtype=jnp.int32)[None, None, :]
    )
    angle = (place * wave % (2 * cells)).astype(jnp.float32) * (math.pi / cells)
    table = jnp.concatenate([jnp.cos(angle), -jnp.sin(angle)], 2)
    table = table.reshape(1, 1, count_x, width, count_y * 2 * rows)
    return jnp.stack(split_high(table), 2)


def column_tables(count_y, local, order):
    height = count_y * local
    wave = np.arange(2 * height)
    block = np.arange(count_y)[:, None] ^ np.array(order)[None, :]
    place = (block[:, :, None] * local + np.arange(local)).reshape(count_y, height)
    angle = (wave[None, :, None] * place[:, None, :] % (2 * height)) * (math.pi / height)
    high, low = split_table(np.concatenate([np.cos(angle), np.sin(angle)], 2))
    forward = np.concatenate([high, high, low], 2)
    angle = angle.transpose(0, 2, 1)
    high, low = split_table(np.concatenate([np.cos(angle), np.sin(angle)], 1))
    inverse = np.concatenate([high, high, low], 2)
    return forward, inverse


def column_tables_here(count_y, local, order):
    height = count_y * local
    wave = jnp.arange(2 * height, dtype=jnp.int32)
    block = lax.bitwise_xor(lax.axis_index("gy"), jnp.array(order, jnp.int32))
    place = (block[:, None] * local + jnp.arange(local, dtype=jnp.int32)).reshape(height)
    angle = (wave[:, None] * place % (2 * height)).astype(jnp.float32) * (math.pi / height)
    high, low = split_high(jnp.concatenate([jnp.cos(angle), jnp.sin(angle)], 1))
    forward = jnp.concatenate([high, high, low], 1)
    high, low = split_high(jnp.concatenate([jnp.cos(angle.T), jnp.sin(angle.T)], 0))
    inverse = jnp.concatenate([high, high, low], 1)
    return forward[None], inverse[None]


def load_kernel(order_x, order_y, place, *refs):
    table_ref, forward_ref, inverse_ref, table, forward, inverse, sem = refs
    gx, gy = place[0], place[1]
    mine_x = gx if table_ref.shape[0] > 1 else 0
    mine_y = gy if forward_ref.shape[0] > 1 else 0
    lanes = table_ref.shape[5]
    copies = [
        pltpu.make_async_copy(forward_ref.at[mine_y], forward, sem.at[0]),
        pltpu.make_async_copy(inverse_ref.at[mine_y], inverse, sem.at[1]),
    ]
    for spot_x, number_x in enumerate(order_x):
        block_x = lax.bitwise_xor(gx, number_x)
        for spot_y in range(table_ref.shape[1]):
            block_y = lax.bitwise_xor(gy, order_y[spot_y]) if table_ref.shape[1] > 1 else 0
            columns = slice(spot_y * lanes, (spot_y + 1) * lanes)
            copies.append(
                pltpu.make_async_copy(
                    table_ref.at[mine_x, block_y, :, block_x],
                    table.at[:, spot_x, :, columns],
                    sem.at[len(copies)],
                )
            )
    for copy in copies:
        copy.start()
    for copy in copies:
        copy.wait()


def sine_cosine(angle):
    turns = jnp.floor(angle * (2.0 / math.pi) + 0.5)
    rest = angle - turns * 1.5703125
    rest = rest - turns * 4.8351287841796875e-4
    rest = rest - turns * 3.1385570764541626e-7
    square = rest * rest
    sine = rest + rest * square * (
        -1.6666654611e-1 + square * (8.3321608736e-3 - square * 1.9515295891e-4)
    )
    cosine = (
        1.0
        - 0.5 * square
        + square * square * (4.166664568298827e-2 + square * (-1.388731625493765e-3 + square * 2.443315711809948e-5))
    )
    quarter = turns.astype(jnp.int32)
    odd = (quarter & 1) == 1
    out_sine = jnp.where(odd, cosine, sine)
    out_cosine = jnp.where(odd, sine, cosine)
    out_sine = jnp.where((quarter & 2) == 2, -out_sine, out_sine)
    out_cosine = jnp.where(((quarter + 1) & 2) == 2, -out_cosine, out_cosine)
    return out_sine, out_cosine


def directions(theta, phi):
    lateral, axial = sine_cosine(theta)
    sine, cosine = sine_cosine(phi)
    return [lateral * cosine, lateral * sine, axial]


def looked_up(labels, region):
    result = jnp.zeros_like(labels) + region[0]
    for index in range(1, region.shape[0]):
        result = jnp.where(labels == float(index), region[index], result)
    return result


def pack_kernel(theta_ref, phi_ref, labels_ref, raw_ref, angle, label, sems):
    copies = [
        pltpu.make_async_copy(theta_ref, angle.at[0], sems.at[0]),
        pltpu.make_async_copy(phi_ref, angle.at[1], sems.at[1]),
        pltpu.make_async_copy(labels_ref, label, sems.at[2]),
    ]
    for copy in copies:
        copy.start()
    for copy in copies:
        copy.wait()
    for index, value in enumerate((angle[0], angle[1], label[...].astype(jnp.float32))):
        raw_ref[index] = value


def lines_kernel(count_x, order_y, far, *refs):
    raw_refs, (region_ref, place, table) = refs[:count_x], refs[count_x : count_x + 3]
    out_refs, (both_ref, region, sem) = refs[count_x + 3 : -3], refs[-3:]
    fetch = pltpu.make_async_copy(region_ref, region, sem)
    fetch.start()
    units = [directions(raw_ref[0], raw_ref[1]) for raw_ref in raw_refs]
    fetch.wait()
    for number in range(count_x):
        saturation = looked_up(raw_refs[number][2], region)
        rows = saturation.shape[0] * saturation.shape[1]
        block = [(part * saturation).reshape(rows, -1) for part in units[number]]
        high, low = split_high(jnp.concatenate(block, 0))
        both_ref[number] = jnp.concatenate([high, low], 0)
    put_chunks(both_ref, table, raw_refs[0], place[1], order_y, 0, out_refs)


def near_lines_kernel(order_y, far, both_ref, raw_ref, place, table, *out_refs):
    put_chunks(both_ref, table, raw_ref, place[1], order_y, far, out_refs)


def put_chunks(both_ref, table, raw_ref, gy, order_y, start, out_refs):
    lines, lanes = both_ref.shape[1] // 2, out_refs[-1].shape[1]
    columns = slice(start * lanes, (start + len(out_refs)) * lanes)
    total = None
    for number in range(both_ref.shape[0]):
        both = dot(both_ref[number], table[0, number, :, columns])
        part = both[:lines] + both[lines:] + dot(both_ref[number, :lines], table[1, number, :, columns])
        total = part if total is None else total + part
    last_row = raw_ref.shape[2] - 1
    for spot, out_ref in enumerate(out_refs):
        out_ref[:lines] = total[:, spot * lanes : (spot + 1) * lanes]
        number = order_y[start + spot]
        if number in meeting(len(order_y)):
            up = lax.bitwise_xor(gy, number) > gy
            for field in range(3):
                value = raw_ref[field]
                edge = jnp.where(up, value[:, last_row], value[:, 0])
                put_edge(out_ref, lines, field, edge)


def meeting(devices):
    return [number for number in range(1, devices) if (number & (number + 1)) == 0]


def edge_spots(depth, width, lanes, start, field):
    pieces = width // lanes
    return [start + (field * pieces + piece) * depth for piece in range(pieces)]


def put_edge(ref, start, field, edge):
    lanes = ref.shape[1]
    for piece, row in enumerate(edge_spots(*edge.shape, lanes, start, field)):
        ref[row : row + edge.shape[0]] = edge[:, piece * lanes : (piece + 1) * lanes]


def get_edge(ref, depth, width, start, field):
    spots = edge_spots(depth, width, ref.shape[1], start, field)
    return jnp.concatenate([ref[row : row + depth] for row in spots], 1)


def back_lines_kernel(numbers, count_y, *refs):
    in_refs, table, out_refs = refs[:count_y], refs[count_y], refs[count_y + 1 :]
    high, low = split_high(jnp.concatenate([ref[...] for ref in in_refs], 1))
    both = jnp.concatenate([high, low], 0)
    lines = high.shape[0]
    for number, out_ref in zip(numbers, out_refs):
        wide = dot(both, table[0, number], ((1,), (1,)))
        out_ref[...] = wide[:lines] + wide[lines:] + dot(high, table[1, number], ((1,), (1,)))


def tensor_kernel(kernel_ref, twice_ref, out_ref):
    twice = twice_ref[...]

    unroll = 8

    def step(index, carry):
        for offset in range(unroll):
            turned = dot(kernel_ref[index * unroll + offset], twice, ((0,), (0,)))
            out_ref[index * unroll + offset] = turned.astype(jnp.bfloat16)
        return carry

    lax.fori_loop(0, kernel_ref.shape[0] // unroll, step, 0)


def turn(value, sign):
    lanes = value.shape[-1]
    if lanes == 128:
        return pltpu.roll(value, lanes // 2, value.ndim - 1) * sign
    return jnp.concatenate([value[..., lanes // 2 :], value[..., : lanes // 2]], -1) * sign


def layers_forward(layer, sign):
    d0, d1, d2, d3 = layer
    r2 = turn(d2, sign)
    near, far = d1 + d3, d1 - d3
    far_turned = turn(far, sign)
    near_turned = turn(near, sign)
    even, odd = d0 + d2, d0 - d2
    out = [None] * 8
    out[0], out[4] = even + near, even - near
    out[2], out[6] = odd + far_turned, odd - far_turned
    plus, minus = d0 + r2, d0 - r2
    first = (far + near_turned) * root_half
    second = (near_turned - far) * root_half
    out[1], out[5] = plus + first, plus - first
    out[3], out[7] = minus + second, minus - second
    return out


def layers_inverse(wave, sign):
    a, b = wave[0] + wave[4], wave[0] - wave[4]
    e, f = wave[2] + wave[6], turn(wave[2] - wave[6], sign)
    p, q = wave[1] + wave[5], wave[1] - wave[5]
    s, t = wave[3] + wave[7], turn(wave[3] - wave[7], sign)
    o0, o1, o2, o3 = p + s, q - t, p - s, q + t
    return [
        a + e + o0,
        b - f + (o1 - turn(o1, sign)) * root_half,
        a - e - turn(o2, sign),
        b + f - (o3 + turn(o3, sign)) * root_half,
    ]


def apply_tensor(tensor, wave):
    out = [[], [], []]
    for level in range(8):
        xx, yy, zz, xy, xz, yz = [tensor[part][level] for part in range(6)]
        x, y, z = wave[0][level], wave[1][level], wave[2][level]
        out[0].append(xx * x + xy * y + xz * z)
        out[1].append(xy * x + yy * y + yz * z)
        out[2].append(xz * x + yz * y + zz * z)
    return out


def waves_kernel(scale, count_y, *refs):
    spec_refs, (tensor_ref, forward_ref, inverse_ref) = refs[:count_y], refs[count_y : count_y + 3]
    out_refs, (wave_ref, back_ref) = refs[count_y + 3 : -2], refs[-2:]
    lines, lanes = out_refs[0].shape
    local = 8
    planes = lines // local
    height = count_y * local
    sign = jnp.where(
        lax.broadcasted_iota(jnp.int32, (1, lanes), 1) < lanes // 2, 1.0, -1.0
    ).astype(jnp.float32)
    columns = []
    for plane in range(planes):
        value = jnp.concatenate(
            [spec_ref[plane * local : (plane + 1) * local] for spec_ref in spec_refs], 0
        )
        value = jnp.concatenate([value, turn(value, sign)], 0)
        high, low = split_high(value)
        columns.append(jnp.concatenate([high, low, high], 0))
    wave_ref[...] = dot(forward_ref[...], jnp.concatenate(columns, 1))

    chunk = 16
    depth = planes // 3
    double = 2 * height

    def step(index, carry):
        rows = pl.ds(pl.multiple_of(index * chunk, chunk), chunk)
        wave = []
        for part in range(3):
            layer = [
                wave_ref[rows, (part * depth + z) * lanes : (part * depth + z + 1) * lanes]
                for z in range(depth)
            ]
            wave.append(layers_forward(layer, sign))
        tensor = [
            [tensor_ref[part * 8 + level, rows, :].astype(jnp.float32) for level in range(8)]
            for part in range(6)
        ]
        image = apply_tensor(tensor, wave)
        for part in range(3):
            layer = layers_inverse(image[part], sign)
            for z in range(depth):
                spot = slice((part * depth + z) * lanes, (part * depth + z + 1) * lanes)
                high, low = split_high(layer[z] * scale)
                back_ref[rows, spot] = high
                back_ref[pl.ds(pl.multiple_of(double + index * chunk, chunk), chunk), spot] = low
                back_ref[pl.ds(pl.multiple_of(2 * double + index * chunk, chunk), chunk), spot] = high
        return carry

    lax.fori_loop(0, double // chunk, step, 0)
    back = dot(inverse_ref[...], back_ref[...])
    for plane in range(planes):
        part = slice(plane * lanes, (plane + 1) * lanes)
        value = back[:height, part] - turn(back[height:, part], sign)
        for number in range(count_y):
            out_refs[number][plane * local : (plane + 1) * local] = value[
                number * local : (number + 1) * local
            ]


def exchange_kernel(order_x, count_y, *refs):
    count_x, numbers = len(order_x), meeting(count_y)
    raw_refs, edge_refs, (place, ms_ref, aex_ref) = refs[:count_x], refs[count_x:-6], refs[-6:-3]
    exchange_ref, unit_ref, raw_ref = refs[-3:]
    depth, height, width = raw_ref.shape[2:]
    gx, gy = place[0], place[1]

    def row_meeting(field, other):
        value = None
        for number, edge_ref in zip(numbers, edge_refs):
            edge = get_edge(edge_ref, depth, width, 3 * depth * height, field)
            match = lax.bitwise_xor(gy, number) == other
            value = edge if value is None else jnp.where(match, edge, value)
        return jnp.broadcast_to(value[:, None, :], (depth, height, width))

    for spot, number in enumerate(order_x):
        raw_ref[lax.bitwise_xor(gx, number)] = raw_refs[spot][...]
    left, right = jnp.maximum(gx - 1, 0), jnp.minimum(gx + 1, count_x - 1)
    shape = (depth, height, width)
    lane = lax.broadcasted_iota(jnp.int32, shape, 2)
    row = lax.broadcasted_iota(jnp.int32, shape, 1)

    def quantities(values):
        return directions(values[0], values[1]) + [looked_up(values[2], aex_ref)]

    raw = [raw_refs[0][f] for f in range(3)]
    here = quantities(raw)
    side = quantities([jnp.where(lane == 0, raw_ref[right, f], raw_ref[left, f]) for f in range(3)])
    above = quantities(
        [jnp.where(row == 0, row_meeting(f, gy + 1), row_meeting(f, gy - 1)) for f in range(3)]
    )
    saturation = looked_up(raw[2], ms_ref)
    total = [jnp.zeros(shape, jnp.float32) for _ in range(3)]

    def add(total, beside, weight):
        coupling = 2.0 * here[3] * beside[3] / (here[3] + beside[3]) * weight
        return [total[c] + coupling * (beside[c] - here[c]) for c in range(3)]

    one = jnp.float32(1.0)
    zero = jnp.float32(0.0)
    for shift, edge, there in ((1, 0, gx > 0), (width - 1, width - 1, gx < count_x - 1)):
        beside = [
            jnp.where(lane == edge, pltpu.roll(s, shift, 2), pltpu.roll(h, shift, 2))
            for s, h in zip(side, here)
        ]
        weight = jnp.where(lane == edge, jnp.where(there, one, zero), one) * side_weight
        total = add(total, beside, weight)
    for shift, edge, there in ((1, 0, gy > 0), (height - 1, height - 1, gy < count_y - 1)):
        beside = [
            jnp.where(row == edge, pltpu.roll(s, shift, 1), pltpu.roll(h, shift, 1))
            for s, h in zip(above, here)
        ]
        weight = jnp.where(row == edge, jnp.where(there, one, zero), one) * side_weight
        total = add(total, beside, weight)
    for part in range(3):
        unit_ref[part] = here[part]
    for z in range(depth):
        out = [total[c][z] for c in range(3)]
        for other in (z - 1, z + 1):
            if 0 <= other < depth:
                a, b = here[3][z], here[3][other]
                coupling = 2.0 * a * b / (a + b) * layer_weight
                out = [out[c] + coupling * (here[c][other] - here[c][z]) for c in range(3)]
        for c in range(3):
            exchange_ref[c, z] = out[c] / saturation[z]


def cross(first, second):
    return [
        first[1] * second[2] - first[2] * second[1],
        first[2] * second[0] - first[0] * second[2],
        first[0] * second[1] - first[1] * second[0],
    ]


def final_kernel(count_x, *refs):
    part_refs, (exchange_ref, unit_ref, field_ref, predicted_ref) = refs[:count_x], refs[count_x:]
    depth, height, width = unit_ref.shape[1:]
    rows = depth * height
    unit, field = [], []
    for c in range(3):
        place = slice(c * rows, (c + 1) * rows)
        total = part_refs[0][place]
        for part_ref in part_refs[1:]:
            total = total + part_ref[place]
        field.append(exchange_ref[c] + total.reshape(depth, height, width))
        unit.append(unit_ref[c])
        field_ref[c] = field[c]
    twist = cross(unit, field)
    second = cross(unit, twist)
    moved = [
        unit[c] - (time_step / (1.0 + damping * damping)) * (twist[c] + damping * second[c])
        for c in range(3)
    ]
    length = jnp.sqrt(moved[0] * moved[0] + moved[1] * moved[1] + moved[2] * moved[2])
    for c in range(3):
        predicted_ref[c] = moved[c] / length


vmem = pl.BlockSpec(memory_space=pltpu.VMEM)
smem = pl.BlockSpec(memory_space=pltpu.SMEM)
hbm = pl.BlockSpec(memory_space=pltpu.HBM)


def call(body, out, ins, operands, scratch=(), flops=0, name=None, grant=16 << 20):
    operands = [
        pltpu.with_memory_space_constraint(o, pltpu.HBM) if i is hbm else o
        for i, o in zip(ins, operands)
    ]
    size = sum(math.prod(o.shape) * o.dtype.itemsize for o in operands)
    outs = out if isinstance(out, (list, tuple)) else [out]
    size += sum(math.prod(o.shape) * jnp.dtype(o.dtype).itemsize for o in outs)
    return pl.pallas_call(
        body,
        out_shape=out,
        in_specs=ins,
        out_specs=[vmem] * len(outs) if outs is out else vmem,
        scratch_shapes=list(scratch),
        compiler_params=pltpu.CompilerParams(vmem_limit_bytes=grant),
        cost_estimate=pl.CostEstimate(flops=flops, bytes_accessed=size, transcendentals=0),
        name=name,
    )(*operands)


def f32(*shape):
    return jax.ShapeDtypeStruct(shape, jnp.float32)


def swapped(chunk, axis, number):
    devices = lax.axis_size(axis)
    return lax.ppermute(chunk, axis, [(i, i ^ number) for i in range(devices)])


def exchanged(chunks, axis, order):
    return [swapped(c, axis, n) if n else c for c, n in zip(chunks, order)]


def after(value, other):
    return lax.optimization_barrier((value, other))[0]


def spread(block, axis, first):
    blocks = {0: block}
    bit = lax.axis_size(axis) // 2
    while bit:
        for number in list(blocks):
            blocks[number ^ bit] = swapped(blocks[number], axis, bit)
        if first is not None:
            blocks[bit], first = lax.optimization_barrier((blocks[bit], first))
            ready, first = first, None
        bit //= 2
    return [blocks[number] for number in range(lax.axis_size(axis))], ready


def gathered_sums(blocks, axis):
    blocks = {number: [block] for number, block in enumerate(blocks)}
    bit = 1
    while bit < lax.axis_size(axis):
        for number in sorted(blocks, reverse=True):
            if number & bit:
                block = functools.reduce(jnp.add, blocks.pop(number))
                blocks[number ^ bit].append(swapped(block, axis, bit))
        bit *= 2
    return blocks[0]


def per_device(theta, phi, labels, ms_region, aex_region, kernel):
    count_x, count_y = lax.axis_size("gx"), lax.axis_size("gy")
    gx, gy = lax.axis_index("gx"), lax.axis_index("gy")
    depth, height, width = theta.shape
    rows = kernel.shape[2]
    lanes = 2 * rows
    lines = 3 * depth * height
    whole_y = count_y * height

    place = jnp.stack([gx, gy]).astype(jnp.int32)
    cells = f32(3, depth, height, width)
    order_x, order_y = list(range(count_x)), list(range(count_y - 1, -1, -1))
    table = line_table(count_x, count_y, width, rows)
    if table is None:
        table = line_table_here(count_x, width, rows, order_y)
        columns_tables = column_tables_here(count_y, height, order_y)
    else:
        columns_tables = column_tables(count_y, height, order_y)
    sources = [jnp.asarray(t) for t in (table, *columns_tables)]
    twice = np.concatenate([np.eye(rows), np.eye(rows)], 1).astype(ml_dtypes.bfloat16)
    transform_flops = 6 * lines * count_x * width * count_y * lanes

    packed = call(
        pack_kernel,
        cells,
        [hbm] * 3,
        (theta, phi, labels),
        scratch=(
            pltpu.VMEM((2, depth, height, width), jnp.float32),
            pltpu.VMEM((depth, height, width), jnp.int32),
            pltpu.SemaphoreType.DMA((3,)),
        ),
        name="pack",
    )
    table, forward, inverse = call(
        functools.partial(load_kernel, order_x, order_y),
        [
            pltpu.VMEM((2, count_x, width, count_y * lanes), jnp.bfloat16),
            pltpu.VMEM(sources[1].shape[1:], jnp.bfloat16),
            pltpu.VMEM(sources[2].shape[1:], jnp.bfloat16),
        ],
        [smem] + [hbm] * 3,
        (place, *sources),
        scratch=(pltpu.SemaphoreType.DMA((2 + count_x * count_y,)),),
        name="load",
    )

    gathered, table = spread(packed, "gx", table)
    tensor = call(
        tensor_kernel,
        jax.ShapeDtypeStruct((48, 2 * whole_y, lanes), jnp.bfloat16),
        [vmem, vmem],
        (kernel.reshape(48, rows, 2 * whole_y), jnp.asarray(twice)),
        flops=48 * 2 * rows * lanes * 2 * whole_y,
        name="tensor",
    )
    edge_rows = 3 * depth * width // lanes
    far = count_y // 2
    chunk_shapes = [f32(lines + (edge_rows if n in meeting(count_y) else 0), lanes) for n in order_y]
    *far_chunks, both = call(
        functools.partial(lines_kernel, count_x, order_y, far),
        chunk_shapes[:far] + [jax.ShapeDtypeStruct((count_x, 2 * lines, width), jnp.bfloat16)],
        [vmem] * count_x + [hbm, smem, vmem],
        (*gathered, ms_region, place, table),
        scratch=(pltpu.SMEM(ms_region.shape, jnp.float32), pltpu.SemaphoreType.DMA),
        flops=transform_flops // 2,
        name="far_lines",
    )
    far_columns = exchanged(far_chunks, "gy", order_y[:far])
    both = after(both, far_columns[0])
    near_chunks = call(
        functools.partial(near_lines_kernel, order_y, far),
        chunk_shapes[far:],
        [vmem, vmem, smem, vmem],
        (both, gathered[0], place, table),
        flops=transform_flops // 2,
        name="near_lines",
    )
    columns = [*far_columns, *exchanged(near_chunks, "gy", order_y[far:])]
    columns = lax.optimization_barrier(columns)
    scale = -1.0 / (2 * depth * 2 * whole_y * 2 * count_x * width)
    waves = call(
        functools.partial(waves_kernel, scale, count_y),
        [f32(lines, lanes)] * count_y,
        [vmem] * (count_y + 3),
        (*columns, tensor, forward, inverse),
        scratch=(
            pltpu.VMEM((2 * whole_y, 3 * depth * lanes), jnp.float32),
            pltpu.VMEM((6 * whole_y, 3 * depth * lanes), jnp.bfloat16),
        ),
        flops=20 * whole_y * whole_y * 3 * depth * lanes,
        name="waves",
    )
    returned = exchanged(waves, "gy", order_y)
    across = [number for number in range(count_x) if number % 2]
    within = [number for number in range(count_x) if not number % 2]
    partial = [None] * count_x
    for numbers, name in ((across, "back_across"), (within, "back_within")):
        blocks = call(
            functools.partial(back_lines_kernel, numbers, count_y),
            [f32(lines, width)] * len(numbers),
            [vmem] * (count_y + 1),
            (*returned, table),
            flops=transform_flops // 2,
            name=name,
        )
        for number, block in zip(numbers, blocks):
            partial[number] = block
    edges = [columns[order_y.index(number)] for number in meeting(count_y)]
    edges, partial[0] = lax.optimization_barrier((edges, partial[0]))
    exchange, unit = call(
        functools.partial(exchange_kernel, order_x, count_y),
        [cells, cells],
        [vmem] * (count_x + len(edges)) + [smem] * 3,
        (*gathered, *edges, place, ms_region, aex_region),
        scratch=(pltpu.VMEM((count_x, 3, depth, height, width), jnp.float32),),
        flops=300 * depth * height * width,
        name="exchange",
    )
    parts = gathered_sums(partial, "gx")
    field, predicted = call(
        functools.partial(final_kernel, len(parts)),
        [cells, cells],
        [vmem] * (len(parts) + 2),
        (*parts, exchange, unit),
        flops=60 * depth * height * width,
        name="predict",
    )
    return field, predicted


def solution(mesh):
    in_specs = (
        P(None, "gy", "gx"),
        P(None, "gy", "gx"),
        P(None, "gy", "gx"),
        P(),
        P(),
        P(None, None, ("gx", "gy"), None),
    )
    out_specs = (P(None, None, "gy", "gx"), P(None, None, "gy", "gx"))
    return jax.shard_map(
        per_device, mesh=mesh, in_specs=in_specs, out_specs=out_specs, check_vma=False
    )
```

```python
import functools
import math

import jax
import jax.numpy as jnp
import ml_dtypes
import numpy as np
from jax import lax
from jax.experimental import pallas as pl
from jax.experimental.pallas import tpu as pltpu
from jax.sharding import PartitionSpec as P

damping = 0.5
time_step = 0.2
side_weight = 0.25
layer_weight = 0.5
root_half = math.sqrt(0.5)
constant_limit = 20 << 20


def split_high(value):
    high = value.astype(jnp.bfloat16)
    low = (value - high.astype(jnp.float32)).astype(jnp.bfloat16)
    return high, low


def split_table(table):
    high = table.astype(np.float32).astype(ml_dtypes.bfloat16)
    low = (table - high.astype(np.float64)).astype(np.float32).astype(ml_dtypes.bfloat16)
    return high, low


def dot(left, right, contract=((1,), (0,))):
    return lax.dot_general(left, right, (contract, ((), ())), preferred_element_type=jnp.float32)


def line_table(count_x, count_y, width, rows):
    cells = count_x * width
    if count_x * 2 * cells * count_y * 2 * rows * 2 > constant_limit:
        return None
    place = np.arange(cells)[None, None, :, None]
    wave = (
        np.arange(count_x)[:, None, None, None] * (count_y * rows)
        + np.arange(count_y)[None, :, None, None] * rows
        + np.arange(rows)[None, None, None, :]
    )
    angle = (place * wave % (2 * cells)) * (2.0 * math.pi / (2 * cells))
    table = np.concatenate([np.cos(angle), -np.sin(angle)], 3)
    table = table.reshape(count_x, count_y, count_x, width, 2 * rows)
    high, low = split_table(table)
    return np.stack([high, low], 2)


def line_table_here(count_x, width, rows, order):
    cells = count_x * width
    count_y = len(order)
    place = jnp.arange(cells, dtype=jnp.int32)[:, None, None]
    block = lax.bitwise_xor(lax.axis_index("gy"), jnp.array(order, jnp.int32))
    wave = (
        lax.axis_index("gx") * (count_y * rows)
        + block[None, :, None] * rows
        + jnp.arange(rows, dtype=jnp.int32)[None, None, :]
    )
    angle = (place * wave % (2 * cells)).astype(jnp.float32) * (math.pi / cells)
    table = jnp.concatenate([jnp.cos(angle), -jnp.sin(angle)], 2)
    table = table.reshape(1, 1, count_x, width, count_y * 2 * rows)
    return jnp.stack(split_high(table), 2)


def column_tables(count_y, local, order):
    height = count_y * local
    wave = np.arange(2 * height)
    block = np.arange(count_y)[:, None] ^ np.array(order)[None, :]
    place = (block[:, :, None] * local + np.arange(local)).reshape(count_y, height)
    angle = (wave[None, :, None] * place[:, None, :] % (2 * height)) * (math.pi / height)
    high, low = split_table(np.concatenate([np.cos(angle), np.sin(angle)], 2))
    forward = np.concatenate([high, high, low], 2)
    angle = angle.transpose(0, 2, 1)
    high, low = split_table(np.concatenate([np.cos(angle), np.sin(angle)], 1))
    inverse = np.concatenate([high, high, low], 2)
    return forward, inverse


def column_tables_here(count_y, local, order):
    height = count_y * local
    wave = jnp.arange(2 * height, dtype=jnp.int32)
    block = lax.bitwise_xor(lax.axis_index("gy"), jnp.array(order, jnp.int32))
    place = (block[:, None] * local + jnp.arange(local, dtype=jnp.int32)).reshape(height)
    angle = (wave[:, None] * place % (2 * height)).astype(jnp.float32) * (math.pi / height)
    high, low = split_high(jnp.concatenate([jnp.cos(angle), jnp.sin(angle)], 1))
    forward = jnp.concatenate([high, high, low], 1)
    high, low = split_high(jnp.concatenate([jnp.cos(angle.T), jnp.sin(angle.T)], 0))
    inverse = jnp.concatenate([high, high, low], 1)
    return forward[None], inverse[None]


def load_kernel(order_x, order_y, place, *refs):
    table_ref, forward_ref, inverse_ref, table, forward, inverse, sem = refs
    gx, gy = place[0], place[1]
    mine_x = gx if table_ref.shape[0] > 1 else 0
    mine_y = gy if forward_ref.shape[0] > 1 else 0
    lanes = table_ref.shape[5]
    copies = [
        pltpu.make_async_copy(forward_ref.at[mine_y], forward, sem.at[0]),
        pltpu.make_async_copy(inverse_ref.at[mine_y], inverse, sem.at[1]),
    ]
    for spot_x, number_x in enumerate(order_x):
        block_x = lax.bitwise_xor(gx, number_x)
        for spot_y in range(table_ref.shape[1]):
            block_y = lax.bitwise_xor(gy, order_y[spot_y]) if table_ref.shape[1] > 1 else 0
            columns = slice(spot_y * lanes, (spot_y + 1) * lanes)
            copies.append(
                pltpu.make_async_copy(
                    table_ref.at[mine_x, block_y, :, block_x],
                    table.at[:, spot_x, :, columns],
                    sem.at[len(copies)],
                )
            )
    for copy in copies:
        copy.start()
    for copy in copies:
        copy.wait()


def sine_cosine(angle):
    turns = jnp.floor(angle * (2.0 / math.pi) + 0.5)
    rest = angle - turns * 1.5703125
    rest = rest - turns * 4.8351287841796875e-4
    rest = rest - turns * 3.1385570764541626e-7
    square = rest * rest
    sine = rest + rest * square * (
        -1.6666654611e-1 + square * (8.3321608736e-3 - square * 1.9515295891e-4)
    )
    cosine = (
        1.0
        - 0.5 * square
        + square * square * (4.166664568298827e-2 + square * (-1.388731625493765e-3 + square * 2.443315711809948e-5))
    )
    quarter = turns.astype(jnp.int32)
    odd = (quarter & 1) == 1
    out_sine = jnp.where(odd, cosine, sine)
    out_cosine = jnp.where(odd, sine, cosine)
    out_sine = jnp.where((quarter & 2) == 2, -out_sine, out_sine)
    out_cosine = jnp.where(((quarter + 1) & 2) == 2, -out_cosine, out_cosine)
    return out_sine, out_cosine


def directions(theta, phi):
    lateral, axial = sine_cosine(theta)
    sine, cosine = sine_cosine(phi)
    return [lateral * cosine, lateral * sine, axial]


def looked_up(labels, region):
    result = jnp.zeros_like(labels) + region[0]
    for index in range(1, region.shape[0]):
        result = jnp.where(labels == float(index), region[index], result)
    return result


def pack_kernel(theta_ref, phi_ref, labels_ref, raw_ref, first_ref, last_ref, angle, label, sems):
    height = theta_ref.shape[1]
    copies = [
        pltpu.make_async_copy(theta_ref, angle.at[0], sems.at[0]),
        pltpu.make_async_copy(phi_ref, angle.at[1], sems.at[1]),
        pltpu.make_async_copy(labels_ref, label, sems.at[2]),
    ]
    for copy in copies:
        copy.start()
    for copy in copies:
        copy.wait()
    for index, value in enumerate((angle[0], angle[1], label[...].astype(jnp.float32))):
        raw_ref[index] = value
        first_ref[index] = value[:, 0]
        last_ref[index] = value[:, height - 1]


def lines_kernel(count_x, *refs):
    raw_refs, (region_ref, table) = refs[:count_x], refs[count_x : count_x + 2]
    out_refs, (region, sem) = refs[count_x + 2 : -2], refs[-2:]
    fetch = pltpu.make_async_copy(region_ref, region, sem)
    fetch.start()
    units = [directions(raw_ref[0], raw_ref[1]) for raw_ref in raw_refs]
    fetch.wait()
    total = None
    for number in range(count_x):
        saturation = looked_up(raw_refs[number][2], region)
        rows = saturation.shape[0] * saturation.shape[1]
        block = [(part * saturation).reshape(rows, -1) for part in units[number]]
        high, low = split_high(jnp.concatenate(block, 0))
        both = dot(jnp.concatenate([high, low], 0), table[0, number])
        part = both[: 3 * rows] + both[3 * rows :] + dot(high, table[1, number])
        total = part if total is None else total + part
    lanes = out_refs[0].shape[1]
    for spot, out_ref in enumerate(out_refs):
        out_ref[...] = total[:, spot * lanes : (spot + 1) * lanes]


def back_lines_kernel(numbers, count_y, *refs):
    in_refs, table, out_refs = refs[:count_y], refs[count_y], refs[count_y + 1 :]
    high, low = split_high(jnp.concatenate([ref[...] for ref in in_refs], 1))
    both = jnp.concatenate([high, low], 0)
    lines = high.shape[0]
    for number, out_ref in zip(numbers, out_refs):
        wide = dot(both, table[0, number], ((1,), (1,)))
        out_ref[...] = wide[:lines] + wide[lines:] + dot(high, table[1, number], ((1,), (1,)))


def tensor_kernel(kernel_ref, twice_ref, out_ref):
    twice = twice_ref[...]

    unroll = 8

    def step(index, carry):
        for offset in range(unroll):
            turned = dot(kernel_ref[index * unroll + offset], twice, ((0,), (0,)))
            out_ref[index * unroll + offset] = turned.astype(jnp.bfloat16)
        return carry

    lax.fori_loop(0, kernel_ref.shape[0] // unroll, step, 0)


def turn(value, sign):
    lanes = value.shape[-1]
    if lanes == 128:
        return pltpu.roll(value, lanes // 2, value.ndim - 1) * sign
    return jnp.concatenate([value[..., lanes // 2 :], value[..., : lanes // 2]], -1) * sign


def layers_forward(layer, sign):
    d0, d1, d2, d3 = layer
    r2 = turn(d2, sign)
    near, far = d1 + d3, d1 - d3
    far_turned = turn(far, sign)
    near_turned = turn(near, sign)
    even, odd = d0 + d2, d0 - d2
    out = [None] * 8
    out[0], out[4] = even + near, even - near
    out[2], out[6] = odd + far_turned, odd - far_turned
    plus, minus = d0 + r2, d0 - r2
    first = (far + near_turned) * root_half
    second = (near_turned - far) * root_half
    out[1], out[5] = plus + first, plus - first
    out[3], out[7] = minus + second, minus - second
    return out


def layers_inverse(wave, sign):
    a, b = wave[0] + wave[4], wave[0] - wave[4]
    e, f = wave[2] + wave[6], turn(wave[2] - wave[6], sign)
    p, q = wave[1] + wave[5], wave[1] - wave[5]
    s, t = wave[3] + wave[7], turn(wave[3] - wave[7], sign)
    o0, o1, o2, o3 = p + s, q - t, p - s, q + t
    return [
        a + e + o0,
        b - f + (o1 - turn(o1, sign)) * root_half,
        a - e - turn(o2, sign),
        b + f - (o3 + turn(o3, sign)) * root_half,
    ]


def apply_tensor(tensor, wave):
    out = [[], [], []]
    for level in range(8):
        xx, yy, zz, xy, xz, yz = [tensor[part][level] for part in range(6)]
        x, y, z = wave[0][level], wave[1][level], wave[2][level]
        out[0].append(xx * x + xy * y + xz * z)
        out[1].append(xy * x + yy * y + yz * z)
        out[2].append(xz * x + yz * y + zz * z)
    return out


def waves_kernel(scale, count_y, *refs):
    spec_refs, (tensor_ref, forward_ref, inverse_ref) = refs[:count_y], refs[count_y : count_y + 3]
    out_refs, (wave_ref, back_ref) = refs[count_y + 3 : -2], refs[-2:]
    lines, lanes = out_refs[0].shape
    local = 8
    planes = lines // local
    height = count_y * local
    sign = jnp.where(
        lax.broadcasted_iota(jnp.int32, (1, lanes), 1) < lanes // 2, 1.0, -1.0
    ).astype(jnp.float32)
    columns = []
    for plane in range(planes):
        value = jnp.concatenate(
            [spec_ref[plane * local : (plane + 1) * local] for spec_ref in spec_refs], 0
        )
        value = jnp.concatenate([value, turn(value, sign)], 0)
        high, low = split_high(value)
        columns.append(jnp.concatenate([high, low, high], 0))
    wave_ref[...] = dot(forward_ref[...], jnp.concatenate(columns, 1))

    chunk = 16
    depth = planes // 3
    double = 2 * height

    def step(index, carry):
        rows = pl.ds(pl.multiple_of(index * chunk, chunk), chunk)
        wave = []
        for part in range(3):
            layer = [
                wave_ref[rows, (part * depth + z) * lanes : (part * depth + z + 1) * lanes]
                for z in range(depth)
            ]
            wave.append(layers_forward(layer, sign))
        tensor = [
            [tensor_ref[part * 8 + level, rows, :].astype(jnp.float32) for level in range(8)]
            for part in range(6)
        ]
        image = apply_tensor(tensor, wave)
        for part in range(3):
            layer = layers_inverse(image[part], sign)
            for z in range(depth):
                spot = slice((part * depth + z) * lanes, (part * depth + z + 1) * lanes)
                high, low = split_high(layer[z] * scale)
                back_ref[rows, spot] = high
                back_ref[pl.ds(pl.multiple_of(double + index * chunk, chunk), chunk), spot] = low
                back_ref[pl.ds(pl.multiple_of(2 * double + index * chunk, chunk), chunk), spot] = high
        return carry

    lax.fori_loop(0, double // chunk, step, 0)
    back = dot(inverse_ref[...], back_ref[...])
    for plane in range(planes):
        part = slice(plane * lanes, (plane + 1) * lanes)
        value = back[:height, part] - turn(back[height:, part], sign)
        for number in range(count_y):
            out_refs[number][plane * local : (plane + 1) * local] = value[
                number * local : (number + 1) * local
            ]


def exchange_kernel(order_x, count_y, *refs):
    count_x = len(order_x)
    raw_refs, (before_ref, after_ref, place, ms_ref, aex_ref) = refs[:count_x], refs[count_x:-3]
    exchange_ref, unit_ref, raw_ref = refs[-3:]
    depth, height, width = raw_ref.shape[2:]
    gx, gy = place[0], place[1]

    for spot, number in enumerate(order_x):
        raw_ref[lax.bitwise_xor(gx, number)] = raw_refs[spot][...]
    left, right = jnp.maximum(gx - 1, 0), jnp.minimum(gx + 1, count_x - 1)
    shape = (depth, height, width)
    lane = lax.broadcasted_iota(jnp.int32, shape, 2)
    row = lax.broadcasted_iota(jnp.int32, shape, 1)

    def quantities(values):
        return directions(values[0], values[1]) + [looked_up(values[2], aex_ref)]

    raw = [raw_refs[0][f] for f in range(3)]
    here = quantities(raw)
    side = quantities([jnp.where(lane == 0, raw_ref[right, f], raw_ref[left, f]) for f in range(3)])
    above = quantities(
        [jnp.where(row == 0, after_ref[f][:, None, :], before_ref[f][:, None, :]) for f in range(3)]
    )
    saturation = looked_up(raw[2], ms_ref)
    total = [jnp.zeros(shape, jnp.float32) for _ in range(3)]

    def add(total, beside, weight):
        coupling = 2.0 * here[3] * beside[3] / (here[3] + beside[3]) * weight
        return [total[c] + coupling * (beside[c] - here[c]) for c in range(3)]

    one = jnp.float32(1.0)
    zero = jnp.float32(0.0)
    for shift, edge, there in ((1, 0, gx > 0), (width - 1, width - 1, gx < count_x - 1)):
        beside = [
            jnp.where(lane == edge, pltpu.roll(s, shift, 2), pltpu.roll(h, shift, 2))
            for s, h in zip(side, here)
        ]
        weight = jnp.where(lane == edge, jnp.where(there, one, zero), one) * side_weight
        total = add(total, beside, weight)
    for shift, edge, there in ((1, 0, gy > 0), (height - 1, height - 1, gy < count_y - 1)):
        beside = [
            jnp.where(row == edge, pltpu.roll(s, shift, 1), pltpu.roll(h, shift, 1))
            for s, h in zip(above, here)
        ]
        weight = jnp.where(row == edge, jnp.where(there, one, zero), one) * side_weight
        total = add(total, beside, weight)
    for part in range(3):
        unit_ref[part] = here[part]
    for z in range(depth):
        out = [total[c][z] for c in range(3)]
        for other in (z - 1, z + 1):
            if 0 <= other < depth:
                a, b = here[3][z], here[3][other]
                coupling = 2.0 * a * b / (a + b) * layer_weight
                out = [out[c] + coupling * (here[c][other] - here[c][z]) for c in range(3)]
        for c in range(3):
            exchange_ref[c, z] = out[c] / saturation[z]


def cross(first, second):
    return [
        first[1] * second[2] - first[2] * second[1],
        first[2] * second[0] - first[0] * second[2],
        first[0] * second[1] - first[1] * second[0],
    ]


def final_kernel(count_x, *refs):
    part_refs, (exchange_ref, unit_ref, field_ref, predicted_ref) = refs[:count_x], refs[count_x:]
    depth, height, width = unit_ref.shape[1:]
    rows = depth * height
    unit, field = [], []
    for c in range(3):
        place = slice(c * rows, (c + 1) * rows)
        total = part_refs[0][place]
        for part_ref in part_refs[1:]:
            total = total + part_ref[place]
        field.append(exchange_ref[c] + total.reshape(depth, height, width))
        unit.append(unit_ref[c])
        field_ref[c] = field[c]
    twist = cross(unit, field)
    second = cross(unit, twist)
    moved = [
        unit[c] - (time_step / (1.0 + damping * damping)) * (twist[c] + damping * second[c])
        for c in range(3)
    ]
    length = jnp.sqrt(moved[0] * moved[0] + moved[1] * moved[1] + moved[2] * moved[2])
    for c in range(3):
        predicted_ref[c] = moved[c] / length


vmem = pl.BlockSpec(memory_space=pltpu.VMEM)
smem = pl.BlockSpec(memory_space=pltpu.SMEM)
hbm = pl.BlockSpec(memory_space=pltpu.HBM)


def call(body, out, ins, operands, scratch=(), flops=0, name=None, grant=16 << 20):
    operands = [
        pltpu.with_memory_space_constraint(o, pltpu.HBM) if i is hbm else o
        for i, o in zip(ins, operands)
    ]
    size = sum(math.prod(o.shape) * o.dtype.itemsize for o in operands)
    outs = out if isinstance(out, (list, tuple)) else [out]
    size += sum(math.prod(o.shape) * jnp.dtype(o.dtype).itemsize for o in outs)
    return pl.pallas_call(
        body,
        out_shape=out,
        in_specs=ins,
        out_specs=[vmem] * len(outs) if outs is out else vmem,
        scratch_shapes=list(scratch),
        compiler_params=pltpu.CompilerParams(vmem_limit_bytes=grant),
        cost_estimate=pl.CostEstimate(flops=flops, bytes_accessed=size, transcendentals=0),
        name=name,
    )(*operands)


def f32(*shape):
    return jax.ShapeDtypeStruct(shape, jnp.float32)


def swapped(chunk, axis, number):
    devices = lax.axis_size(axis)
    return lax.ppermute(chunk, axis, [(i, i ^ number) for i in range(devices)])


def exchanged(chunks, axis, order):
    return [swapped(c, axis, n) if n else c for c, n in zip(chunks, order)]


def after(value, other):
    return lax.optimization_barrier((value, other))[0]


def spread(block, axis, first):
    blocks = {0: block}
    bit = lax.axis_size(axis) // 2
    while bit:
        for number in list(blocks):
            blocks[number ^ bit] = swapped(blocks[number], axis, bit)
        if first is not None:
            blocks[bit], first = lax.optimization_barrier((blocks[bit], first))
            ready, first = first, None
        bit //= 2
    return [blocks[number] for number in range(lax.axis_size(axis))], ready


def gathered_sums(blocks, axis):
    blocks = {number: [block] for number, block in enumerate(blocks)}
    bit = 1
    while bit < lax.axis_size(axis):
        for number in sorted(blocks, reverse=True):
            if number & bit:
                block = functools.reduce(jnp.add, blocks.pop(number))
                blocks[number ^ bit].append(swapped(block, axis, bit))
        bit *= 2
    return blocks[0], block


def per_device(theta, phi, labels, ms_region, aex_region, kernel):
    count_x, count_y = lax.axis_size("gx"), lax.axis_size("gy")
    gx, gy = lax.axis_index("gx"), lax.axis_index("gy")
    depth, height, width = theta.shape
    rows = kernel.shape[2]
    lanes = 2 * rows
    lines = 3 * depth * height
    whole_y = count_y * height

    place = jnp.stack([gx, gy]).astype(jnp.int32)
    cells = f32(3, depth, height, width)
    order_x, order_y = list(range(count_x)), list(range(count_y - 1, -1, -1))
    table = line_table(count_x, count_y, width, rows)
    if table is None:
        table = line_table_here(count_x, width, rows, order_y)
        columns_tables = column_tables_here(count_y, height, order_y)
    else:
        columns_tables = column_tables(count_y, height, order_y)
    sources = [jnp.asarray(t) for t in (table, *columns_tables)]
    twice = np.concatenate([np.eye(rows), np.eye(rows)], 1).astype(ml_dtypes.bfloat16)
    transform_flops = 6 * lines * count_x * width * count_y * lanes

    edge = f32(3, depth, width)
    packed, first, last = call(
        pack_kernel,
        [cells, edge, edge],
        [hbm] * 3,
        (theta, phi, labels),
        scratch=(
            pltpu.VMEM((2, depth, height, width), jnp.float32),
            pltpu.VMEM((depth, height, width), jnp.int32),
            pltpu.SemaphoreType.DMA((3,)),
        ),
        name="pack",
    )
    table, forward, inverse = call(
        functools.partial(load_kernel, order_x, order_y),
        [
            pltpu.VMEM((2, count_x, width, count_y * lanes), jnp.bfloat16),
            pltpu.VMEM(sources[1].shape[1:], jnp.bfloat16),
            pltpu.VMEM(sources[2].shape[1:], jnp.bfloat16),
        ],
        [smem] + [hbm] * 3,
        (place, *sources),
        scratch=(pltpu.SemaphoreType.DMA((2 + count_x * count_y,)),),
        name="load",
    )

    gathered, table = spread(packed, "gx", table)
    tensor = call(
        tensor_kernel,
        jax.ShapeDtypeStruct((48, 2 * whole_y, lanes), jnp.bfloat16),
        [vmem, vmem],
        (kernel.reshape(48, rows, 2 * whole_y), jnp.asarray(twice)),
        flops=48 * 2 * rows * lanes * 2 * whole_y,
        name="tensor",
    )
    gathered, tensor = lax.optimization_barrier((gathered, tensor))
    spectrum = call(
        functools.partial(lines_kernel, count_x),
        [f32(lines, lanes)] * count_y,
        [vmem] * count_x + [hbm, vmem],
        (*gathered, ms_region, table),
        scratch=(pltpu.SMEM(ms_region.shape, jnp.float32), pltpu.SemaphoreType.DMA),
        flops=transform_flops,
        name="lines",
    )
    columns = exchanged(spectrum, "gy", order_y)
    scale = -1.0 / (2 * depth * 2 * whole_y * 2 * count_x * width)
    waves = call(
        functools.partial(waves_kernel, scale, count_y),
        [f32(lines, lanes)] * count_y,
        [vmem] * (count_y + 3),
        (*columns, tensor, forward, inverse),
        scratch=(
            pltpu.VMEM((2 * whole_y, 3 * depth * lanes), jnp.float32),
            pltpu.VMEM((6 * whole_y, 3 * depth * lanes), jnp.bfloat16),
        ),
        flops=20 * whole_y * whole_y * 3 * depth * lanes,
        name="waves",
    )
    returned = exchanged(waves, "gy", order_y)
    across = [number for number in range(count_x) if number % 2]
    within = [number for number in range(count_x) if not number % 2]
    partial = [None] * count_x
    for numbers, name in ((across, "back_across"), (within, "back_within")):
        blocks = call(
            functools.partial(back_lines_kernel, numbers, count_y),
            [f32(lines, width)] * len(numbers),
            [vmem] * (count_y + 1),
            (*returned, table),
            flops=transform_flops // 2,
            name=name,
        )
        for number, block in zip(numbers, blocks):
            partial[number] = block
    parts, far_sum = gathered_sums(partial, "gx")
    first, last = after((first, last), far_sum)
    up = [(i, i + 1) for i in range(count_y - 1)]
    row_before = lax.ppermute(last, "gy", up)
    row_after = lax.ppermute(first, "gy", [(j, i) for i, j in up])
    exchange, unit = call(
        functools.partial(exchange_kernel, order_x, count_y),
        [cells, cells],
        [vmem] * (count_x + 2) + [smem] * 3,
        (*gathered, row_before, row_after, place, ms_region, aex_region),
        scratch=(pltpu.VMEM((count_x, 3, depth, height, width), jnp.float32),),
        flops=300 * depth * height * width,
        name="exchange",
    )
    field, predicted = call(
        functools.partial(final_kernel, len(parts)),
        [cells, cells],
        [vmem] * (len(parts) + 2),
        (*parts, exchange, unit),
        flops=60 * depth * height * width,
        name="predict",
    )
    return field, predicted


def solution(mesh):
    in_specs = (
        P(None, "gy", "gx"),
        P(None, "gy", "gx"),
        P(None, "gy", "gx"),
        P(),
        P(),
        P(None, None, ("gx", "gy"), None),
    )
    out_specs = (P(None, None, "gy", "gx"), P(None, None, "gy", "gx"))
    return jax.shard_map(
        per_device, mesh=mesh, in_specs=in_specs, out_specs=out_specs, check_vma=False
    )
```

```python
import functools
import math

import jax
import jax.numpy as jnp
import ml_dtypes
import numpy as np
from jax import lax
from jax.experimental import pallas as pl
from jax.experimental.pallas import tpu as pltpu
from jax.sharding import PartitionSpec as P

damping = 0.5
time_step = 0.2
side_weight = 0.25
layer_weight = 0.5
root_half = math.sqrt(0.5)
constant_limit = 20 << 20


def split_high(value):
    high = value.astype(jnp.bfloat16)
    low = (value - high.astype(jnp.float32)).astype(jnp.bfloat16)
    return high, low


def split_table(table):
    high = table.astype(np.float32).astype(ml_dtypes.bfloat16)
    low = (table - high.astype(np.float64)).astype(np.float32).astype(ml_dtypes.bfloat16)
    return high, low


def dot(left, right, contract=((1,), (0,))):
    return lax.dot_general(left, right, (contract, ((), ())), preferred_element_type=jnp.float32)


def line_table(count_x, count_y, width, rows):
    cells = count_x * width
    if count_x * 2 * cells * count_y * 2 * rows * 2 > constant_limit:
        return None
    place = np.arange(cells)[None, None, :, None]
    wave = (
        np.arange(count_x)[:, None, None, None] * (count_y * rows)
        + np.arange(count_y)[None, :, None, None] * rows
        + np.arange(rows)[None, None, None, :]
    )
    angle = (place * wave % (2 * cells)) * (2.0 * math.pi / (2 * cells))
    table = np.concatenate([np.cos(angle), -np.sin(angle)], 3)
    table = table.reshape(count_x, count_y, count_x, width, 2 * rows)
    high, low = split_table(table)
    return np.stack([high, low], 2)


def line_table_here(count_x, width, rows, order):
    cells = count_x * width
    count_y = len(order)
    place = jnp.arange(cells, dtype=jnp.int32)[:, None, None]
    block = lax.bitwise_xor(lax.axis_index("gy"), jnp.array(order, jnp.int32))
    wave = (
        lax.axis_index("gx") * (count_y * rows)
        + block[None, :, None] * rows
        + jnp.arange(rows, dtype=jnp.int32)[None, None, :]
    )
    angle = (place * wave % (2 * cells)).astype(jnp.float32) * (math.pi / cells)
    table = jnp.concatenate([jnp.cos(angle), -jnp.sin(angle)], 2)
    table = table.reshape(1, 1, count_x, width, count_y * 2 * rows)
    return jnp.stack(split_high(table), 2)


def column_tables(count_y, local, order):
    height = count_y * local
    wave = np.arange(2 * height)
    block = np.arange(count_y)[:, None] ^ np.array(order)[None, :]
    place = (block[:, :, None] * local + np.arange(local)).reshape(count_y, height)
    angle = (wave[None, :, None] * place[:, None, :] % (2 * height)) * (math.pi / height)
    high, low = split_table(np.concatenate([np.cos(angle), np.sin(angle)], 2))
    forward = np.concatenate([high, high, low], 2)
    angle = angle.transpose(0, 2, 1)
    high, low = split_table(np.concatenate([np.cos(angle), np.sin(angle)], 1))
    inverse = np.concatenate([high, high, low], 2)
    return forward, inverse


def column_tables_here(count_y, local, order):
    height = count_y * local
    wave = jnp.arange(2 * height, dtype=jnp.int32)
    block = lax.bitwise_xor(lax.axis_index("gy"), jnp.array(order, jnp.int32))
    place = (block[:, None] * local + jnp.arange(local, dtype=jnp.int32)).reshape(height)
    angle = (wave[:, None] * place % (2 * height)).astype(jnp.float32) * (math.pi / height)
    high, low = split_high(jnp.concatenate([jnp.cos(angle), jnp.sin(angle)], 1))
    forward = jnp.concatenate([high, high, low], 1)
    high, low = split_high(jnp.concatenate([jnp.cos(angle.T), jnp.sin(angle.T)], 0))
    inverse = jnp.concatenate([high, high, low], 1)
    return forward[None], inverse[None]


def load_kernel(order_x, order_y, place, *refs):
    table_ref, forward_ref, inverse_ref, table, forward, inverse, sem = refs
    gx, gy = place[0], place[1]
    mine_x = gx if table_ref.shape[0] > 1 else 0
    mine_y = gy if forward_ref.shape[0] > 1 else 0
    lanes = table_ref.shape[5]
    copies = [
        pltpu.make_async_copy(forward_ref.at[mine_y], forward, sem.at[0]),
        pltpu.make_async_copy(inverse_ref.at[mine_y], inverse, sem.at[1]),
    ]
    for spot_x, number_x in enumerate(order_x):
        block_x = lax.bitwise_xor(gx, number_x)
        for spot_y in range(table_ref.shape[1]):
            block_y = lax.bitwise_xor(gy, order_y[spot_y]) if table_ref.shape[1] > 1 else 0
            columns = slice(spot_y * lanes, (spot_y + 1) * lanes)
            copies.append(
                pltpu.make_async_copy(
                    table_ref.at[mine_x, block_y, :, block_x],
                    table.at[:, spot_x, :, columns],
                    sem.at[len(copies)],
                )
            )
    for copy in copies:
        copy.start()
    for copy in copies:
        copy.wait()


def sine_cosine(angle):
    turns = jnp.floor(angle * (2.0 / math.pi) + 0.5)
    rest = angle - turns * 1.5703125
    rest = rest - turns * 4.8351287841796875e-4
    rest = rest - turns * 3.1385570764541626e-7
    square = rest * rest
    sine = rest + rest * square * (
        -1.6666654611e-1 + square * (8.3321608736e-3 - square * 1.9515295891e-4)
    )
    cosine = (
        1.0
        - 0.5 * square
        + square * square * (4.166664568298827e-2 + square * (-1.388731625493765e-3 + square * 2.443315711809948e-5))
    )
    quarter = turns.astype(jnp.int32)
    odd = (quarter & 1) == 1
    out_sine = jnp.where(odd, cosine, sine)
    out_cosine = jnp.where(odd, sine, cosine)
    out_sine = jnp.where((quarter & 2) == 2, -out_sine, out_sine)
    out_cosine = jnp.where(((quarter + 1) & 2) == 2, -out_cosine, out_cosine)
    return out_sine, out_cosine


def directions(theta, phi):
    lateral, axial = sine_cosine(theta)
    sine, cosine = sine_cosine(phi)
    return [lateral * cosine, lateral * sine, axial]


def looked_up(labels, region):
    result = jnp.zeros_like(labels) + region[0]
    for index in range(1, region.shape[0]):
        result = jnp.where(labels == float(index), region[index], result)
    return result


def pack_kernel(theta_ref, phi_ref, labels_ref, raw_ref, first_ref, last_ref, angle, label, sems):
    height = theta_ref.shape[1]
    copies = [
        pltpu.make_async_copy(theta_ref, angle.at[0], sems.at[0]),
        pltpu.make_async_copy(phi_ref, angle.at[1], sems.at[1]),
        pltpu.make_async_copy(labels_ref, label, sems.at[2]),
    ]
    for copy in copies:
        copy.start()
    for copy in copies:
        copy.wait()
    for index, value in enumerate((angle[0], angle[1], label[...].astype(jnp.float32))):
        raw_ref[index] = value
        first_ref[index] = value[:, 0]
        last_ref[index] = value[:, height - 1]


def lines_kernel(count_x, *refs):
    raw_refs, (region_ref, table) = refs[:count_x], refs[count_x : count_x + 2]
    out_refs, (region, sem) = refs[count_x + 2 : -2], refs[-2:]
    fetch = pltpu.make_async_copy(region_ref, region, sem)
    fetch.start()
    units = [directions(raw_ref[0], raw_ref[1]) for raw_ref in raw_refs]
    fetch.wait()
    total = None
    for number in range(count_x):
        saturation = looked_up(raw_refs[number][2], region)
        rows = saturation.shape[0] * saturation.shape[1]
        block = [(part * saturation).reshape(rows, -1) for part in units[number]]
        high, low = split_high(jnp.concatenate(block, 0))
        both = dot(jnp.concatenate([high, low], 0), table[0, number])
        part = both[: 3 * rows] + both[3 * rows :] + dot(high, table[1, number])
        total = part if total is None else total + part
    lanes = out_refs[0].shape[1]
    for spot, out_ref in enumerate(out_refs):
        out_ref[...] = total[:, spot * lanes : (spot + 1) * lanes]


def back_lines_kernel(numbers, count_y, *refs):
    in_refs, table, out_refs = refs[:count_y], refs[count_y], refs[count_y + 1 :]
    high, low = split_high(jnp.concatenate([ref[...] for ref in in_refs], 1))
    both = jnp.concatenate([high, low], 0)
    lines = high.shape[0]
    for number, out_ref in zip(numbers, out_refs):
        wide = dot(both, table[0, number], ((1,), (1,)))
        out_ref[...] = wide[:lines] + wide[lines:] + dot(high, table[1, number], ((1,), (1,)))


def tensor_kernel(kernel_ref, twice_ref, out_ref):
    twice = twice_ref[...]

    unroll = 8

    def step(index, carry):
        for offset in range(unroll):
            turned = dot(kernel_ref[index * unroll + offset], twice, ((0,), (0,)))
            out_ref[index * unroll + offset] = turned.astype(jnp.bfloat16)
        return carry

    lax.fori_loop(0, kernel_ref.shape[0] // unroll, step, 0)


def turn(value, sign):
    lanes = value.shape[-1]
    if lanes == 128:
        return pltpu.roll(value, lanes // 2, value.ndim - 1) * sign
    return jnp.concatenate([value[..., lanes // 2 :], value[..., : lanes // 2]], -1) * sign


def layers_forward(layer, sign):
    d0, d1, d2, d3 = layer
    r2 = turn(d2, sign)
    near, far = d1 + d3, d1 - d3
    far_turned = turn(far, sign)
    near_turned = turn(near, sign)
    even, odd = d0 + d2, d0 - d2
    out = [None] * 8
    out[0], out[4] = even + near, even - near
    out[2], out[6] = odd + far_turned, odd - far_turned
    plus, minus = d0 + r2, d0 - r2
    first = (far + near_turned) * root_half
    second = (near_turned - far) * root_half
    out[1], out[5] = plus + first, plus - first
    out[3], out[7] = minus + second, minus - second
    return out


def layers_inverse(wave, sign):
    a, b = wave[0] + wave[4], wave[0] - wave[4]
    e, f = wave[2] + wave[6], turn(wave[2] - wave[6], sign)
    p, q = wave[1] + wave[5], wave[1] - wave[5]
    s, t = wave[3] + wave[7], turn(wave[3] - wave[7], sign)
    o0, o1, o2, o3 = p + s, q - t, p - s, q + t
    return [
        a + e + o0,
        b - f + (o1 - turn(o1, sign)) * root_half,
        a - e - turn(o2, sign),
        b + f - (o3 + turn(o3, sign)) * root_half,
    ]


def apply_tensor(tensor, wave):
    out = [[], [], []]
    for level in range(8):
        xx, yy, zz, xy, xz, yz = [tensor[part][level] for part in range(6)]
        x, y, z = wave[0][level], wave[1][level], wave[2][level]
        out[0].append(xx * x + xy * y + xz * z)
        out[1].append(xy * x + yy * y + yz * z)
        out[2].append(xz * x + yz * y + zz * z)
    return out


def waves_kernel(scale, count_y, *refs):
    spec_refs, (tensor_ref, forward_ref, inverse_ref) = refs[:count_y], refs[count_y : count_y + 3]
    out_refs, (wave_ref, back_ref) = refs[count_y + 3 : -2], refs[-2:]
    lines, lanes = out_refs[0].shape
    local = 8
    planes = lines // local
    height = count_y * local
    sign = jnp.where(
        lax.broadcasted_iota(jnp.int32, (1, lanes), 1) < lanes // 2, 1.0, -1.0
    ).astype(jnp.float32)
    columns = []
    for plane in range(planes):
        value = jnp.concatenate(
            [spec_ref[plane * local : (plane + 1) * local] for spec_ref in spec_refs], 0
        )
        value = jnp.concatenate([value, turn(value, sign)], 0)
        high, low = split_high(value)
        columns.append(jnp.concatenate([high, low, high], 0))
    wave_ref[...] = dot(forward_ref[...], jnp.concatenate(columns, 1))

    chunk = 16
    depth = planes // 3
    double = 2 * height

    def step(index, carry):
        rows = pl.ds(pl.multiple_of(index * chunk, chunk), chunk)
        wave = []
        for part in range(3):
            layer = [
                wave_ref[rows, (part * depth + z) * lanes : (part * depth + z + 1) * lanes]
                for z in range(depth)
            ]
            wave.append(layers_forward(layer, sign))
        tensor = [
            [tensor_ref[part * 8 + level, rows, :].astype(jnp.float32) for level in range(8)]
            for part in range(6)
        ]
        image = apply_tensor(tensor, wave)
        for part in range(3):
            layer = layers_inverse(image[part], sign)
            for z in range(depth):
                spot = slice((part * depth + z) * lanes, (part * depth + z + 1) * lanes)
                high, low = split_high(layer[z] * scale)
                back_ref[rows, spot] = high
                back_ref[pl.ds(pl.multiple_of(double + index * chunk, chunk), chunk), spot] = low
                back_ref[pl.ds(pl.multiple_of(2 * double + index * chunk, chunk), chunk), spot] = high
        return carry

    lax.fori_loop(0, double // chunk, step, 0)
    back = dot(inverse_ref[...], back_ref[...])
    for plane in range(planes):
        part = slice(plane * lanes, (plane + 1) * lanes)
        value = back[:height, part] - turn(back[height:, part], sign)
        for number in range(count_y):
            out_refs[number][plane * local : (plane + 1) * local] = value[
                number * local : (number + 1) * local
            ]


def meeting(devices):
    return [number for number in range(devices - 1, 0, -1) if (number & (number + 1)) == 0]


def exchange_kernel(order_x, count_y, *refs):
    count_x, numbers = len(order_x), meeting(count_y)
    raw_refs, edge_refs, (place, ms_ref, aex_ref) = refs[:count_x], refs[count_x:-6], refs[-6:-3]
    exchange_ref, unit_ref, raw_ref = refs[-3:]
    depth, height, width = raw_ref.shape[2:]
    gx, gy = place[0], place[1]

    def row_beside(field, other):
        value = None
        for number, edge_ref in zip(numbers, edge_refs):
            edge = edge_ref[field]
            match = lax.bitwise_xor(gy, number) == other
            value = edge if value is None else jnp.where(match, edge, value)
        return value[:, None, :]

    for spot, number in enumerate(order_x):
        raw_ref[lax.bitwise_xor(gx, number)] = raw_refs[spot][...]
    left, right = jnp.maximum(gx - 1, 0), jnp.minimum(gx + 1, count_x - 1)
    shape = (depth, height, width)
    lane = lax.broadcasted_iota(jnp.int32, shape, 2)
    row = lax.broadcasted_iota(jnp.int32, shape, 1)

    def quantities(values):
        return directions(values[0], values[1]) + [looked_up(values[2], aex_ref)]

    raw = [raw_refs[0][f] for f in range(3)]
    here = quantities(raw)
    side = quantities([jnp.where(lane == 0, raw_ref[right, f], raw_ref[left, f]) for f in range(3)])
    above = quantities(
        [jnp.where(row == 0, row_beside(f, gy + 1), row_beside(f, gy - 1)) for f in range(3)]
    )
    saturation = looked_up(raw[2], ms_ref)
    total = [jnp.zeros(shape, jnp.float32) for _ in range(3)]

    def add(total, beside, weight):
        coupling = 2.0 * here[3] * beside[3] / (here[3] + beside[3]) * weight
        return [total[c] + coupling * (beside[c] - here[c]) for c in range(3)]

    one = jnp.float32(1.0)
    zero = jnp.float32(0.0)
    for shift, edge, there in ((1, 0, gx > 0), (width - 1, width - 1, gx < count_x - 1)):
        beside = [
            jnp.where(lane == edge, pltpu.roll(s, shift, 2), pltpu.roll(h, shift, 2))
            for s, h in zip(side, here)
        ]
        weight = jnp.where(lane == edge, jnp.where(there, one, zero), one) * side_weight
        total = add(total, beside, weight)
    for shift, edge, there in ((1, 0, gy > 0), (height - 1, height - 1, gy < count_y - 1)):
        beside = [
            jnp.where(row == edge, pltpu.roll(s, shift, 1), pltpu.roll(h, shift, 1))
            for s, h in zip(above, here)
        ]
        weight = jnp.where(row == edge, jnp.where(there, one, zero), one) * side_weight
        total = add(total, beside, weight)
    for part in range(3):
        unit_ref[part] = here[part]
    for z in range(depth):
        out = [total[c][z] for c in range(3)]
        for other in (z - 1, z + 1):
            if 0 <= other < depth:
                a, b = here[3][z], here[3][other]
                coupling = 2.0 * a * b / (a + b) * layer_weight
                out = [out[c] + coupling * (here[c][other] - here[c][z]) for c in range(3)]
        for c in range(3):
            exchange_ref[c, z] = out[c] / saturation[z]


def cross(first, second):
    return [
        first[1] * second[2] - first[2] * second[1],
        first[2] * second[0] - first[0] * second[2],
        first[0] * second[1] - first[1] * second[0],
    ]


def final_kernel(count_x, *refs):
    part_refs, (exchange_ref, unit_ref, field_ref, predicted_ref) = refs[:count_x], refs[count_x:]
    depth, height, width = unit_ref.shape[1:]
    rows = depth * height
    unit, field = [], []
    for c in range(3):
        place = slice(c * rows, (c + 1) * rows)
        total = part_refs[0][place]
        for part_ref in part_refs[1:]:
            total = total + part_ref[place]
        field.append(exchange_ref[c] + total.reshape(depth, height, width))
        unit.append(unit_ref[c])
        field_ref[c] = field[c]
    twist = cross(unit, field)
    second = cross(unit, twist)
    moved = [
        unit[c] - (time_step / (1.0 + damping * damping)) * (twist[c] + damping * second[c])
        for c in range(3)
    ]
    length = jnp.sqrt(moved[0] * moved[0] + moved[1] * moved[1] + moved[2] * moved[2])
    for c in range(3):
        predicted_ref[c] = moved[c] / length


vmem = pl.BlockSpec(memory_space=pltpu.VMEM)
smem = pl.BlockSpec(memory_space=pltpu.SMEM)
hbm = pl.BlockSpec(memory_space=pltpu.HBM)


def call(body, out, ins, operands, scratch=(), flops=0, name=None, grant=16 << 20):
    operands = [
        pltpu.with_memory_space_constraint(o, pltpu.HBM) if i is hbm else o
        for i, o in zip(ins, operands)
    ]
    size = sum(math.prod(o.shape) * o.dtype.itemsize for o in operands)
    outs = out if isinstance(out, (list, tuple)) else [out]
    size += sum(math.prod(o.shape) * jnp.dtype(o.dtype).itemsize for o in outs)
    return pl.pallas_call(
        body,
        out_shape=out,
        in_specs=ins,
        out_specs=[vmem] * len(outs) if outs is out else vmem,
        scratch_shapes=list(scratch),
        compiler_params=pltpu.CompilerParams(vmem_limit_bytes=grant),
        cost_estimate=pl.CostEstimate(flops=flops, bytes_accessed=size, transcendentals=0),
        name=name,
    )(*operands)


def f32(*shape):
    return jax.ShapeDtypeStruct(shape, jnp.float32)


def swapped(chunk, axis, number):
    devices = lax.axis_size(axis)
    return lax.ppermute(chunk, axis, [(i, i ^ number) for i in range(devices)])


def exchanged(chunks, axis, order):
    return [swapped(c, axis, n) if n else c for c, n in zip(chunks, order)]


def after(value, other):
    return lax.optimization_barrier((value, other))[0]


def spread(block, axis, first):
    blocks = {0: block}
    bit = lax.axis_size(axis) // 2
    while bit:
        for number in list(blocks):
            blocks[number ^ bit] = swapped(blocks[number], axis, bit)
        if first is not None:
            blocks[bit], first = lax.optimization_barrier((blocks[bit], first))
            ready, first = first, None
        bit //= 2
    return [blocks[number] for number in range(lax.axis_size(axis))], ready


def gathered_sums(blocks, axis):
    blocks = {number: [block] for number, block in enumerate(blocks)}
    bit = 1
    while bit < lax.axis_size(axis):
        for number in sorted(blocks, reverse=True):
            if number & bit:
                block = functools.reduce(jnp.add, blocks.pop(number))
                blocks[number ^ bit].append(swapped(block, axis, bit))
        bit *= 2
    return blocks[0], block


def per_device(theta, phi, labels, ms_region, aex_region, kernel):
    count_x, count_y = lax.axis_size("gx"), lax.axis_size("gy")
    gx, gy = lax.axis_index("gx"), lax.axis_index("gy")
    depth, height, width = theta.shape
    rows = kernel.shape[2]
    lanes = 2 * rows
    lines = 3 * depth * height
    whole_y = count_y * height

    place = jnp.stack([gx, gy]).astype(jnp.int32)
    cells = f32(3, depth, height, width)
    order_x, order_y = list(range(count_x)), list(range(count_y - 1, -1, -1))
    table = line_table(count_x, count_y, width, rows)
    if table is None:
        table = line_table_here(count_x, width, rows, order_y)
        columns_tables = column_tables_here(count_y, height, order_y)
    else:
        columns_tables = column_tables(count_y, height, order_y)
    sources = [jnp.asarray(t) for t in (table, *columns_tables)]
    twice = np.concatenate([np.eye(rows), np.eye(rows)], 1).astype(ml_dtypes.bfloat16)
    transform_flops = 6 * lines * count_x * width * count_y * lanes

    edge = f32(3, depth, width)
    packed, first, last = call(
        pack_kernel,
        [cells, edge, edge],
        [hbm] * 3,
        (theta, phi, labels),
        scratch=(
            pltpu.VMEM((2, depth, height, width), jnp.float32),
            pltpu.VMEM((depth, height, width), jnp.int32),
            pltpu.SemaphoreType.DMA((3,)),
        ),
        name="pack",
    )
    table, forward, inverse = call(
        functools.partial(load_kernel, order_x, order_y),
        [
            pltpu.VMEM((2, count_x, width, count_y * lanes), jnp.bfloat16),
            pltpu.VMEM(sources[1].shape[1:], jnp.bfloat16),
            pltpu.VMEM(sources[2].shape[1:], jnp.bfloat16),
        ],
        [smem] + [hbm] * 3,
        (place, *sources),
        scratch=(pltpu.SemaphoreType.DMA((2 + count_x * count_y,)),),
        name="load",
    )

    gathered, table = spread(packed, "gx", table)
    tensor = call(
        tensor_kernel,
        jax.ShapeDtypeStruct((48, 2 * whole_y, lanes), jnp.bfloat16),
        [vmem, vmem],
        (kernel.reshape(48, rows, 2 * whole_y), jnp.asarray(twice)),
        flops=48 * 2 * rows * lanes * 2 * whole_y,
        name="tensor",
    )
    gathered, tensor = lax.optimization_barrier((gathered, tensor))
    spectrum = call(
        functools.partial(lines_kernel, count_x),
        [f32(lines, lanes)] * count_y,
        [vmem] * count_x + [hbm, vmem],
        (*gathered, ms_region, table),
        scratch=(pltpu.SMEM(ms_region.shape, jnp.float32), pltpu.SemaphoreType.DMA),
        flops=transform_flops,
        name="lines",
    )
    columns = exchanged(spectrum, "gy", order_y)
    first, last = after((first, last), columns[1])
    edges = [
        swapped(jnp.where(lax.bitwise_xor(gy, number) > gy, last, first), "gy", number)
        for number in meeting(count_y)
    ]
    columns, edges = lax.optimization_barrier((columns, edges))
    scale = -1.0 / (2 * depth * 2 * whole_y * 2 * count_x * width)
    waves = call(
        functools.partial(waves_kernel, scale, count_y),
        [f32(lines, lanes)] * count_y,
        [vmem] * (count_y + 3),
        (*columns, tensor, forward, inverse),
        scratch=(
            pltpu.VMEM((2 * whole_y, 3 * depth * lanes), jnp.float32),
            pltpu.VMEM((6 * whole_y, 3 * depth * lanes), jnp.bfloat16),
        ),
        flops=20 * whole_y * whole_y * 3 * depth * lanes,
        name="waves",
    )
    returned = exchanged(waves, "gy", order_y)
    across = [number for number in range(count_x) if number % 2]
    within = [number for number in range(count_x) if not number % 2]
    partial = [None] * count_x
    for numbers, name in ((across, "back_across"), (within, "back_within")):
        blocks = call(
            functools.partial(back_lines_kernel, numbers, count_y),
            [f32(lines, width)] * len(numbers),
            [vmem] * (count_y + 1),
            (*returned, table),
            flops=transform_flops // 2,
            name=name,
        )
        for number, block in zip(numbers, blocks):
            partial[number] = block
    parts, far_sum = gathered_sums(partial, "gx")
    edges, far_sum = lax.optimization_barrier((edges, far_sum))
    exchange, unit = call(
        functools.partial(exchange_kernel, order_x, count_y),
        [cells, cells],
        [vmem] * (count_x + len(edges)) + [smem] * 3,
        (*gathered, *edges, place, ms_region, aex_region),
        scratch=(pltpu.VMEM((count_x, 3, depth, height, width), jnp.float32),),
        flops=300 * depth * height * width,
        name="exchange",
    )
    field, predicted = call(
        functools.partial(final_kernel, len(parts)),
        [cells, cells],
        [vmem] * (len(parts) + 2),
        (*parts, exchange, unit),
        flops=60 * depth * height * width,
        name="predict",
    )
    return field, predicted


def solution(mesh):
    in_specs = (
        P(None, "gy", "gx"),
        P(None, "gy", "gx"),
        P(None, "gy", "gx"),
        P(),
        P(),
        P(None, None, ("gx", "gy"), None),
    )
    out_specs = (P(None, None, "gy", "gx"), P(None, None, "gy", "gx"))
    return jax.shard_map(
        per_device, mesh=mesh, in_specs=in_specs, out_specs=out_specs, check_vma=False
    )
```

```python
import functools
import math

import jax
import jax.numpy as jnp
import ml_dtypes
import numpy as np
from jax import lax
from jax.experimental import pallas as pl
from jax.experimental.pallas import tpu as pltpu
from jax.sharding import PartitionSpec as P

damping = 0.5
time_step = 0.2
side_weight = 0.25
layer_weight = 0.5
root_half = math.sqrt(0.5)
constant_limit = 20 << 20


def split_high(value):
    high = value.astype(jnp.bfloat16)
    low = (value - high.astype(jnp.float32)).astype(jnp.bfloat16)
    return high, low


def split_table(table):
    high = table.astype(np.float32).astype(ml_dtypes.bfloat16)
    low = (table - high.astype(np.float64)).astype(np.float32).astype(ml_dtypes.bfloat16)
    return high, low


def dot(left, right, contract=((1,), (0,))):
    return lax.dot_general(left, right, (contract, ((), ())), preferred_element_type=jnp.float32)


def line_table(count_x, count_y, width, rows):
    cells = count_x * width
    if count_x * 2 * cells * count_y * 2 * rows * 2 > constant_limit:
        return None
    place = np.arange(cells)[None, None, :, None]
    wave = (
        np.arange(count_x)[:, None, None, None] * (count_y * rows)
        + np.arange(count_y)[None, :, None, None] * rows
        + np.arange(rows)[None, None, None, :]
    )
    angle = (place * wave % (2 * cells)) * (2.0 * math.pi / (2 * cells))
    table = np.concatenate([np.cos(angle), -np.sin(angle)], 3)
    table = table.reshape(count_x, count_y, count_x, width, 2 * rows)
    high, low = split_table(table)
    return np.stack([high, low], 2)


def line_table_here(count_x, width, rows, order):
    cells = count_x * width
    count_y = len(order)
    place = jnp.arange(cells, dtype=jnp.int32)[:, None, None]
    block = lax.bitwise_xor(lax.axis_index("gy"), jnp.array(order, jnp.int32))
    wave = (
        lax.axis_index("gx") * (count_y * rows)
        + block[None, :, None] * rows
        + jnp.arange(rows, dtype=jnp.int32)[None, None, :]
    )
    angle = (place * wave % (2 * cells)).astype(jnp.float32) * (math.pi / cells)
    table = jnp.concatenate([jnp.cos(angle), -jnp.sin(angle)], 2)
    table = table.reshape(1, 1, count_x, width, count_y * 2 * rows)
    return jnp.stack(split_high(table), 2)


def column_tables(count_y, local, order):
    height = count_y * local
    wave = np.arange(2 * height)
    block = np.arange(count_y)[:, None] ^ np.array(order)[None, :]
    place = (block[:, :, None] * local + np.arange(local)).reshape(count_y, height)
    angle = (wave[None, :, None] * place[:, None, :] % (2 * height)) * (math.pi / height)
    high, low = split_table(np.concatenate([np.cos(angle), np.sin(angle)], 2))
    forward = np.concatenate([high, high, low], 2)
    angle = angle.transpose(0, 2, 1)
    high, low = split_table(np.concatenate([np.cos(angle), np.sin(angle)], 1))
    inverse = np.concatenate([high, high, low], 2)
    return forward, inverse


def column_tables_here(count_y, local, order):
    height = count_y * local
    wave = jnp.arange(2 * height, dtype=jnp.int32)
    block = lax.bitwise_xor(lax.axis_index("gy"), jnp.array(order, jnp.int32))
    place = (block[:, None] * local + jnp.arange(local, dtype=jnp.int32)).reshape(height)
    angle = (wave[:, None] * place % (2 * height)).astype(jnp.float32) * (math.pi / height)
    high, low = split_high(jnp.concatenate([jnp.cos(angle), jnp.sin(angle)], 1))
    forward = jnp.concatenate([high, high, low], 1)
    high, low = split_high(jnp.concatenate([jnp.cos(angle.T), jnp.sin(angle.T)], 0))
    inverse = jnp.concatenate([high, high, low], 1)
    return forward[None], inverse[None]


def load_kernel(order_x, order_y, place, *refs):
    table_ref, forward_ref, inverse_ref, table, forward, inverse, sem = refs
    gx, gy = place[0], place[1]
    mine_x = gx if table_ref.shape[0] > 1 else 0
    mine_y = gy if forward_ref.shape[0] > 1 else 0
    lanes = table_ref.shape[5]
    copies = [
        pltpu.make_async_copy(forward_ref.at[mine_y], forward, sem.at[0]),
        pltpu.make_async_copy(inverse_ref.at[mine_y], inverse, sem.at[1]),
    ]
    for spot_x, number_x in enumerate(order_x):
        block_x = lax.bitwise_xor(gx, number_x)
        for spot_y in range(table_ref.shape[1]):
            block_y = lax.bitwise_xor(gy, order_y[spot_y]) if table_ref.shape[1] > 1 else 0
            columns = slice(spot_y * lanes, (spot_y + 1) * lanes)
            copies.append(
                pltpu.make_async_copy(
                    table_ref.at[mine_x, block_y, :, block_x],
                    table.at[:, spot_x, :, columns],
                    sem.at[len(copies)],
                )
            )
    for copy in copies:
        copy.start()
    for copy in copies:
        copy.wait()


def sine_cosine(angle):
    turns = jnp.floor(angle * (2.0 / math.pi) + 0.5)
    rest = angle - turns * 1.5703125
    rest = rest - turns * 4.8351287841796875e-4
    rest = rest - turns * 3.1385570764541626e-7
    square = rest * rest
    sine = rest + rest * square * (
        -1.6666654611e-1 + square * (8.3321608736e-3 - square * 1.9515295891e-4)
    )
    cosine = (
        1.0
        - 0.5 * square
        + square * square * (4.166664568298827e-2 + square * (-1.388731625493765e-3 + square * 2.443315711809948e-5))
    )
    quarter = turns.astype(jnp.int32)
    odd = (quarter & 1) == 1
    out_sine = jnp.where(odd, cosine, sine)
    out_cosine = jnp.where(odd, sine, cosine)
    out_sine = jnp.where((quarter & 2) == 2, -out_sine, out_sine)
    out_cosine = jnp.where(((quarter + 1) & 2) == 2, -out_cosine, out_cosine)
    return out_sine, out_cosine


def directions(theta, phi):
    lateral, axial = sine_cosine(theta)
    sine, cosine = sine_cosine(phi)
    return [lateral * cosine, lateral * sine, axial]


def looked_up(labels, region):
    result = jnp.zeros_like(labels) + region[0]
    for index in range(1, region.shape[0]):
        result = jnp.where(labels == float(index), region[index], result)
    return result


def pack_kernel(theta_ref, phi_ref, labels_ref, raw_ref, first_ref, last_ref, angle, label, sems):
    height = theta_ref.shape[1]
    copies = [
        pltpu.make_async_copy(theta_ref, angle.at[0], sems.at[0]),
        pltpu.make_async_copy(phi_ref, angle.at[1], sems.at[1]),
        pltpu.make_async_copy(labels_ref, label, sems.at[2]),
    ]
    for copy in copies:
        copy.start()
    for copy in copies:
        copy.wait()
    for index, value in enumerate((angle[0], angle[1], label[...].astype(jnp.float32))):
        raw_ref[index] = value
        put_edge(first_ref, index, value[:, 0])
        put_edge(last_ref, index, value[:, height - 1])


def meeting(devices):
    return [number for number in range(1, devices) if (number & (number + 1)) == 0]


def edge_spots(depth, width, lanes, start, field):
    pieces = width // lanes
    return [start + (field * pieces + piece) * depth for piece in range(pieces)]


def put_edge(ref, field, edge):
    lanes = ref.shape[1]
    for piece, row in enumerate(edge_spots(*edge.shape, lanes, 0, field)):
        ref[row : row + edge.shape[0]] = edge[:, piece * lanes : (piece + 1) * lanes]


def get_edge(ref, depth, width, start, field):
    spots = edge_spots(depth, width, ref.shape[1], start, field)
    return jnp.concatenate([ref[row : row + depth] for row in spots], 1)


def lines_kernel(count_x, order_y, *refs):
    raw_refs, operands = refs[:count_x], refs[count_x : count_x + 5]
    first_ref, last_ref, region_ref, place, table = operands
    out_refs, (region, sem) = refs[count_x + 5 : -2], refs[-2:]
    fetch = pltpu.make_async_copy(region_ref, region, sem)
    fetch.start()
    units = [directions(raw_ref[0], raw_ref[1]) for raw_ref in raw_refs]
    fetch.wait()
    total = None
    for number in range(count_x):
        saturation = looked_up(raw_refs[number][2], region)
        rows = saturation.shape[0] * saturation.shape[1]
        block = [(part * saturation).reshape(rows, -1) for part in units[number]]
        high, low = split_high(jnp.concatenate(block, 0))
        both = dot(jnp.concatenate([high, low], 0), table[0, number])
        part = both[: 3 * rows] + both[3 * rows :] + dot(high, table[1, number])
        total = part if total is None else total + part
    lanes = out_refs[0].shape[1]
    for spot, (number, out_ref) in enumerate(zip(order_y, out_refs)):
        out_ref[: 3 * rows] = total[:, spot * lanes : (spot + 1) * lanes]
        if number in meeting(len(order_y)):
            up = lax.bitwise_xor(place[1], number) > place[1]
            out_ref[3 * rows :] = jnp.where(up, last_ref[...], first_ref[...])


def back_lines_kernel(numbers, count_y, *refs):
    in_refs, table, out_refs = refs[:count_y], refs[count_y], refs[count_y + 1 :]
    high, low = split_high(jnp.concatenate([ref[...] for ref in in_refs], 1))
    both = jnp.concatenate([high, low], 0)
    lines = high.shape[0]
    for number, out_ref in zip(numbers, out_refs):
        wide = dot(both, table[0, number], ((1,), (1,)))
        out_ref[...] = wide[:lines] + wide[lines:] + dot(high, table[1, number], ((1,), (1,)))


def tensor_kernel(kernel_ref, twice_ref, out_ref):
    twice = twice_ref[...]

    unroll = 8

    def step(index, carry):
        for offset in range(unroll):
            turned = dot(kernel_ref[index * unroll + offset], twice, ((0,), (0,)))
            out_ref[index * unroll + offset] = turned.astype(jnp.bfloat16)
        return carry

    lax.fori_loop(0, kernel_ref.shape[0] // unroll, step, 0)


def turn(value, sign):
    lanes = value.shape[-1]
    if lanes == 128:
        return pltpu.roll(value, lanes // 2, value.ndim - 1) * sign
    return jnp.concatenate([value[..., lanes // 2 :], value[..., : lanes // 2]], -1) * sign


def layers_forward(layer, sign):
    d0, d1, d2, d3 = layer
    r2 = turn(d2, sign)
    near, far = d1 + d3, d1 - d3
    far_turned = turn(far, sign)
    near_turned = turn(near, sign)
    even, odd = d0 + d2, d0 - d2
    out = [None] * 8
    out[0], out[4] = even + near, even - near
    out[2], out[6] = odd + far_turned, odd - far_turned
    plus, minus = d0 + r2, d0 - r2
    first = (far + near_turned) * root_half
    second = (near_turned - far) * root_half
    out[1], out[5] = plus + first, plus - first
    out[3], out[7] = minus + second, minus - second
    return out


def layers_inverse(wave, sign):
    a, b = wave[0] + wave[4], wave[0] - wave[4]
    e, f = wave[2] + wave[6], turn(wave[2] - wave[6], sign)
    p, q = wave[1] + wave[5], wave[1] - wave[5]
    s, t = wave[3] + wave[7], turn(wave[3] - wave[7], sign)
    o0, o1, o2, o3 = p + s, q - t, p - s, q + t
    return [
        a + e + o0,
        b - f + (o1 - turn(o1, sign)) * root_half,
        a - e - turn(o2, sign),
        b + f - (o3 + turn(o3, sign)) * root_half,
    ]


def apply_tensor(tensor, wave):
    out = [[], [], []]
    for level in range(8):
        xx, yy, zz, xy, xz, yz = [tensor[part][level] for part in range(6)]
        x, y, z = wave[0][level], wave[1][level], wave[2][level]
        out[0].append(xx * x + xy * y + xz * z)
        out[1].append(xy * x + yy * y + yz * z)
        out[2].append(xz * x + yz * y + zz * z)
    return out


def waves_kernel(scale, count_y, *refs):
    spec_refs, (tensor_ref, forward_ref, inverse_ref) = refs[:count_y], refs[count_y : count_y + 3]
    out_refs, (wave_ref, back_ref) = refs[count_y + 3 : -2], refs[-2:]
    lines, lanes = out_refs[0].shape
    local = 8
    planes = lines // local
    height = count_y * local
    sign = jnp.where(
        lax.broadcasted_iota(jnp.int32, (1, lanes), 1) < lanes // 2, 1.0, -1.0
    ).astype(jnp.float32)
    columns = []
    for plane in range(planes):
        value = jnp.concatenate(
            [spec_ref[plane * local : (plane + 1) * local] for spec_ref in spec_refs], 0
        )
        value = jnp.concatenate([value, turn(value, sign)], 0)
        high, low = split_high(value)
        columns.append(jnp.concatenate([high, low, high], 0))
    wave_ref[...] = dot(forward_ref[...], jnp.concatenate(columns, 1))

    chunk = 16
    depth = planes // 3
    double = 2 * height

    def step(index, carry):
        rows = pl.ds(pl.multiple_of(index * chunk, chunk), chunk)
        wave = []
        for part in range(3):
            layer = [
                wave_ref[rows, (part * depth + z) * lanes : (part * depth + z + 1) * lanes]
                for z in range(depth)
            ]
            wave.append(layers_forward(layer, sign))
        tensor = [
            [tensor_ref[part * 8 + level, rows, :].astype(jnp.float32) for level in range(8)]
            for part in range(6)
        ]
        image = apply_tensor(tensor, wave)
        for part in range(3):
            layer = layers_inverse(image[part], sign)
            for z in range(depth):
                spot = slice((part * depth + z) * lanes, (part * depth + z + 1) * lanes)
                high, low = split_high(layer[z] * scale)
                back_ref[rows, spot] = high
                back_ref[pl.ds(pl.multiple_of(double + index * chunk, chunk), chunk), spot] = low
                back_ref[pl.ds(pl.multiple_of(2 * double + index * chunk, chunk), chunk), spot] = high
        return carry

    lax.fori_loop(0, double // chunk, step, 0)
    back = dot(inverse_ref[...], back_ref[...])
    for plane in range(planes):
        part = slice(plane * lanes, (plane + 1) * lanes)
        value = back[:height, part] - turn(back[height:, part], sign)
        for number in range(count_y):
            out_refs[number][plane * local : (plane + 1) * local] = value[
                number * local : (number + 1) * local
            ]


def exchange_kernel(order_x, count_y, *refs):
    count_x, numbers = len(order_x), meeting(count_y)
    raw_refs, edge_refs, (place, ms_ref, aex_ref) = refs[:count_x], refs[count_x:-6], refs[-6:-3]
    exchange_ref, unit_ref, raw_ref = refs[-3:]
    depth, height, width = raw_ref.shape[2:]
    gx, gy = place[0], place[1]

    def row_beside(field, other):
        value = None
        for number, edge_ref in zip(numbers, edge_refs):
            edge = get_edge(edge_ref, depth, width, 3 * depth * height, field)
            match = lax.bitwise_xor(gy, number) == other
            value = edge if value is None else jnp.where(match, edge, value)
        return value[:, None, :]

    for spot, number in enumerate(order_x):
        raw_ref[lax.bitwise_xor(gx, number)] = raw_refs[spot][...]
    left, right = jnp.maximum(gx - 1, 0), jnp.minimum(gx + 1, count_x - 1)
    shape = (depth, height, width)
    lane = lax.broadcasted_iota(jnp.int32, shape, 2)
    row = lax.broadcasted_iota(jnp.int32, shape, 1)

    def quantities(values):
        return directions(values[0], values[1]) + [looked_up(values[2], aex_ref)]

    raw = [raw_refs[0][f] for f in range(3)]
    here = quantities(raw)
    side = quantities([jnp.where(lane == 0, raw_ref[right, f], raw_ref[left, f]) for f in range(3)])
    above = quantities(
        [jnp.where(row == 0, row_beside(f, gy + 1), row_beside(f, gy - 1)) for f in range(3)]
    )
    saturation = looked_up(raw[2], ms_ref)
    total = [jnp.zeros(shape, jnp.float32) for _ in range(3)]

    def add(total, beside, weight):
        coupling = 2.0 * here[3] * beside[3] / (here[3] + beside[3]) * weight
        return [total[c] + coupling * (beside[c] - here[c]) for c in range(3)]

    one = jnp.float32(1.0)
    zero = jnp.float32(0.0)
    for shift, edge, there in ((1, 0, gx > 0), (width - 1, width - 1, gx < count_x - 1)):
        beside = [
            jnp.where(lane == edge, pltpu.roll(s, shift, 2), pltpu.roll(h, shift, 2))
            for s, h in zip(side, here)
        ]
        weight = jnp.where(lane == edge, jnp.where(there, one, zero), one) * side_weight
        total = add(total, beside, weight)
    for shift, edge, there in ((1, 0, gy > 0), (height - 1, height - 1, gy < count_y - 1)):
        beside = [
            jnp.where(row == edge, pltpu.roll(s, shift, 1), pltpu.roll(h, shift, 1))
            for s, h in zip(above, here)
        ]
        weight = jnp.where(row == edge, jnp.where(there, one, zero), one) * side_weight
        total = add(total, beside, weight)
    for part in range(3):
        unit_ref[part] = here[part]
    for z in range(depth):
        out = [total[c][z] for c in range(3)]
        for other in (z - 1, z + 1):
            if 0 <= other < depth:
                a, b = here[3][z], here[3][other]
                coupling = 2.0 * a * b / (a + b) * layer_weight
                out = [out[c] + coupling * (here[c][other] - here[c][z]) for c in range(3)]
        for c in range(3):
            exchange_ref[c, z] = out[c] / saturation[z]


def cross(first, second):
    return [
        first[1] * second[2] - first[2] * second[1],
        first[2] * second[0] - first[0] * second[2],
        first[0] * second[1] - first[1] * second[0],
    ]


def final_kernel(count_x, *refs):
    part_refs, (exchange_ref, unit_ref, field_ref, predicted_ref) = refs[:count_x], refs[count_x:]
    depth, height, width = unit_ref.shape[1:]
    rows = depth * height
    unit, field = [], []
    for c in range(3):
        place = slice(c * rows, (c + 1) * rows)
        total = part_refs[0][place]
        for part_ref in part_refs[1:]:
            total = total + part_ref[place]
        field.append(exchange_ref[c] + total.reshape(depth, height, width))
        unit.append(unit_ref[c])
        field_ref[c] = field[c]
    twist = cross(unit, field)
    second = cross(unit, twist)
    moved = [
        unit[c] - (time_step / (1.0 + damping * damping)) * (twist[c] + damping * second[c])
        for c in range(3)
    ]
    length = jnp.sqrt(moved[0] * moved[0] + moved[1] * moved[1] + moved[2] * moved[2])
    for c in range(3):
        predicted_ref[c] = moved[c] / length


vmem = pl.BlockSpec(memory_space=pltpu.VMEM)
smem = pl.BlockSpec(memory_space=pltpu.SMEM)
hbm = pl.BlockSpec(memory_space=pltpu.HBM)


def call(body, out, ins, operands, scratch=(), flops=0, name=None, grant=16 << 20):
    operands = [
        pltpu.with_memory_space_constraint(o, pltpu.HBM) if i is hbm else o
        for i, o in zip(ins, operands)
    ]
    size = sum(math.prod(o.shape) * o.dtype.itemsize for o in operands)
    outs = out if isinstance(out, (list, tuple)) else [out]
    size += sum(math.prod(o.shape) * jnp.dtype(o.dtype).itemsize for o in outs)
    return pl.pallas_call(
        body,
        out_shape=out,
        in_specs=ins,
        out_specs=[vmem] * len(outs) if outs is out else vmem,
        scratch_shapes=list(scratch),
        compiler_params=pltpu.CompilerParams(vmem_limit_bytes=grant),
        cost_estimate=pl.CostEstimate(flops=flops, bytes_accessed=size, transcendentals=0),
        name=name,
    )(*operands)


def f32(*shape):
    return jax.ShapeDtypeStruct(shape, jnp.float32)


def swapped(chunk, axis, number):
    devices = lax.axis_size(axis)
    return lax.ppermute(chunk, axis, [(i, i ^ number) for i in range(devices)])


def exchanged(chunks, axis, order):
    return [swapped(c, axis, n) if n else c for c, n in zip(chunks, order)]


def held(value):
    return pltpu.with_memory_space_constraint(value, pltpu.VMEM)


def after(value, other):
    return lax.optimization_barrier((value, other))[0]


def spread(block, axis, first):
    blocks = {0: block}
    bit = lax.axis_size(axis) // 2
    while bit:
        for number in list(blocks):
            blocks[number ^ bit] = swapped(blocks[number], axis, bit)
        if first is not None:
            blocks[bit], first = lax.optimization_barrier((blocks[bit], first))
            ready, first = first, None
        bit //= 2
    return [blocks[number] for number in range(lax.axis_size(axis))], ready


def gathered_sums(blocks, axis):
    blocks = {number: [block] for number, block in enumerate(blocks)}
    bit = 1
    while bit < lax.axis_size(axis):
        for number in sorted(blocks, reverse=True):
            if number & bit:
                block = functools.reduce(jnp.add, blocks.pop(number))
                blocks[number ^ bit].append(swapped(block, axis, bit))
        bit *= 2
    return blocks[0], block


def per_device(theta, phi, labels, ms_region, aex_region, kernel):
    count_x, count_y = lax.axis_size("gx"), lax.axis_size("gy")
    gx, gy = lax.axis_index("gx"), lax.axis_index("gy")
    depth, height, width = theta.shape
    rows = kernel.shape[2]
    lanes = 2 * rows
    lines = 3 * depth * height
    whole_y = count_y * height

    place = jnp.stack([gx, gy]).astype(jnp.int32)
    cells = f32(3, depth, height, width)
    order_x, order_y = list(range(count_x)), list(range(count_y - 1, -1, -1))
    table = line_table(count_x, count_y, width, rows)
    if table is None:
        table = line_table_here(count_x, width, rows, order_y)
        columns_tables = column_tables_here(count_y, height, order_y)
    else:
        columns_tables = column_tables(count_y, height, order_y)
    sources = [jnp.asarray(t) for t in (table, *columns_tables)]
    twice = np.concatenate([np.eye(rows), np.eye(rows)], 1).astype(ml_dtypes.bfloat16)
    transform_flops = 6 * lines * count_x * width * count_y * lanes

    edge_rows = 3 * depth * width // lanes
    edge = f32(edge_rows, lanes)
    packed, first, last = call(
        pack_kernel,
        [cells, edge, edge],
        [hbm] * 3,
        (theta, phi, labels),
        scratch=(
            pltpu.VMEM((2, depth, height, width), jnp.float32),
            pltpu.VMEM((depth, height, width), jnp.int32),
            pltpu.SemaphoreType.DMA((3,)),
        ),
        name="pack",
    )
    table, forward, inverse = call(
        functools.partial(load_kernel, order_x, order_y),
        [
            pltpu.VMEM((2, count_x, width, count_y * lanes), jnp.bfloat16),
            pltpu.VMEM(sources[1].shape[1:], jnp.bfloat16),
            pltpu.VMEM(sources[2].shape[1:], jnp.bfloat16),
        ],
        [smem] + [hbm] * 3,
        (place, *sources),
        scratch=(pltpu.SemaphoreType.DMA((2 + count_x * count_y,)),),
        name="load",
    )

    gathered, table = spread(packed, "gx", table)
    tensor = call(
        tensor_kernel,
        jax.ShapeDtypeStruct((48, 2 * whole_y, lanes), jnp.bfloat16),
        [vmem, vmem],
        (kernel.reshape(48, rows, 2 * whole_y), jnp.asarray(twice)),
        flops=48 * 2 * rows * lanes * 2 * whole_y,
        name="tensor",
    )
    spectrum = call(
        functools.partial(lines_kernel, count_x, order_y),
        [f32(lines + (edge_rows if n in meeting(count_y) else 0), lanes) for n in order_y],
        [vmem] * (count_x + 2) + [hbm, smem, vmem],
        (*gathered, first, last, ms_region, place, held(table)),
        scratch=(pltpu.SMEM(ms_region.shape, jnp.float32), pltpu.SemaphoreType.DMA),
        flops=transform_flops,
        name="lines",
    )
    columns = lax.optimization_barrier(exchanged(spectrum, "gy", order_y))
    scale = -1.0 / (2 * depth * 2 * whole_y * 2 * count_x * width)
    waves = call(
        functools.partial(waves_kernel, scale, count_y),
        [f32(lines, lanes)] * count_y,
        [vmem] * (count_y + 3),
        (*columns, tensor, forward, inverse),
        scratch=(
            pltpu.VMEM((2 * whole_y, 3 * depth * lanes), jnp.float32),
            pltpu.VMEM((6 * whole_y, 3 * depth * lanes), jnp.bfloat16),
        ),
        flops=20 * whole_y * whole_y * 3 * depth * lanes,
        name="waves",
    )
    returned = exchanged(waves, "gy", order_y)
    across = [number for number in range(count_x) if number % 2]
    within = [number for number in range(count_x) if not number % 2]
    partial = [None] * count_x
    for numbers, name in ((across, "back_across"), (within, "back_within")):
        blocks = call(
            functools.partial(back_lines_kernel, numbers, count_y),
            [f32(lines, width)] * len(numbers),
            [vmem] * (count_y + 1),
            (*returned, held(table)),
            flops=transform_flops // 2,
            name=name,
        )
        for number, block in zip(numbers, blocks):
            partial[number] = block
    parts, far_sum = gathered_sums(partial, "gx")
    edges = [columns[order_y.index(number)] for number in meeting(count_y)]
    edges, far_sum = lax.optimization_barrier((edges, far_sum))
    exchange, unit = call(
        functools.partial(exchange_kernel, order_x, count_y),
        [cells, cells],
        [vmem] * (count_x + len(edges)) + [smem] * 3,
        (*gathered, *edges, place, ms_region, aex_region),
        scratch=(pltpu.VMEM((count_x, 3, depth, height, width), jnp.float32),),
        flops=300 * depth * height * width,
        name="exchange",
    )
    field, predicted = call(
        functools.partial(final_kernel, len(parts)),
        [cells, cells],
        [vmem] * (len(parts) + 2),
        (*parts, exchange, unit),
        flops=60 * depth * height * width,
        name="predict",
    )
    return field, predicted


def solution(mesh):
    in_specs = (
        P(None, "gy", "gx"),
        P(None, "gy", "gx"),
        P(None, "gy", "gx"),
        P(),
        P(),
        P(None, None, ("gx", "gy"), None),
    )
    out_specs = (P(None, None, "gy", "gx"), P(None, None, "gy", "gx"))
    return jax.shard_map(
        per_device, mesh=mesh, in_specs=in_specs, out_specs=out_specs, check_vma=False
    )
```

```python
import functools
import math

import jax
import jax.numpy as jnp
import ml_dtypes
import numpy as np
from jax import lax
from jax.experimental import pallas as pl
from jax.experimental.pallas import tpu as pltpu
from jax.sharding import PartitionSpec as P

damping = 0.5
time_step = 0.2
side_weight = 0.25
layer_weight = 0.5
root_half = math.sqrt(0.5)
constant_limit = 20 << 20


def split_high(value):
    high = value.astype(jnp.bfloat16)
    low = (value - high.astype(jnp.float32)).astype(jnp.bfloat16)
    return high, low


def split_table(table):
    high = table.astype(np.float32).astype(ml_dtypes.bfloat16)
    low = (table - high.astype(np.float64)).astype(np.float32).astype(ml_dtypes.bfloat16)
    return high, low


def dot(left, right, contract=((1,), (0,))):
    return lax.dot_general(left, right, (contract, ((), ())), preferred_element_type=jnp.float32)


def line_table(count_x, count_y, width, rows):
    cells = count_x * width
    if count_x * 2 * cells * count_y * 2 * rows * 2 > constant_limit:
        return None
    place = np.arange(cells)[None, None, :, None]
    wave = (
        np.arange(count_x)[:, None, None, None] * (count_y * rows)
        + np.arange(count_y)[None, :, None, None] * rows
        + np.arange(rows)[None, None, None, :]
    )
    angle = (place * wave % (2 * cells)) * (2.0 * math.pi / (2 * cells))
    table = np.concatenate([np.cos(angle), -np.sin(angle)], 3)
    table = table.reshape(count_x, count_y, count_x, width, 2 * rows)
    high, low = split_table(table)
    return np.stack([high, low], 2)


def line_table_here(count_x, width, rows, order):
    cells = count_x * width
    count_y = len(order)
    place = jnp.arange(cells, dtype=jnp.int32)[:, None, None]
    block = lax.bitwise_xor(lax.axis_index("gy"), jnp.array(order, jnp.int32))
    wave = (
        lax.axis_index("gx") * (count_y * rows)
        + block[None, :, None] * rows
        + jnp.arange(rows, dtype=jnp.int32)[None, None, :]
    )
    angle = (place * wave % (2 * cells)).astype(jnp.float32) * (math.pi / cells)
    table = jnp.concatenate([jnp.cos(angle), -jnp.sin(angle)], 2)
    table = table.reshape(1, 1, count_x, width, count_y * 2 * rows)
    return jnp.stack(split_high(table), 2)


def column_tables(count_y, local, order):
    height = count_y * local
    wave = np.arange(2 * height)
    block = np.arange(count_y)[:, None] ^ np.array(order)[None, :]
    place = (block[:, :, None] * local + np.arange(local)).reshape(count_y, height)
    angle = (wave[None, :, None] * place[:, None, :] % (2 * height)) * (math.pi / height)
    high, low = split_table(np.concatenate([np.cos(angle), np.sin(angle)], 2))
    forward = np.concatenate([high, high, low], 2)
    angle = angle.transpose(0, 2, 1)
    high, low = split_table(np.concatenate([np.cos(angle), np.sin(angle)], 1))
    inverse = np.concatenate([high, high, low], 2)
    return forward, inverse


def column_tables_here(count_y, local, order):
    height = count_y * local
    wave = jnp.arange(2 * height, dtype=jnp.int32)
    block = lax.bitwise_xor(lax.axis_index("gy"), jnp.array(order, jnp.int32))
    place = (block[:, None] * local + jnp.arange(local, dtype=jnp.int32)).reshape(height)
    angle = (wave[:, None] * place % (2 * height)).astype(jnp.float32) * (math.pi / height)
    high, low = split_high(jnp.concatenate([jnp.cos(angle), jnp.sin(angle)], 1))
    forward = jnp.concatenate([high, high, low], 1)
    high, low = split_high(jnp.concatenate([jnp.cos(angle.T), jnp.sin(angle.T)], 0))
    inverse = jnp.concatenate([high, high, low], 1)
    return forward[None], inverse[None]


def load_kernel(order_x, order_y, *refs):
    table_ref, forward_ref, inverse_ref, table, forward, inverse, sem = refs
    gx, gy = lax.axis_index("gx"), lax.axis_index("gy")
    mine_x = gx if table_ref.shape[0] > 1 else 0
    mine_y = gy if forward_ref.shape[0] > 1 else 0
    lanes = table_ref.shape[5]
    copies = [
        pltpu.make_async_copy(forward_ref.at[mine_y], forward, sem.at[0]),
        pltpu.make_async_copy(inverse_ref.at[mine_y], inverse, sem.at[1]),
    ]
    for spot_x, number_x in enumerate(order_x):
        block_x = lax.bitwise_xor(gx, number_x)
        for spot_y in range(table_ref.shape[1]):
            block_y = lax.bitwise_xor(gy, order_y[spot_y]) if table_ref.shape[1] > 1 else 0
            columns = slice(spot_y * lanes, (spot_y + 1) * lanes)
            copies.append(
                pltpu.make_async_copy(
                    table_ref.at[mine_x, block_y, :, block_x],
                    table.at[:, spot_x, :, columns],
                    sem.at[len(copies)],
                )
            )
    for copy in copies:
        copy.start()
    for copy in copies:
        copy.wait()


def sine_cosine(angle):
    turns = jnp.floor(angle * (2.0 / math.pi) + 0.5)
    rest = angle - turns * 1.5703125
    rest = rest - turns * 4.8351287841796875e-4
    rest = rest - turns * 3.1385570764541626e-7
    square = rest * rest
    sine = rest + rest * square * (
        -1.6666654611e-1 + square * (8.3321608736e-3 - square * 1.9515295891e-4)
    )
    cosine = (
        1.0
        - 0.5 * square
        + square * square * (4.166664568298827e-2 + square * (-1.388731625493765e-3 + square * 2.443315711809948e-5))
    )
    quarter = turns.astype(jnp.int32)
    odd = (quarter & 1) == 1
    out_sine = jnp.where(odd, cosine, sine)
    out_cosine = jnp.where(odd, sine, cosine)
    out_sine = jnp.where((quarter & 2) == 2, -out_sine, out_sine)
    out_cosine = jnp.where(((quarter + 1) & 2) == 2, -out_cosine, out_cosine)
    return out_sine, out_cosine


def directions(theta, phi):
    lateral, axial = sine_cosine(theta)
    sine, cosine = sine_cosine(phi)
    return [lateral * cosine, lateral * sine, axial]


def looked_up(labels, region):
    result = jnp.zeros_like(labels) + region[0]
    for index in range(1, region.shape[0]):
        result = jnp.where(labels == float(index), region[index], result)
    return result


def pack_kernel(theta_ref, phi_ref, labels_ref, raw_ref, first_ref, last_ref, angle, label, sems):
    height = theta_ref.shape[1]
    copies = [
        pltpu.make_async_copy(theta_ref, angle.at[0], sems.at[0]),
        pltpu.make_async_copy(phi_ref, angle.at[1], sems.at[1]),
        pltpu.make_async_copy(labels_ref, label, sems.at[2]),
    ]
    for copy in copies:
        copy.start()
    for copy in copies:
        copy.wait()
    for index, value in enumerate((angle[0], angle[1], label[...].astype(jnp.float32))):
        raw_ref[index] = value
        put_edge(first_ref, index, value[:, 0])
        put_edge(last_ref, index, value[:, height - 1])


def meeting(devices):
    return [number for number in range(1, devices) if (number & (number + 1)) == 0]


def edge_spots(depth, width, lanes, start, field):
    pieces = width // lanes
    return [start + (field * pieces + piece) * depth for piece in range(pieces)]


def put_edge(ref, field, edge):
    lanes = ref.shape[1]
    for piece, row in enumerate(edge_spots(*edge.shape, lanes, 0, field)):
        ref[row : row + edge.shape[0]] = edge[:, piece * lanes : (piece + 1) * lanes]


def get_edge(ref, depth, width, start, field):
    spots = edge_spots(depth, width, ref.shape[1], start, field)
    return jnp.concatenate([ref[row : row + depth] for row in spots], 1)


def lines_kernel(count_x, order_y, *refs):
    raw_refs, operands = refs[:count_x], refs[count_x : count_x + 4]
    first_ref, last_ref, region_ref, table = operands
    gy = lax.axis_index("gy")
    out_refs, (region, sem) = refs[count_x + 4 : -2], refs[-2:]
    fetch = pltpu.make_async_copy(region_ref, region, sem)
    fetch.start()
    units = [directions(raw_ref[0], raw_ref[1]) for raw_ref in raw_refs]
    fetch.wait()
    total = None
    for number in range(count_x):
        saturation = looked_up(raw_refs[number][2], region)
        rows = saturation.shape[0] * saturation.shape[1]
        block = [(part * saturation).reshape(rows, -1) for part in units[number]]
        high, low = split_high(jnp.concatenate(block, 0))
        both = dot(jnp.concatenate([high, low], 0), table[0, number])
        part = both[: 3 * rows] + both[3 * rows :] + dot(high, table[1, number])
        total = part if total is None else total + part
    lanes = out_refs[0].shape[1]
    for spot, (number, out_ref) in enumerate(zip(order_y, out_refs)):
        out_ref[: 3 * rows] = total[:, spot * lanes : (spot + 1) * lanes]
        if number in meeting(len(order_y)):
            up = lax.bitwise_xor(gy, number) > gy
            out_ref[3 * rows :] = jnp.where(up, last_ref[...], first_ref[...])


def back_lines_kernel(numbers, count_y, *refs):
    in_refs, table, out_refs = refs[:count_y], refs[count_y], refs[count_y + 1 :]
    high, low = split_high(jnp.concatenate([ref[...] for ref in in_refs], 1))
    both = jnp.concatenate([high, low], 0)
    lines = high.shape[0]
    for number, out_ref in zip(numbers, out_refs):
        wide = dot(both, table[0, number], ((1,), (1,)))
        out_ref[...] = wide[:lines] + wide[lines:] + dot(high, table[1, number], ((1,), (1,)))


def tensor_kernel(kernel_ref, twice_ref, out_ref):
    twice = twice_ref[...]

    unroll = 8

    def step(index, carry):
        for offset in range(unroll):
            turned = dot(kernel_ref[index * unroll + offset], twice, ((0,), (0,)))
            out_ref[index * unroll + offset] = turned.astype(jnp.bfloat16)
        return carry

    lax.fori_loop(0, kernel_ref.shape[0] // unroll, step, 0)


def turn(value, sign):
    lanes = value.shape[-1]
    if lanes == 128:
        return pltpu.roll(value, lanes // 2, value.ndim - 1) * sign
    return jnp.concatenate([value[..., lanes // 2 :], value[..., : lanes // 2]], -1) * sign


def layers_forward(layer, sign):
    d0, d1, d2, d3 = layer
    r2 = turn(d2, sign)
    near, far = d1 + d3, d1 - d3
    far_turned = turn(far, sign)
    near_turned = turn(near, sign)
    even, odd = d0 + d2, d0 - d2
    out = [None] * 8
    out[0], out[4] = even + near, even - near
    out[2], out[6] = odd + far_turned, odd - far_turned
    plus, minus = d0 + r2, d0 - r2
    first = (far + near_turned) * root_half
    second = (near_turned - far) * root_half
    out[1], out[5] = plus + first, plus - first
    out[3], out[7] = minus + second, minus - second
    return out


def layers_inverse(wave, sign):
    a, b = wave[0] + wave[4], wave[0] - wave[4]
    e, f = wave[2] + wave[6], turn(wave[2] - wave[6], sign)
    p, q = wave[1] + wave[5], wave[1] - wave[5]
    s, t = wave[3] + wave[7], turn(wave[3] - wave[7], sign)
    o0, o1, o2, o3 = p + s, q - t, p - s, q + t
    return [
        a + e + o0,
        b - f + (o1 - turn(o1, sign)) * root_half,
        a - e - turn(o2, sign),
        b + f - (o3 + turn(o3, sign)) * root_half,
    ]


def apply_tensor(tensor, wave):
    out = [[], [], []]
    for level in range(8):
        xx, yy, zz, xy, xz, yz = [tensor[part][level] for part in range(6)]
        x, y, z = wave[0][level], wave[1][level], wave[2][level]
        out[0].append(xx * x + xy * y + xz * z)
        out[1].append(xy * x + yy * y + yz * z)
        out[2].append(xz * x + yz * y + zz * z)
    return out


def waves_kernel(scale, count_y, *refs):
    spec_refs, (tensor_ref, forward_ref, inverse_ref) = refs[:count_y], refs[count_y : count_y + 3]
    out_refs, (wave_ref, back_ref) = refs[count_y + 3 : -2], refs[-2:]
    lines, lanes = out_refs[0].shape
    local = 8
    planes = lines // local
    height = count_y * local
    sign = jnp.where(
        lax.broadcasted_iota(jnp.int32, (1, lanes), 1) < lanes // 2, 1.0, -1.0
    ).astype(jnp.float32)
    columns = []
    for plane in range(planes):
        value = jnp.concatenate(
            [spec_ref[plane * local : (plane + 1) * local] for spec_ref in spec_refs], 0
        )
        value = jnp.concatenate([value, turn(value, sign)], 0)
        high, low = split_high(value)
        columns.append(jnp.concatenate([high, low, high], 0))
    wave_ref[...] = dot(forward_ref[...], jnp.concatenate(columns, 1))

    chunk = 16
    depth = planes // 3
    double = 2 * height

    def step(index, carry):
        rows = pl.ds(pl.multiple_of(index * chunk, chunk), chunk)
        wave = []
        for part in range(3):
            layer = [
                wave_ref[rows, (part * depth + z) * lanes : (part * depth + z + 1) * lanes]
                for z in range(depth)
            ]
            wave.append(layers_forward(layer, sign))
        tensor = [
            [tensor_ref[part * 8 + level, rows, :].astype(jnp.float32) for level in range(8)]
            for part in range(6)
        ]
        image = apply_tensor(tensor, wave)
        for part in range(3):
            layer = layers_inverse(image[part], sign)
            for z in range(depth):
                spot = slice((part * depth + z) * lanes, (part * depth + z + 1) * lanes)
                high, low = split_high(layer[z] * scale)
                back_ref[rows, spot] = high
                back_ref[pl.ds(pl.multiple_of(double + index * chunk, chunk), chunk), spot] = low
                back_ref[pl.ds(pl.multiple_of(2 * double + index * chunk, chunk), chunk), spot] = high
        return carry

    lax.fori_loop(0, double // chunk, step, 0, unroll=True)
    back = dot(inverse_ref[...], back_ref[...])
    for plane in range(planes):
        part = slice(plane * lanes, (plane + 1) * lanes)
        value = back[:height, part] - turn(back[height:, part], sign)
        for number in range(count_y):
            out_refs[number][plane * local : (plane + 1) * local] = value[
                number * local : (number + 1) * local
            ]


def exchange_kernel(order_x, count_y, *refs):
    count_x, numbers = len(order_x), meeting(count_y)
    raw_refs, edge_refs, (ms_ref, aex_ref) = refs[:count_x], refs[count_x:-5], refs[-5:-3]
    exchange_ref, unit_ref, raw_ref = refs[-3:]
    depth, height, width = raw_ref.shape[2:]
    gx, gy = lax.axis_index("gx"), lax.axis_index("gy")

    def row_beside(field, other):
        value = None
        for number, edge_ref in zip(numbers, edge_refs):
            edge = get_edge(edge_ref, depth, width, 3 * depth * height, field)
            match = lax.bitwise_xor(gy, number) == other
            value = edge if value is None else jnp.where(match, edge, value)
        return value[:, None, :]

    for spot, number in enumerate(order_x):
        raw_ref[lax.bitwise_xor(gx, number)] = raw_refs[spot][...]
    left, right = jnp.maximum(gx - 1, 0), jnp.minimum(gx + 1, count_x - 1)
    shape = (depth, height, width)
    lane = lax.broadcasted_iota(jnp.int32, shape, 2)
    row = lax.broadcasted_iota(jnp.int32, shape, 1)

    def quantities(values):
        return directions(values[0], values[1]) + [looked_up(values[2], aex_ref)]

    raw = [raw_refs[0][f] for f in range(3)]
    here = quantities(raw)
    side = quantities([jnp.where(lane == 0, raw_ref[right, f], raw_ref[left, f]) for f in range(3)])
    above = quantities(
        [jnp.where(row == 0, row_beside(f, gy + 1), row_beside(f, gy - 1)) for f in range(3)]
    )
    saturation = looked_up(raw[2], ms_ref)
    total = [jnp.zeros(shape, jnp.float32) for _ in range(3)]

    def add(total, beside, weight):
        coupling = 2.0 * here[3] * beside[3] / (here[3] + beside[3]) * weight
        return [total[c] + coupling * (beside[c] - here[c]) for c in range(3)]

    one = jnp.float32(1.0)
    zero = jnp.float32(0.0)
    for shift, edge, there in ((1, 0, gx > 0), (width - 1, width - 1, gx < count_x - 1)):
        beside = [
            jnp.where(lane == edge, pltpu.roll(s, shift, 2), pltpu.roll(h, shift, 2))
            for s, h in zip(side, here)
        ]
        weight = jnp.where(lane == edge, jnp.where(there, one, zero), one) * side_weight
        total = add(total, beside, weight)
    for shift, edge, there in ((1, 0, gy > 0), (height - 1, height - 1, gy < count_y - 1)):
        beside = [
            jnp.where(row == edge, pltpu.roll(s, shift, 1), pltpu.roll(h, shift, 1))
            for s, h in zip(above, here)
        ]
        weight = jnp.where(row == edge, jnp.where(there, one, zero), one) * side_weight
        total = add(total, beside, weight)
    for part in range(3):
        unit_ref[part] = here[part]
    for z in range(depth):
        out = [total[c][z] for c in range(3)]
        for other in (z - 1, z + 1):
            if 0 <= other < depth:
                a, b = here[3][z], here[3][other]
                coupling = 2.0 * a * b / (a + b) * layer_weight
                out = [out[c] + coupling * (here[c][other] - here[c][z]) for c in range(3)]
        for c in range(3):
            exchange_ref[c, z] = out[c] / saturation[z]


def cross(first, second):
    return [
        first[1] * second[2] - first[2] * second[1],
        first[2] * second[0] - first[0] * second[2],
        first[0] * second[1] - first[1] * second[0],
    ]


def final_kernel(count_x, *refs):
    part_refs, (exchange_ref, unit_ref, field_ref, predicted_ref) = refs[:count_x], refs[count_x:]
    depth, height, width = unit_ref.shape[1:]
    rows = depth * height
    unit, field = [], []
    for c in range(3):
        place = slice(c * rows, (c + 1) * rows)
        total = part_refs[0][place]
        for part_ref in part_refs[1:]:
            total = total + part_ref[place]
        field.append(exchange_ref[c] + total.reshape(depth, height, width))
        unit.append(unit_ref[c])
        field_ref[c] = field[c]
    twist = cross(unit, field)
    second = cross(unit, twist)
    moved = [
        unit[c] - (time_step / (1.0 + damping * damping)) * (twist[c] + damping * second[c])
        for c in range(3)
    ]
    length = jnp.sqrt(moved[0] * moved[0] + moved[1] * moved[1] + moved[2] * moved[2])
    for c in range(3):
        predicted_ref[c] = moved[c] / length


vmem = pl.BlockSpec(memory_space=pltpu.VMEM)
smem = pl.BlockSpec(memory_space=pltpu.SMEM)
hbm = pl.BlockSpec(memory_space=pltpu.HBM)


def call(body, out, ins, operands, scratch=(), flops=0, name=None, grant=16 << 20):
    operands = [
        pltpu.with_memory_space_constraint(o, pltpu.HBM) if i is hbm else o
        for i, o in zip(ins, operands)
    ]
    size = sum(math.prod(o.shape) * o.dtype.itemsize for o in operands)
    outs = out if isinstance(out, (list, tuple)) else [out]
    size += sum(math.prod(o.shape) * jnp.dtype(o.dtype).itemsize for o in outs)
    return pl.pallas_call(
        body,
        out_shape=out,
        in_specs=ins,
        out_specs=[vmem] * len(outs) if outs is out else vmem,
        scratch_shapes=list(scratch),
        compiler_params=pltpu.CompilerParams(vmem_limit_bytes=grant),
        cost_estimate=pl.CostEstimate(flops=flops, bytes_accessed=size, transcendentals=0),
        name=name,
    )(*operands)


def f32(*shape):
    return jax.ShapeDtypeStruct(shape, jnp.float32)


def swapped(chunk, axis, number):
    devices = lax.axis_size(axis)
    return lax.ppermute(chunk, axis, [(i, i ^ number) for i in range(devices)])


def exchanged(chunks, axis, order):
    return [swapped(c, axis, n) if n else c for c, n in zip(chunks, order)]


def held(value):
    return pltpu.with_memory_space_constraint(value, pltpu.VMEM)


def after(value, other):
    return lax.optimization_barrier((value, other))[0]


def spread(block, axis, first):
    blocks = {0: block}
    bit = lax.axis_size(axis) // 2
    while bit:
        for number in list(blocks):
            blocks[number ^ bit] = swapped(blocks[number], axis, bit)
        if first is not None:
            blocks[bit], first = lax.optimization_barrier((blocks[bit], first))
            ready, first = first, None
        bit //= 2
    return [blocks[number] for number in range(lax.axis_size(axis))], ready


def gathered_sums(blocks, axis):
    blocks = {number: [block] for number, block in enumerate(blocks)}
    bit = 1
    while bit < lax.axis_size(axis):
        for number in sorted(blocks, reverse=True):
            if number & bit:
                block = functools.reduce(jnp.add, blocks.pop(number))
                blocks[number ^ bit].append(swapped(block, axis, bit))
        bit *= 2
    return blocks[0], block


def per_device(theta, phi, labels, ms_region, aex_region, kernel):
    count_x, count_y = lax.axis_size("gx"), lax.axis_size("gy")
    gx, gy = lax.axis_index("gx"), lax.axis_index("gy")
    depth, height, width = theta.shape
    rows = kernel.shape[2]
    lanes = 2 * rows
    lines = 3 * depth * height
    whole_y = count_y * height

    cells = f32(3, depth, height, width)
    order_x, order_y = list(range(count_x)), list(range(count_y - 1, -1, -1))
    table = line_table(count_x, count_y, width, rows)
    if table is None:
        table = line_table_here(count_x, width, rows, order_y)
        columns_tables = column_tables_here(count_y, height, order_y)
    else:
        columns_tables = column_tables(count_y, height, order_y)
    sources = [jnp.asarray(t) for t in (table, *columns_tables)]
    twice = np.concatenate([np.eye(rows), np.eye(rows)], 1).astype(ml_dtypes.bfloat16)
    transform_flops = 6 * lines * count_x * width * count_y * lanes

    edge_rows = 3 * depth * width // lanes
    edge = f32(edge_rows, lanes)
    packed, first, last = call(
        pack_kernel,
        [cells, edge, edge],
        [hbm] * 3,
        (theta, phi, labels),
        scratch=(
            pltpu.VMEM((2, depth, height, width), jnp.float32),
            pltpu.VMEM((depth, height, width), jnp.int32),
            pltpu.SemaphoreType.DMA((3,)),
        ),
        name="pack",
    )
    table, forward, inverse = call(
        functools.partial(load_kernel, order_x, order_y),
        [
            pltpu.VMEM((2, count_x, width, count_y * lanes), jnp.bfloat16),
            pltpu.VMEM(sources[1].shape[1:], jnp.bfloat16),
            pltpu.VMEM(sources[2].shape[1:], jnp.bfloat16),
        ],
        [hbm] * 3,
        tuple(sources),
        scratch=(pltpu.SemaphoreType.DMA((2 + count_x * count_y,)),),
        name="load",
    )

    gathered, table = spread(packed, "gx", table)
    tensor = call(
        tensor_kernel,
        jax.ShapeDtypeStruct((48, 2 * whole_y, lanes), jnp.bfloat16),
        [vmem, vmem],
        (kernel.reshape(48, rows, 2 * whole_y), jnp.asarray(twice)),
        flops=48 * 2 * rows * lanes * 2 * whole_y,
        name="tensor",
    )
    spectrum = call(
        functools.partial(lines_kernel, count_x, order_y),
        [f32(lines + (edge_rows if n in meeting(count_y) else 0), lanes) for n in order_y],
        [vmem] * (count_x + 2) + [hbm, vmem],
        (*gathered, first, last, ms_region, held(table)),
        scratch=(pltpu.SMEM(ms_region.shape, jnp.float32), pltpu.SemaphoreType.DMA),
        flops=transform_flops,
        name="lines",
    )
    columns = lax.optimization_barrier(exchanged(spectrum, "gy", order_y))
    scale = -1.0 / (2 * depth * 2 * whole_y * 2 * count_x * width)
    waves = call(
        functools.partial(waves_kernel, scale, count_y),
        [f32(lines, lanes)] * count_y,
        [vmem] * (count_y + 3),
        (*columns, tensor, forward, inverse),
        scratch=(
            pltpu.VMEM((2 * whole_y, 3 * depth * lanes), jnp.float32),
            pltpu.VMEM((6 * whole_y, 3 * depth * lanes), jnp.bfloat16),
        ),
        flops=20 * whole_y * whole_y * 3 * depth * lanes,
        name="waves",
    )
    returned = exchanged(waves, "gy", order_y)
    across = [number for number in range(count_x) if number % 2]
    within = [number for number in range(count_x) if not number % 2]
    partial = [None] * count_x
    for numbers, name in ((across, "back_across"), (within, "back_within")):
        blocks = call(
            functools.partial(back_lines_kernel, numbers, count_y),
            [f32(lines, width)] * len(numbers),
            [vmem] * (count_y + 1),
            (*returned, held(table)),
            flops=transform_flops // 2,
            name=name,
        )
        for number, block in zip(numbers, blocks):
            partial[number] = block
    parts, far_sum = gathered_sums(partial, "gx")
    edges = [columns[order_y.index(number)] for number in meeting(count_y)]
    edges, far_sum = lax.optimization_barrier((edges, far_sum))
    exchange, unit = call(
        functools.partial(exchange_kernel, order_x, count_y),
        [cells, cells],
        [vmem] * (count_x + len(edges)) + [smem] * 2,
        (*gathered, *edges, ms_region, aex_region),
        scratch=(pltpu.VMEM((count_x, 3, depth, height, width), jnp.float32),),
        flops=300 * depth * height * width,
        name="exchange",
    )
    field, predicted = call(
        functools.partial(final_kernel, len(parts)),
        [cells, cells],
        [vmem] * (len(parts) + 2),
        (*parts, exchange, unit),
        flops=60 * depth * height * width,
        name="predict",
    )
    return field, predicted


def solution(mesh):
    in_specs = (
        P(None, "gy", "gx"),
        P(None, "gy", "gx"),
        P(None, "gy", "gx"),
        P(),
        P(),
        P(None, None, ("gx", "gy"), None),
    )
    out_specs = (P(None, None, "gy", "gx"), P(None, None, "gy", "gx"))
    return jax.shard_map(
        per_device, mesh=mesh, in_specs=in_specs, out_specs=out_specs, check_vma=False
    )
```

```python
import functools
import math

import jax
import jax.numpy as jnp
import ml_dtypes
import numpy as np
from jax import lax
from jax.experimental import pallas as pl
from jax.experimental.pallas import tpu as pltpu
from jax.sharding import PartitionSpec as P

damping = 0.5
time_step = 0.2
side_weight = 0.25
layer_weight = 0.5
root_half = math.sqrt(0.5)
constant_limit = 20 << 20


def split_high(value):
    high = value.astype(jnp.bfloat16)
    low = (value - high.astype(jnp.float32)).astype(jnp.bfloat16)
    return high, low


def split_table(table):
    high = table.astype(np.float32).astype(ml_dtypes.bfloat16)
    low = (table - high.astype(np.float64)).astype(np.float32).astype(ml_dtypes.bfloat16)
    return high, low


def dot(left, right, contract=((1,), (0,))):
    return lax.dot_general(left, right, (contract, ((), ())), preferred_element_type=jnp.float32)


def line_table(count_x, count_y, width, rows):
    cells = count_x * width
    if count_x * 2 * cells * count_y * 2 * rows * 2 > constant_limit:
        return None
    place = np.arange(cells)[None, None, :, None]
    wave = (
        np.arange(count_x)[:, None, None, None] * (count_y * rows)
        + np.arange(count_y)[None, :, None, None] * rows
        + np.arange(rows)[None, None, None, :]
    )
    angle = (place * wave % (2 * cells)) * (2.0 * math.pi / (2 * cells))
    table = np.concatenate([np.cos(angle), -np.sin(angle)], 3)
    table = table.reshape(count_x, count_y, count_x, width, 2 * rows)
    high, low = split_table(table)
    return np.stack([high, low], 2)


def line_table_here(count_x, width, rows, order):
    cells = count_x * width
    count_y = len(order)
    place = jnp.arange(cells, dtype=jnp.int32)[:, None, None]
    block = lax.bitwise_xor(lax.axis_index("gy"), jnp.array(order, jnp.int32))
    wave = (
        lax.axis_index("gx") * (count_y * rows)
        + block[None, :, None] * rows
        + jnp.arange(rows, dtype=jnp.int32)[None, None, :]
    )
    angle = (place * wave % (2 * cells)).astype(jnp.float32) * (math.pi / cells)
    table = jnp.concatenate([jnp.cos(angle), -jnp.sin(angle)], 2)
    table = table.reshape(1, 1, count_x, width, count_y * 2 * rows)
    return jnp.stack(split_high(table), 2)


def column_tables(count_y, local, order):
    height = count_y * local
    wave = np.arange(2 * height)
    block = np.arange(count_y)[:, None] ^ np.array(order)[None, :]
    place = (block[:, :, None] * local + np.arange(local)).reshape(count_y, height)
    angle = (wave[None, :, None] * place[:, None, :] % (2 * height)) * (math.pi / height)
    high, low = split_table(np.concatenate([np.cos(angle), np.sin(angle)], 2))
    forward = np.concatenate([high, high, low], 2)
    angle = angle.transpose(0, 2, 1)
    high, low = split_table(np.concatenate([np.cos(angle), np.sin(angle)], 1))
    inverse = np.concatenate([high, high, low], 2)
    return forward, inverse


def column_tables_here(count_y, local, order):
    height = count_y * local
    wave = jnp.arange(2 * height, dtype=jnp.int32)
    block = lax.bitwise_xor(lax.axis_index("gy"), jnp.array(order, jnp.int32))
    place = (block[:, None] * local + jnp.arange(local, dtype=jnp.int32)).reshape(height)
    angle = (wave[:, None] * place % (2 * height)).astype(jnp.float32) * (math.pi / height)
    high, low = split_high(jnp.concatenate([jnp.cos(angle), jnp.sin(angle)], 1))
    forward = jnp.concatenate([high, high, low], 1)
    high, low = split_high(jnp.concatenate([jnp.cos(angle.T), jnp.sin(angle.T)], 0))
    inverse = jnp.concatenate([high, high, low], 1)
    return forward[None], inverse[None]


def load_kernel(order_x, order_y, *refs):
    table_ref, forward_ref, inverse_ref, table, forward, inverse, sem = refs
    gx, gy = lax.axis_index("gx"), lax.axis_index("gy")
    mine_x = gx if table_ref.shape[0] > 1 else 0
    mine_y = gy if forward_ref.shape[0] > 1 else 0
    lanes = table_ref.shape[5]
    copies = [
        pltpu.make_async_copy(forward_ref.at[mine_y], forward, sem.at[0]),
        pltpu.make_async_copy(inverse_ref.at[mine_y], inverse, sem.at[1]),
    ]
    for spot_x, number_x in enumerate(order_x):
        block_x = lax.bitwise_xor(gx, number_x)
        for spot_y in range(table_ref.shape[1]):
            block_y = lax.bitwise_xor(gy, order_y[spot_y]) if table_ref.shape[1] > 1 else 0
            columns = slice(spot_y * lanes, (spot_y + 1) * lanes)
            copies.append(
                pltpu.make_async_copy(
                    table_ref.at[mine_x, block_y, :, block_x],
                    table.at[:, spot_x, :, columns],
                    sem.at[len(copies)],
                )
            )
    for copy in copies:
        copy.start()
    for copy in copies:
        copy.wait()


def sine_cosine(angle):
    turns = jnp.floor(angle * (2.0 / math.pi) + 0.5)
    rest = angle - turns * 1.5703125
    rest = rest - turns * 4.8351287841796875e-4
    rest = rest - turns * 3.1385570764541626e-7
    square = rest * rest
    sine = rest + rest * square * (
        -1.6666654611e-1 + square * (8.3321608736e-3 - square * 1.9515295891e-4)
    )
    cosine = (
        1.0
        - 0.5 * square
        + square * square * (4.166664568298827e-2 + square * (-1.388731625493765e-3 + square * 2.443315711809948e-5))
    )
    quarter = turns.astype(jnp.int32)
    odd = (quarter & 1) == 1
    out_sine = jnp.where(odd, cosine, sine)
    out_cosine = jnp.where(odd, sine, cosine)
    out_sine = jnp.where((quarter & 2) == 2, -out_sine, out_sine)
    out_cosine = jnp.where(((quarter + 1) & 2) == 2, -out_cosine, out_cosine)
    return out_sine, out_cosine


def directions(theta, phi):
    lateral, axial = sine_cosine(theta)
    sine, cosine = sine_cosine(phi)
    return [lateral * cosine, lateral * sine, axial]


def looked_up(labels, region):
    result = jnp.zeros_like(labels) + region[0]
    for index in range(1, region.shape[0]):
        result = jnp.where(labels == float(index), region[index], result)
    return result


def pack_kernel(theta_ref, phi_ref, labels_ref, raw_ref, first_ref, last_ref, angle, label, sems):
    height = theta_ref.shape[1]
    copies = [
        pltpu.make_async_copy(theta_ref, angle.at[0], sems.at[0]),
        pltpu.make_async_copy(phi_ref, angle.at[1], sems.at[1]),
        pltpu.make_async_copy(labels_ref, label, sems.at[2]),
    ]
    for copy in copies:
        copy.start()
    for copy in copies:
        copy.wait()
    for index, value in enumerate((angle[0], angle[1], label[...].astype(jnp.float32))):
        raw_ref[index] = value
        put_edge(first_ref, index, value[:, 0])
        put_edge(last_ref, index, value[:, height - 1])


def meeting(devices):
    return [number for number in range(1, devices) if (number & (number + 1)) == 0]


def edge_spots(depth, width, lanes, start, field):
    pieces = width // lanes
    return [start + (field * pieces + piece) * depth for piece in range(pieces)]


def put_edge(ref, field, edge):
    lanes = ref.shape[1]
    for piece, row in enumerate(edge_spots(*edge.shape, lanes, 0, field)):
        ref[row : row + edge.shape[0]] = edge[:, piece * lanes : (piece + 1) * lanes]


def get_edge(ref, depth, width, start, field):
    spots = edge_spots(depth, width, ref.shape[1], start, field)
    return jnp.concatenate([ref[row : row + depth] for row in spots], 1)


def lines_of(raw_refs, numbers, region_ref, region, sem, table):
    fetch = pltpu.make_async_copy(region_ref, region, sem)
    fetch.start()
    units = [directions(raw_ref[0], raw_ref[1]) for raw_ref in raw_refs]
    fetch.wait()
    total = None
    for raw_ref, unit, number in zip(raw_refs, units, numbers):
        saturation = looked_up(raw_ref[2], region)
        rows = saturation.shape[0] * saturation.shape[1]
        block = [(part * saturation).reshape(rows, -1) for part in unit]
        high, low = split_high(jnp.concatenate(block, 0))
        both = dot(jnp.concatenate([high, low], 0), table[0, number])
        part = both[: 3 * rows] + both[3 * rows :] + dot(high, table[1, number])
        total = part if total is None else total + part
    return total


def early_lines_kernel(numbers, *refs):
    raw_refs, (region_ref, table, out_ref, region, sem) = refs[: len(numbers)], refs[len(numbers) :]
    out_ref[...] = lines_of(raw_refs, numbers, region_ref, region, sem, table)


def lines_kernel(numbers, order_y, *refs):
    raw_refs, operands = refs[: len(numbers)], refs[len(numbers) : len(numbers) + 5]
    early_ref, first_ref, last_ref, region_ref, table = operands
    gy = lax.axis_index("gy")
    out_refs, (region, sem) = refs[len(numbers) + 5 : -2], refs[-2:]
    total = lines_of(raw_refs, numbers, region_ref, region, sem, table) + early_ref[...]
    lines, lanes = total.shape[0], first_ref.shape[1]
    for spot, (number, out_ref) in enumerate(zip(order_y, out_refs)):
        out_ref[:lines] = total[:, spot * lanes : (spot + 1) * lanes]
        if number in meeting(len(order_y)):
            up = lax.bitwise_xor(gy, number) > gy
            out_ref[lines:] = jnp.where(up, last_ref[...], first_ref[...])


def back_lines_kernel(numbers, count_y, *refs):
    in_refs, table, out_refs = refs[:count_y], refs[count_y], refs[count_y + 1 :]
    high, low = split_high(jnp.concatenate([ref[...] for ref in in_refs], 1))
    both = jnp.concatenate([high, low], 0)
    lines = high.shape[0]
    for number, out_ref in zip(numbers, out_refs):
        wide = dot(both, table[0, number], ((1,), (1,)))
        out_ref[...] = wide[:lines] + wide[lines:] + dot(high, table[1, number], ((1,), (1,)))


def tensor_kernel(kernel_ref, twice_ref, out_ref):
    twice = twice_ref[...]

    unroll = 8

    def step(index, carry):
        for offset in range(unroll):
            turned = dot(kernel_ref[index * unroll + offset], twice, ((0,), (0,)))
            out_ref[index * unroll + offset] = turned.astype(jnp.bfloat16)
        return carry

    lax.fori_loop(0, kernel_ref.shape[0] // unroll, step, 0)


def turn(value, sign):
    lanes = value.shape[-1]
    if lanes == 128:
        return pltpu.roll(value, lanes // 2, value.ndim - 1) * sign
    return jnp.concatenate([value[..., lanes // 2 :], value[..., : lanes // 2]], -1) * sign


def layers_forward(layer, sign):
    d0, d1, d2, d3 = layer
    r2 = turn(d2, sign)
    near, far = d1 + d3, d1 - d3
    far_turned = turn(far, sign)
    near_turned = turn(near, sign)
    even, odd = d0 + d2, d0 - d2
    out = [None] * 8
    out[0], out[4] = even + near, even - near
    out[2], out[6] = odd + far_turned, odd - far_turned
    plus, minus = d0 + r2, d0 - r2
    first = (far + near_turned) * root_half
    second = (near_turned - far) * root_half
    out[1], out[5] = plus + first, plus - first
    out[3], out[7] = minus + second, minus - second
    return out


def layers_inverse(wave, sign):
    a, b = wave[0] + wave[4], wave[0] - wave[4]
    e, f = wave[2] + wave[6], turn(wave[2] - wave[6], sign)
    p, q = wave[1] + wave[5], wave[1] - wave[5]
    s, t = wave[3] + wave[7], turn(wave[3] - wave[7], sign)
    o0, o1, o2, o3 = p + s, q - t, p - s, q + t
    return [
        a + e + o0,
        b - f + (o1 - turn(o1, sign)) * root_half,
        a - e - turn(o2, sign),
        b + f - (o3 + turn(o3, sign)) * root_half,
    ]


def apply_tensor(tensor, wave):
    out = [[], [], []]
    for level in range(8):
        xx, yy, zz, xy, xz, yz = [tensor[part][level] for part in range(6)]
        x, y, z = wave[0][level], wave[1][level], wave[2][level]
        out[0].append(xx * x + xy * y + xz * z)
        out[1].append(xy * x + yy * y + yz * z)
        out[2].append(xz * x + yz * y + zz * z)
    return out


def waves_kernel(scale, count_y, *refs):
    spec_refs, (tensor_ref, forward_ref, inverse_ref) = refs[:count_y], refs[count_y : count_y + 3]
    out_refs, (wave_ref, back_ref) = refs[count_y + 3 : -2], refs[-2:]
    lines, lanes = out_refs[0].shape
    local = 8
    planes = lines // local
    height = count_y * local
    sign = jnp.where(
        lax.broadcasted_iota(jnp.int32, (1, lanes), 1) < lanes // 2, 1.0, -1.0
    ).astype(jnp.float32)
    columns = []
    for plane in range(planes):
        value = jnp.concatenate(
            [spec_ref[plane * local : (plane + 1) * local] for spec_ref in spec_refs], 0
        )
        value = jnp.concatenate([value, turn(value, sign)], 0)
        high, low = split_high(value)
        columns.append(jnp.concatenate([high, low, high], 0))
    wave_ref[...] = dot(forward_ref[...], jnp.concatenate(columns, 1))

    chunk = 16
    depth = planes // 3
    double = 2 * height

    def step(index, carry):
        rows = pl.ds(pl.multiple_of(index * chunk, chunk), chunk)
        wave = []
        for part in range(3):
            layer = [
                wave_ref[rows, (part * depth + z) * lanes : (part * depth + z + 1) * lanes]
                for z in range(depth)
            ]
            wave.append(layers_forward(layer, sign))
        tensor = [
            [tensor_ref[part * 8 + level, rows, :].astype(jnp.float32) for level in range(8)]
            for part in range(6)
        ]
        image = apply_tensor(tensor, wave)
        for part in range(3):
            layer = layers_inverse(image[part], sign)
            for z in range(depth):
                spot = slice((part * depth + z) * lanes, (part * depth + z + 1) * lanes)
                high, low = split_high(layer[z] * scale)
                back_ref[rows, spot] = high
                back_ref[pl.ds(pl.multiple_of(double + index * chunk, chunk), chunk), spot] = low
                back_ref[pl.ds(pl.multiple_of(2 * double + index * chunk, chunk), chunk), spot] = high
        return carry

    lax.fori_loop(0, double // chunk, step, 0, unroll=True)
    back = dot(inverse_ref[...], back_ref[...])
    for plane in range(planes):
        part = slice(plane * lanes, (plane + 1) * lanes)
        value = back[:height, part] - turn(back[height:, part], sign)
        for number in range(count_y):
            out_refs[number][plane * local : (plane + 1) * local] = value[
                number * local : (number + 1) * local
            ]


def exchange_kernel(order_x, count_y, *refs):
    count_x, numbers = len(order_x), meeting(count_y)
    raw_refs, edge_refs, (ms_ref, aex_ref) = refs[:count_x], refs[count_x:-5], refs[-5:-3]
    exchange_ref, unit_ref, raw_ref = refs[-3:]
    depth, height, width = raw_ref.shape[2:]
    gx, gy = lax.axis_index("gx"), lax.axis_index("gy")

    def row_beside(field, other):
        value = None
        for number, edge_ref in zip(numbers, edge_refs):
            edge = get_edge(edge_ref, depth, width, 3 * depth * height, field)
            match = lax.bitwise_xor(gy, number) == other
            value = edge if value is None else jnp.where(match, edge, value)
        return value[:, None, :]

    for spot, number in enumerate(order_x):
        raw_ref[lax.bitwise_xor(gx, number)] = raw_refs[spot][...]
    left, right = jnp.maximum(gx - 1, 0), jnp.minimum(gx + 1, count_x - 1)
    shape = (depth, height, width)
    lane = lax.broadcasted_iota(jnp.int32, shape, 2)
    row = lax.broadcasted_iota(jnp.int32, shape, 1)

    def quantities(values):
        return directions(values[0], values[1]) + [looked_up(values[2], aex_ref)]

    raw = [raw_refs[0][f] for f in range(3)]
    here = quantities(raw)
    side = quantities([jnp.where(lane == 0, raw_ref[right, f], raw_ref[left, f]) for f in range(3)])
    above = quantities(
        [jnp.where(row == 0, row_beside(f, gy + 1), row_beside(f, gy - 1)) for f in range(3)]
    )
    saturation = looked_up(raw[2], ms_ref)
    total = [jnp.zeros(shape, jnp.float32) for _ in range(3)]

    def add(total, beside, weight):
        coupling = 2.0 * here[3] * beside[3] / (here[3] + beside[3]) * weight
        return [total[c] + coupling * (beside[c] - here[c]) for c in range(3)]

    one = jnp.float32(1.0)
    zero = jnp.float32(0.0)
    for shift, edge, there in ((1, 0, gx > 0), (width - 1, width - 1, gx < count_x - 1)):
        beside = [
            jnp.where(lane == edge, pltpu.roll(s, shift, 2), pltpu.roll(h, shift, 2))
            for s, h in zip(side, here)
        ]
        weight = jnp.where(lane == edge, jnp.where(there, one, zero), one) * side_weight
        total = add(total, beside, weight)
    for shift, edge, there in ((1, 0, gy > 0), (height - 1, height - 1, gy < count_y - 1)):
        beside = [
            jnp.where(row == edge, pltpu.roll(s, shift, 1), pltpu.roll(h, shift, 1))
            for s, h in zip(above, here)
        ]
        weight = jnp.where(row == edge, jnp.where(there, one, zero), one) * side_weight
        total = add(total, beside, weight)
    for part in range(3):
        unit_ref[part] = here[part]
    for z in range(depth):
        out = [total[c][z] for c in range(3)]
        for other in (z - 1, z + 1):
            if 0 <= other < depth:
                a, b = here[3][z], here[3][other]
                coupling = 2.0 * a * b / (a + b) * layer_weight
                out = [out[c] + coupling * (here[c][other] - here[c][z]) for c in range(3)]
        for c in range(3):
            exchange_ref[c, z] = out[c] / saturation[z]


def cross(first, second):
    return [
        first[1] * second[2] - first[2] * second[1],
        first[2] * second[0] - first[0] * second[2],
        first[0] * second[1] - first[1] * second[0],
    ]


def final_kernel(count_x, *refs):
    part_refs, (exchange_ref, unit_ref, field_ref, predicted_ref) = refs[:count_x], refs[count_x:]
    depth, height, width = unit_ref.shape[1:]
    rows = depth * height
    unit, field = [], []
    for c in range(3):
        place = slice(c * rows, (c + 1) * rows)
        total = part_refs[0][place]
        for part_ref in part_refs[1:]:
            total = total + part_ref[place]
        field.append(exchange_ref[c] + total.reshape(depth, height, width))
        unit.append(unit_ref[c])
        field_ref[c] = field[c]
    twist = cross(unit, field)
    second = cross(unit, twist)
    moved = [
        unit[c] - (time_step / (1.0 + damping * damping)) * (twist[c] + damping * second[c])
        for c in range(3)
    ]
    length = jnp.sqrt(moved[0] * moved[0] + moved[1] * moved[1] + moved[2] * moved[2])
    for c in range(3):
        predicted_ref[c] = moved[c] / length


vmem = pl.BlockSpec(memory_space=pltpu.VMEM)
smem = pl.BlockSpec(memory_space=pltpu.SMEM)
hbm = pl.BlockSpec(memory_space=pltpu.HBM)


def call(body, out, ins, operands, scratch=(), flops=0, name=None, grant=16 << 20):
    operands = [
        pltpu.with_memory_space_constraint(o, pltpu.HBM) if i is hbm else o
        for i, o in zip(ins, operands)
    ]
    size = sum(math.prod(o.shape) * o.dtype.itemsize for o in operands)
    outs = out if isinstance(out, (list, tuple)) else [out]
    size += sum(math.prod(o.shape) * jnp.dtype(o.dtype).itemsize for o in outs)
    return pl.pallas_call(
        body,
        out_shape=out,
        in_specs=ins,
        out_specs=[vmem] * len(outs) if outs is out else vmem,
        scratch_shapes=list(scratch),
        compiler_params=pltpu.CompilerParams(vmem_limit_bytes=grant),
        cost_estimate=pl.CostEstimate(flops=flops, bytes_accessed=size, transcendentals=0),
        name=name,
    )(*operands)


def f32(*shape):
    return jax.ShapeDtypeStruct(shape, jnp.float32)


def swapped(chunk, axis, number):
    devices = lax.axis_size(axis)
    return lax.ppermute(chunk, axis, [(i, i ^ number) for i in range(devices)])


def exchanged(chunks, axis, order):
    return [swapped(c, axis, n) if n else c for c, n in zip(chunks, order)]


def held(value):
    return pltpu.with_memory_space_constraint(value, pltpu.VMEM)


def after(value, other):
    return lax.optimization_barrier((value, other))[0]


def spread(block, axis, first):
    blocks = {0: block}
    bit = lax.axis_size(axis) // 2
    while bit:
        for number in list(blocks):
            blocks[number ^ bit] = swapped(blocks[number], axis, bit)
        if first is not None:
            blocks[bit], first = lax.optimization_barrier((blocks[bit], first))
            ready, first = first, None
        bit //= 2
    return [blocks[number] for number in range(lax.axis_size(axis))], ready


def far_sums(blocks, axis):
    blocks = {number: [block] for number, block in blocks.items()}
    terms, bit, block = [], 1, None
    while bit < lax.axis_size(axis):
        for number in sorted(blocks, reverse=True):
            if number & bit:
                block = functools.reduce(jnp.add, blocks.pop(number))
                blocks.get(number ^ bit, terms).append(swapped(block, axis, bit))
        bit *= 2
    return terms, block


def per_device(theta, phi, labels, ms_region, aex_region, kernel):
    count_x, count_y = lax.axis_size("gx"), lax.axis_size("gy")
    gx, gy = lax.axis_index("gx"), lax.axis_index("gy")
    depth, height, width = theta.shape
    rows = kernel.shape[2]
    lanes = 2 * rows
    lines = 3 * depth * height
    whole_y = count_y * height

    cells = f32(3, depth, height, width)
    order_x, order_y = list(range(count_x)), list(range(count_y - 1, -1, -1))
    table = line_table(count_x, count_y, width, rows)
    if table is None:
        table = line_table_here(count_x, width, rows, order_y)
        columns_tables = column_tables_here(count_y, height, order_y)
    else:
        columns_tables = column_tables(count_y, height, order_y)
    sources = [jnp.asarray(t) for t in (table, *columns_tables)]
    twice = np.concatenate([np.eye(rows), np.eye(rows)], 1).astype(ml_dtypes.bfloat16)
    transform_flops = 6 * lines * count_x * width * count_y * lanes

    edge_rows = 3 * depth * width // lanes
    edge = f32(edge_rows, lanes)
    packed, first, last = call(
        pack_kernel,
        [cells, edge, edge],
        [hbm] * 3,
        (theta, phi, labels),
        scratch=(
            pltpu.VMEM((2, depth, height, width), jnp.float32),
            pltpu.VMEM((depth, height, width), jnp.int32),
            pltpu.SemaphoreType.DMA((3,)),
        ),
        name="pack",
    )
    table, forward, inverse = call(
        functools.partial(load_kernel, order_x, order_y),
        [
            pltpu.VMEM((2, count_x, width, count_y * lanes), jnp.bfloat16),
            pltpu.VMEM(sources[1].shape[1:], jnp.bfloat16),
            pltpu.VMEM(sources[2].shape[1:], jnp.bfloat16),
        ],
        [hbm] * 3,
        tuple(sources),
        scratch=(pltpu.SemaphoreType.DMA((2 + count_x * count_y,)),),
        name="load",
    )

    gathered, table = spread(packed, "gx", table)
    tensor = call(
        tensor_kernel,
        jax.ShapeDtypeStruct((48, 2 * whole_y, lanes), jnp.bfloat16),
        [vmem, vmem],
        (kernel.reshape(48, rows, 2 * whole_y), jnp.asarray(twice)),
        flops=48 * 2 * rows * lanes * 2 * whole_y,
        name="tensor",
    )
    region_scratch = (pltpu.SMEM(ms_region.shape, jnp.float32), pltpu.SemaphoreType.DMA)
    early, late = order_x[:-1], order_x[-1:]
    early_sums = call(
        functools.partial(early_lines_kernel, early),
        f32(lines, count_y * lanes),
        [vmem] * len(early) + [hbm, vmem],
        (*gathered[:-1], ms_region, held(table)),
        scratch=region_scratch,
        flops=transform_flops * len(early) // count_x,
        name="early_lines",
    )
    spectrum = call(
        functools.partial(lines_kernel, late, order_y),
        [f32(lines + (edge_rows if n in meeting(count_y) else 0), lanes) for n in order_y],
        [vmem] * 4 + [hbm, vmem],
        (gathered[-1], early_sums, first, last, ms_region, held(table)),
        scratch=region_scratch,
        flops=transform_flops * len(late) // count_x,
        name="lines",
    )
    columns = lax.optimization_barrier(exchanged(spectrum, "gy", order_y))
    scale = -1.0 / (2 * depth * 2 * whole_y * 2 * count_x * width)
    waves = call(
        functools.partial(waves_kernel, scale, count_y),
        [f32(lines, lanes)] * count_y,
        [vmem] * (count_y + 3),
        (*columns, tensor, forward, inverse),
        scratch=(
            pltpu.VMEM((2 * whole_y, 3 * depth * lanes), jnp.float32),
            pltpu.VMEM((6 * whole_y, 3 * depth * lanes), jnp.bfloat16),
        ),
        flops=20 * whole_y * whole_y * 3 * depth * lanes,
        name="waves",
    )
    returned = exchanged(waves, "gy", order_y)
    def back(numbers, chunks, name):
        blocks = call(
            functools.partial(back_lines_kernel, numbers, count_y),
            [f32(lines, width)] * len(numbers),
            [vmem] * (count_y + 1),
            (*chunks, held(table)),
            flops=transform_flops * len(numbers) // count_x,
            name=name,
        )
        return dict(zip(numbers, blocks))

    partial = back([n for n in order_x[2:] if n % 2], returned, "back_across")
    partial |= back([n for n in order_x[2:] if not n % 2] + [1], returned, "back_within")
    near = swapped(partial.pop(1), "gx", 1)
    parts, far_sum = far_sums(partial, "gx")
    returned, far_sum = lax.optimization_barrier((returned, far_sum))
    parts = [back([0], returned, "back_own")[0], near, *parts]
    edges = [columns[order_y.index(number)] for number in meeting(count_y)]
    edges, far_sum = lax.optimization_barrier((edges, far_sum))
    exchange, unit = call(
        functools.partial(exchange_kernel, order_x, count_y),
        [cells, cells],
        [vmem] * (count_x + len(edges)) + [smem] * 2,
        (*gathered, *edges, ms_region, aex_region),
        scratch=(pltpu.VMEM((count_x, 3, depth, height, width), jnp.float32),),
        flops=300 * depth * height * width,
        name="exchange",
    )
    field, predicted = call(
        functools.partial(final_kernel, len(parts)),
        [cells, cells],
        [vmem] * (len(parts) + 2),
        (*parts, exchange, unit),
        flops=60 * depth * height * width,
        name="predict",
    )
    return field, predicted


def solution(mesh):
    in_specs = (
        P(None, "gy", "gx"),
        P(None, "gy", "gx"),
        P(None, "gy", "gx"),
        P(),
        P(),
        P(None, None, ("gx", "gy"), None),
    )
    out_specs = (P(None, None, "gy", "gx"), P(None, None, "gy", "gx"))
    return jax.shard_map(
        per_device, mesh=mesh, in_specs=in_specs, out_specs=out_specs, check_vma=False
    )
```

```python
import functools
import math

import jax
import jax.numpy as jnp
import ml_dtypes
import numpy as np
from jax import lax
from jax.experimental import pallas as pl
from jax.experimental.pallas import tpu as pltpu
from jax.sharding import PartitionSpec as P

damping = 0.5
time_step = 0.2
side_weight = 0.25
layer_weight = 0.5
root_half = math.sqrt(0.5)
constant_limit = 20 << 20


def split_high(value):
    high = value.astype(jnp.bfloat16)
    low = (value - high.astype(jnp.float32)).astype(jnp.bfloat16)
    return high, low


def split_table(table):
    high = table.astype(np.float32).astype(ml_dtypes.bfloat16)
    low = (table - high.astype(np.float64)).astype(np.float32).astype(ml_dtypes.bfloat16)
    return high, low


def dot(left, right, contract=((1,), (0,))):
    return lax.dot_general(left, right, (contract, ((), ())), preferred_element_type=jnp.float32)


def line_table(count_x, count_y, width, rows):
    cells = count_x * width
    if count_x * 2 * cells * count_y * 2 * rows * 2 > constant_limit:
        return None
    place = np.arange(cells)[None, None, :, None]
    wave = (
        np.arange(count_x)[:, None, None, None] * (count_y * rows)
        + np.arange(count_y)[None, :, None, None] * rows
        + np.arange(rows)[None, None, None, :]
    )
    angle = (place * wave % (2 * cells)) * (2.0 * math.pi / (2 * cells))
    table = np.concatenate([np.cos(angle), -np.sin(angle)], 3)
    table = table.reshape(count_x, count_y, count_x, width, 2 * rows)
    high, low = split_table(table)
    return np.stack([high, low], 2)


def line_table_here(count_x, width, rows, order):
    cells = count_x * width
    count_y = len(order)
    place = jnp.arange(cells, dtype=jnp.int32)[:, None, None]
    block = lax.bitwise_xor(lax.axis_index("gy"), jnp.array(order, jnp.int32))
    wave = (
        lax.axis_index("gx") * (count_y * rows)
        + block[None, :, None] * rows
        + jnp.arange(rows, dtype=jnp.int32)[None, None, :]
    )
    angle = (place * wave % (2 * cells)).astype(jnp.float32) * (math.pi / cells)
    table = jnp.concatenate([jnp.cos(angle), -jnp.sin(angle)], 2)
    table = table.reshape(1, 1, count_x, width, count_y * 2 * rows)
    return jnp.stack(split_high(table), 2)


def column_tables(count_y, local, order):
    height = count_y * local
    wave = np.arange(2 * height)
    block = np.arange(count_y)[:, None] ^ np.array(order)[None, :]
    place = (block[:, :, None] * local + np.arange(local)).reshape(count_y, height)
    angle = (wave[None, :, None] * place[:, None, :] % (2 * height)) * (math.pi / height)
    high, low = split_table(np.concatenate([np.cos(angle), np.sin(angle)], 2))
    forward = np.concatenate([high, high, low], 2)
    angle = angle.transpose(0, 2, 1)
    high, low = split_table(np.concatenate([np.cos(angle), np.sin(angle)], 1))
    inverse = np.concatenate([high, high, low], 2)
    return forward, inverse


def column_tables_here(count_y, local, order):
    height = count_y * local
    wave = jnp.arange(2 * height, dtype=jnp.int32)
    block = lax.bitwise_xor(lax.axis_index("gy"), jnp.array(order, jnp.int32))
    place = (block[:, None] * local + jnp.arange(local, dtype=jnp.int32)).reshape(height)
    angle = (wave[:, None] * place % (2 * height)).astype(jnp.float32) * (math.pi / height)
    high, low = split_high(jnp.concatenate([jnp.cos(angle), jnp.sin(angle)], 1))
    forward = jnp.concatenate([high, high, low], 1)
    high, low = split_high(jnp.concatenate([jnp.cos(angle.T), jnp.sin(angle.T)], 0))
    inverse = jnp.concatenate([high, high, low], 1)
    return forward[None], inverse[None]


def load_kernel(order_x, order_y, *refs):
    table_ref, forward_ref, inverse_ref, table, forward, inverse, sem = refs
    gx, gy = lax.axis_index("gx"), lax.axis_index("gy")
    mine_x = gx if table_ref.shape[0] > 1 else 0
    mine_y = gy if forward_ref.shape[0] > 1 else 0
    lanes = table_ref.shape[5]
    copies = [
        pltpu.make_async_copy(forward_ref.at[mine_y], forward, sem.at[0]),
        pltpu.make_async_copy(inverse_ref.at[mine_y], inverse, sem.at[1]),
    ]
    for spot_x, number_x in enumerate(order_x):
        block_x = lax.bitwise_xor(gx, number_x)
        for spot_y in range(table_ref.shape[1]):
            block_y = lax.bitwise_xor(gy, order_y[spot_y]) if table_ref.shape[1] > 1 else 0
            columns = slice(spot_y * lanes, (spot_y + 1) * lanes)
            copies.append(
                pltpu.make_async_copy(
                    table_ref.at[mine_x, block_y, :, block_x],
                    table.at[:, spot_x, :, columns],
                    sem.at[len(copies)],
                )
            )
    for copy in copies:
        copy.start()
    for copy in copies:
        copy.wait()


def sine_cosine(angle):
    turns = jnp.floor(angle * (2.0 / math.pi) + 0.5)
    rest = angle - turns * 1.5703125
    rest = rest - turns * 4.8351287841796875e-4
    rest = rest - turns * 3.1385570764541626e-7
    square = rest * rest
    sine = rest + rest * square * (
        -1.6666654611e-1 + square * (8.3321608736e-3 - square * 1.9515295891e-4)
    )
    cosine = (
        1.0
        - 0.5 * square
        + square * square * (4.166664568298827e-2 + square * (-1.388731625493765e-3 + square * 2.443315711809948e-5))
    )
    quarter = turns.astype(jnp.int32)
    odd = (quarter & 1) == 1
    out_sine = jnp.where(odd, cosine, sine)
    out_cosine = jnp.where(odd, sine, cosine)
    out_sine = jnp.where((quarter & 2) == 2, -out_sine, out_sine)
    out_cosine = jnp.where(((quarter + 1) & 2) == 2, -out_cosine, out_cosine)
    return out_sine, out_cosine


def directions(theta, phi):
    lateral, axial = sine_cosine(theta)
    sine, cosine = sine_cosine(phi)
    return [lateral * cosine, lateral * sine, axial]


def looked_up(labels, region):
    rows = len(region.shape) > 1
    value = [region[i : i + 1, :] if rows else region[i] for i in range(region.shape[0])]
    result = jnp.zeros_like(labels) + value[0]
    for index in range(1, region.shape[0]):
        result = jnp.where(labels == float(index), value[index], result)
    return result


def pack_kernel(theta_ref, phi_ref, labels_ref, region_ref, *refs):
    raw_ref, first_ref, last_ref, rows_ref, angle, label, region, sems = refs
    height = theta_ref.shape[1]
    copies = [
        pltpu.make_async_copy(theta_ref, angle.at[0], sems.at[0]),
        pltpu.make_async_copy(phi_ref, angle.at[1], sems.at[1]),
        pltpu.make_async_copy(labels_ref, label, sems.at[2]),
        pltpu.make_async_copy(region_ref, region, sems.at[3]),
    ]
    for copy in copies:
        copy.start()
    for copy in copies:
        copy.wait()
    for index, value in enumerate((angle[0], angle[1], label[...].astype(jnp.float32))):
        raw_ref[index] = value
        put_edge(first_ref, index, value[:, 0])
        put_edge(last_ref, index, value[:, height - 1])
    for index in range(rows_ref.shape[0]):
        rows_ref[index : index + 1] = jnp.full((1, rows_ref.shape[1]), region[index], jnp.float32)


def meeting(devices):
    return [number for number in range(1, devices) if (number & (number + 1)) == 0]


def edge_spots(depth, width, lanes, start, field):
    pieces = width // lanes
    return [start + (field * pieces + piece) * depth for piece in range(pieces)]


def put_edge(ref, field, edge):
    lanes = ref.shape[1]
    for piece, row in enumerate(edge_spots(*edge.shape, lanes, 0, field)):
        ref[row : row + edge.shape[0]] = edge[:, piece * lanes : (piece + 1) * lanes]


def get_edge(ref, depth, width, start, field):
    spots = edge_spots(depth, width, ref.shape[1], start, field)
    return jnp.concatenate([ref[row : row + depth] for row in spots], 1)


def lines_of(raw_refs, numbers, region, table):
    units = [directions(raw_ref[0], raw_ref[1]) for raw_ref in raw_refs]
    total = None
    for raw_ref, unit, number in zip(raw_refs, units, numbers):
        saturation = looked_up(raw_ref[2], region)
        rows = saturation.shape[0] * saturation.shape[1]
        block = [(part * saturation).reshape(rows, -1) for part in unit]
        high, low = split_high(jnp.concatenate(block, 0))
        both = dot(jnp.concatenate([high, low], 0), table[0, number])
        part = both[: 3 * rows] + both[3 * rows :] + dot(high, table[1, number])
        total = part if total is None else total + part
    return total


def early_lines_kernel(numbers, *refs):
    raw_refs, (region, table, out_ref) = refs[: len(numbers)], refs[len(numbers) :]
    out_ref[...] = lines_of(raw_refs, numbers, region, table)


def lines_kernel(numbers, order_y, *refs):
    raw_refs, operands = refs[: len(numbers)], refs[len(numbers) : len(numbers) + 5]
    early_ref, first_ref, last_ref, region, table = operands
    gy = lax.axis_index("gy")
    out_refs = refs[len(numbers) + 5 :]
    total = lines_of(raw_refs, numbers, region, table) + early_ref[...]
    lines, lanes = total.shape[0], first_ref.shape[1]
    for spot, (number, out_ref) in enumerate(zip(order_y, out_refs)):
        out_ref[:lines] = total[:, spot * lanes : (spot + 1) * lanes]
        if number in meeting(len(order_y)):
            up = lax.bitwise_xor(gy, number) > gy
            out_ref[lines:] = jnp.where(up, last_ref[...], first_ref[...])


def back_lines_kernel(numbers, count_y, *refs):
    in_refs, table, out_refs = refs[:count_y], refs[count_y], refs[count_y + 1 :]
    high, low = split_high(jnp.concatenate([ref[...] for ref in in_refs], 1))
    both = jnp.concatenate([high, low], 0)
    lines = high.shape[0]
    for number, out_ref in zip(numbers, out_refs):
        wide = dot(both, table[0, number], ((1,), (1,)))
        out_ref[...] = wide[:lines] + wide[lines:] + dot(high, table[1, number], ((1,), (1,)))


def tensor_kernel(kernel_ref, twice_ref, out_ref):
    twice = twice_ref[...]

    unroll = 8

    def step(index, carry):
        for offset in range(unroll):
            turned = dot(kernel_ref[index * unroll + offset], twice, ((0,), (0,)))
            out_ref[index * unroll + offset] = turned.astype(jnp.bfloat16)
        return carry

    lax.fori_loop(0, kernel_ref.shape[0] // unroll, step, 0)


def turn(value, sign):
    lanes = value.shape[-1]
    if lanes == 128:
        return pltpu.roll(value, lanes // 2, value.ndim - 1) * sign
    return jnp.concatenate([value[..., lanes // 2 :], value[..., : lanes // 2]], -1) * sign


def layers_forward(layer, sign):
    d0, d1, d2, d3 = layer
    r2 = turn(d2, sign)
    near, far = d1 + d3, d1 - d3
    far_turned = turn(far, sign)
    near_turned = turn(near, sign)
    even, odd = d0 + d2, d0 - d2
    out = [None] * 8
    out[0], out[4] = even + near, even - near
    out[2], out[6] = odd + far_turned, odd - far_turned
    plus, minus = d0 + r2, d0 - r2
    first = (far + near_turned) * root_half
    second = (near_turned - far) * root_half
    out[1], out[5] = plus + first, plus - first
    out[3], out[7] = minus + second, minus - second
    return out


def layers_inverse(wave, sign):
    a, b = wave[0] + wave[4], wave[0] - wave[4]
    e, f = wave[2] + wave[6], turn(wave[2] - wave[6], sign)
    p, q = wave[1] + wave[5], wave[1] - wave[5]
    s, t = wave[3] + wave[7], turn(wave[3] - wave[7], sign)
    o0, o1, o2, o3 = p + s, q - t, p - s, q + t
    return [
        a + e + o0,
        b - f + (o1 - turn(o1, sign)) * root_half,
        a - e - turn(o2, sign),
        b + f - (o3 + turn(o3, sign)) * root_half,
    ]


def apply_tensor(tensor, wave):
    out = [[], [], []]
    for level in range(8):
        xx, yy, zz, xy, xz, yz = [tensor[part][level] for part in range(6)]
        x, y, z = wave[0][level], wave[1][level], wave[2][level]
        out[0].append(xx * x + xy * y + xz * z)
        out[1].append(xy * x + yy * y + yz * z)
        out[2].append(xz * x + yz * y + zz * z)
    return out


def waves_kernel(scale, count_y, *refs):
    spec_refs, (tensor_ref, forward_ref, inverse_ref) = refs[:count_y], refs[count_y : count_y + 3]
    out_refs, (wave_ref, back_ref) = refs[count_y + 3 : -2], refs[-2:]
    lines, lanes = out_refs[0].shape
    local = 8
    planes = lines // local
    height = count_y * local
    sign = jnp.where(
        lax.broadcasted_iota(jnp.int32, (1, lanes), 1) < lanes // 2, 1.0, -1.0
    ).astype(jnp.float32)
    columns = []
    for plane in range(planes):
        value = jnp.concatenate(
            [spec_ref[plane * local : (plane + 1) * local] for spec_ref in spec_refs], 0
        )
        value = jnp.concatenate([value, turn(value, sign)], 0)
        high, low = split_high(value)
        columns.append(jnp.concatenate([high, low, high], 0))
    wave_ref[...] = dot(forward_ref[...], jnp.concatenate(columns, 1))

    chunk = 16
    depth = planes // 3
    double = 2 * height

    def step(index, carry):
        rows = pl.ds(pl.multiple_of(index * chunk, chunk), chunk)
        wave = []
        for part in range(3):
            layer = [
                wave_ref[rows, (part * depth + z) * lanes : (part * depth + z + 1) * lanes]
                for z in range(depth)
            ]
            wave.append(layers_forward(layer, sign))
        tensor = [
            [tensor_ref[part * 8 + level, rows, :].astype(jnp.float32) for level in range(8)]
            for part in range(6)
        ]
        image = apply_tensor(tensor, wave)
        for part in range(3):
            layer = layers_inverse(image[part], sign)
            for z in range(depth):
                spot = slice((part * depth + z) * lanes, (part * depth + z + 1) * lanes)
                high, low = split_high(layer[z] * scale)
                back_ref[rows, spot] = high
                back_ref[pl.ds(pl.multiple_of(double + index * chunk, chunk), chunk), spot] = low
                back_ref[pl.ds(pl.multiple_of(2 * double + index * chunk, chunk), chunk), spot] = high
        return carry

    lax.fori_loop(0, double // chunk, step, 0, unroll=True)
    back = dot(inverse_ref[...], back_ref[...])
    for plane in range(planes):
        part = slice(plane * lanes, (plane + 1) * lanes)
        value = back[:height, part] - turn(back[height:, part], sign)
        for number in range(count_y):
            out_refs[number][plane * local : (plane + 1) * local] = value[
                number * local : (number + 1) * local
            ]


def exchange_kernel(order_x, count_y, *refs):
    count_x, numbers = len(order_x), meeting(count_y)
    raw_refs, edge_refs, (ms_ref, aex_ref) = refs[:count_x], refs[count_x:-5], refs[-5:-3]
    exchange_ref, unit_ref, raw_ref = refs[-3:]
    depth, height, width = raw_ref.shape[2:]
    gx, gy = lax.axis_index("gx"), lax.axis_index("gy")

    def row_beside(field, other):
        value = None
        for number, edge_ref in zip(numbers, edge_refs):
            edge = get_edge(edge_ref, depth, width, 3 * depth * height, field)
            match = lax.bitwise_xor(gy, number) == other
            value = edge if value is None else jnp.where(match, edge, value)
        return value[:, None, :]

    for spot, number in enumerate(order_x):
        raw_ref[lax.bitwise_xor(gx, number)] = raw_refs[spot][...]
    left, right = jnp.maximum(gx - 1, 0), jnp.minimum(gx + 1, count_x - 1)
    shape = (depth, height, width)
    lane = lax.broadcasted_iota(jnp.int32, shape, 2)
    row = lax.broadcasted_iota(jnp.int32, shape, 1)

    def quantities(values):
        return directions(values[0], values[1]) + [looked_up(values[2], aex_ref)]

    raw = [raw_refs[0][f] for f in range(3)]
    here = quantities(raw)
    side = quantities([jnp.where(lane == 0, raw_ref[right, f], raw_ref[left, f]) for f in range(3)])
    above = quantities(
        [jnp.where(row == 0, row_beside(f, gy + 1), row_beside(f, gy - 1)) for f in range(3)]
    )
    saturation = looked_up(raw[2], ms_ref)
    total = [jnp.zeros(shape, jnp.float32) for _ in range(3)]

    def add(total, beside, weight):
        coupling = 2.0 * here[3] * beside[3] / (here[3] + beside[3]) * weight
        return [total[c] + coupling * (beside[c] - here[c]) for c in range(3)]

    one = jnp.float32(1.0)
    zero = jnp.float32(0.0)
    for shift, edge, there in ((1, 0, gx > 0), (width - 1, width - 1, gx < count_x - 1)):
        beside = [
            jnp.where(lane == edge, pltpu.roll(s, shift, 2), pltpu.roll(h, shift, 2))
            for s, h in zip(side, here)
        ]
        weight = jnp.where(lane == edge, jnp.where(there, one, zero), one) * side_weight
        total = add(total, beside, weight)
    for shift, edge, there in ((1, 0, gy > 0), (height - 1, height - 1, gy < count_y - 1)):
        beside = [
            jnp.where(row == edge, pltpu.roll(s, shift, 1), pltpu.roll(h, shift, 1))
            for s, h in zip(above, here)
        ]
        weight = jnp.where(row == edge, jnp.where(there, one, zero), one) * side_weight
        total = add(total, beside, weight)
    for part in range(3):
        unit_ref[part] = here[part]
    for z in range(depth):
        out = [total[c][z] for c in range(3)]
        for other in (z - 1, z + 1):
            if 0 <= other < depth:
                a, b = here[3][z], here[3][other]
                coupling = 2.0 * a * b / (a + b) * layer_weight
                out = [out[c] + coupling * (here[c][other] - here[c][z]) for c in range(3)]
        for c in range(3):
            exchange_ref[c, z] = out[c] / saturation[z]


def cross(first, second):
    return [
        first[1] * second[2] - first[2] * second[1],
        first[2] * second[0] - first[0] * second[2],
        first[0] * second[1] - first[1] * second[0],
    ]


def final_kernel(count_x, *refs):
    part_refs, (exchange_ref, unit_ref, field_ref, predicted_ref) = refs[:count_x], refs[count_x:]
    depth, height, width = unit_ref.shape[1:]
    rows = depth * height
    unit, field = [], []
    for c in range(3):
        place = slice(c * rows, (c + 1) * rows)
        total = part_refs[0][place]
        for part_ref in part_refs[1:]:
            total = total + part_ref[place]
        field.append(exchange_ref[c] + total.reshape(depth, height, width))
        unit.append(unit_ref[c])
        field_ref[c] = field[c]
    twist = cross(unit, field)
    second = cross(unit, twist)
    moved = [
        unit[c] - (time_step / (1.0 + damping * damping)) * (twist[c] + damping * second[c])
        for c in range(3)
    ]
    length = jnp.sqrt(moved[0] * moved[0] + moved[1] * moved[1] + moved[2] * moved[2])
    for c in range(3):
        predicted_ref[c] = moved[c] / length


vmem = pl.BlockSpec(memory_space=pltpu.VMEM)
smem = pl.BlockSpec(memory_space=pltpu.SMEM)
hbm = pl.BlockSpec(memory_space=pltpu.HBM)


def call(body, out, ins, operands, scratch=(), flops=0, name=None, grant=16 << 20):
    operands = [
        pltpu.with_memory_space_constraint(o, pltpu.HBM) if i is hbm else o
        for i, o in zip(ins, operands)
    ]
    size = sum(math.prod(o.shape) * o.dtype.itemsize for o in operands)
    outs = out if isinstance(out, (list, tuple)) else [out]
    size += sum(math.prod(o.shape) * jnp.dtype(o.dtype).itemsize for o in outs)
    return pl.pallas_call(
        body,
        out_shape=out,
        in_specs=ins,
        out_specs=[vmem] * len(outs) if outs is out else vmem,
        scratch_shapes=list(scratch),
        compiler_params=pltpu.CompilerParams(vmem_limit_bytes=grant),
        cost_estimate=pl.CostEstimate(flops=flops, bytes_accessed=size, transcendentals=0),
        name=name,
    )(*operands)


def f32(*shape):
    return jax.ShapeDtypeStruct(shape, jnp.float32)


def swapped(chunk, axis, number):
    devices = lax.axis_size(axis)
    return lax.ppermute(chunk, axis, [(i, i ^ number) for i in range(devices)])


def exchanged(chunks, axis, order):
    return [swapped(c, axis, n) if n else c for c, n in zip(chunks, order)]


def held(value):
    return pltpu.with_memory_space_constraint(value, pltpu.VMEM)


def after(value, other):
    return lax.optimization_barrier((value, other))[0]


def spread(block, axis, first):
    blocks = {0: block}
    bit = lax.axis_size(axis) // 2
    while bit:
        for number in list(blocks):
            blocks[number ^ bit] = swapped(blocks[number], axis, bit)
        if first is not None:
            blocks[bit], first = lax.optimization_barrier((blocks[bit], first))
            ready, first = first, None
        bit //= 2
    return [blocks[number] for number in range(lax.axis_size(axis))], ready


def far_sums(blocks, axis):
    blocks = {number: [block] for number, block in blocks.items()}
    terms, bit, block = [], 1, None
    while bit < lax.axis_size(axis):
        for number in sorted(blocks, reverse=True):
            if number & bit:
                block = functools.reduce(jnp.add, blocks.pop(number))
                blocks.get(number ^ bit, terms).append(swapped(block, axis, bit))
        bit *= 2
    return terms, block


def per_device(theta, phi, labels, ms_region, aex_region, kernel):
    count_x, count_y = lax.axis_size("gx"), lax.axis_size("gy")
    gx, gy = lax.axis_index("gx"), lax.axis_index("gy")
    depth, height, width = theta.shape
    rows = kernel.shape[2]
    lanes = 2 * rows
    lines = 3 * depth * height
    whole_y = count_y * height

    cells = f32(3, depth, height, width)
    order_x, order_y = list(range(count_x)), list(range(count_y - 1, -1, -1))
    table = line_table(count_x, count_y, width, rows)
    if table is None:
        table = line_table_here(count_x, width, rows, order_y)
        columns_tables = column_tables_here(count_y, height, order_y)
    else:
        columns_tables = column_tables(count_y, height, order_y)
    sources = [jnp.asarray(t) for t in (table, *columns_tables)]
    twice = np.concatenate([np.eye(rows), np.eye(rows)], 1).astype(ml_dtypes.bfloat16)
    transform_flops = 6 * lines * count_x * width * count_y * lanes

    edge_rows = 3 * depth * width // lanes
    edge = f32(edge_rows, lanes)
    packed, first, last, ms_rows = call(
        pack_kernel,
        [cells, edge, edge, f32(*ms_region.shape, width)],
        [hbm] * 4,
        (theta, phi, labels, ms_region),
        scratch=(
            pltpu.VMEM((2, depth, height, width), jnp.float32),
            pltpu.VMEM((depth, height, width), jnp.int32),
            pltpu.SMEM(ms_region.shape, jnp.float32),
            pltpu.SemaphoreType.DMA((4,)),
        ),
        name="pack",
    )
    table, forward, inverse = call(
        functools.partial(load_kernel, order_x, order_y),
        [
            pltpu.VMEM((2, count_x, width, count_y * lanes), jnp.bfloat16),
            pltpu.VMEM(sources[1].shape[1:], jnp.bfloat16),
            pltpu.VMEM(sources[2].shape[1:], jnp.bfloat16),
        ],
        [hbm] * 3,
        tuple(sources),
        scratch=(pltpu.SemaphoreType.DMA((2 + count_x * count_y,)),),
        name="load",
    )

    gathered, table = spread(packed, "gx", table)
    tensor = call(
        tensor_kernel,
        jax.ShapeDtypeStruct((48, 2 * whole_y, lanes), jnp.bfloat16),
        [vmem, vmem],
        (kernel.reshape(48, rows, 2 * whole_y), jnp.asarray(twice)),
        flops=48 * 2 * rows * lanes * 2 * whole_y,
        name="tensor",
    )
    early, late = order_x[:-1], order_x[-1:]
    early_sums = call(
        functools.partial(early_lines_kernel, early),
        f32(lines, count_y * lanes),
        [vmem] * len(early) + [vmem, vmem],
        (*gathered[:-1], ms_rows, held(table)),
        flops=transform_flops * len(early) // count_x,
        name="early_lines",
    )
    spectrum = call(
        functools.partial(lines_kernel, late, order_y),
        [f32(lines + (edge_rows if n in meeting(count_y) else 0), lanes) for n in order_y],
        [vmem] * 6,
        (gathered[-1], early_sums, first, last, ms_rows, held(table)),
        flops=transform_flops * len(late) // count_x,
        name="lines",
    )
    columns = lax.optimization_barrier(exchanged(spectrum, "gy", order_y))
    scale = -1.0 / (2 * depth * 2 * whole_y * 2 * count_x * width)
    waves = call(
        functools.partial(waves_kernel, scale, count_y),
        [f32(lines, lanes)] * count_y,
        [vmem] * (count_y + 3),
        (*columns, tensor, forward, inverse),
        scratch=(
            pltpu.VMEM((2 * whole_y, 3 * depth * lanes), jnp.float32),
            pltpu.VMEM((6 * whole_y, 3 * depth * lanes), jnp.bfloat16),
        ),
        flops=20 * whole_y * whole_y * 3 * depth * lanes,
        name="waves",
    )
    returned = exchanged(waves, "gy", order_y)
    def back(numbers, chunks, name):
        blocks = call(
            functools.partial(back_lines_kernel, numbers, count_y),
            [f32(lines, width)] * len(numbers),
            [vmem] * (count_y + 1),
            (*chunks, held(table)),
            flops=transform_flops * len(numbers) // count_x,
            name=name,
        )
        return dict(zip(numbers, blocks))

    partial = back([n for n in order_x[2:] if n % 2], returned, "back_across")
    partial |= back([n for n in order_x[2:] if not n % 2] + [1], returned, "back_within")
    near = swapped(partial.pop(1), "gx", 1)
    parts, far_sum = far_sums(partial, "gx")
    returned, far_sum = lax.optimization_barrier((returned, far_sum))
    parts = [back([0], returned, "back_own")[0], near, *parts]
    edges = [columns[order_y.index(number)] for number in meeting(count_y)]
    edges, far_sum = lax.optimization_barrier((edges, far_sum))
    exchange, unit = call(
        functools.partial(exchange_kernel, order_x, count_y),
        [cells, cells],
        [vmem] * (count_x + len(edges)) + [smem] * 2,
        (*gathered, *edges, ms_region, aex_region),
        scratch=(pltpu.VMEM((count_x, 3, depth, height, width), jnp.float32),),
        flops=300 * depth * height * width,
        name="exchange",
    )
    field, predicted = call(
        functools.partial(final_kernel, len(parts)),
        [cells, cells],
        [vmem] * (len(parts) + 2),
        (*parts, exchange, unit),
        flops=60 * depth * height * width,
        name="predict",
    )
    return field, predicted


def solution(mesh):
    in_specs = (
        P(None, "gy", "gx"),
        P(None, "gy", "gx"),
        P(None, "gy", "gx"),
        P(),
        P(),
        P(None, None, ("gx", "gy"), None),
    )
    out_specs = (P(None, None, "gy", "gx"), P(None, None, "gy", "gx"))
    return jax.shard_map(
        per_device, mesh=mesh, in_specs=in_specs, out_specs=out_specs, check_vma=False
    )
```

```python
import functools
import math

import jax
import jax.numpy as jnp
import ml_dtypes
import numpy as np
from jax import lax
from jax.experimental import pallas as pl
from jax.experimental.pallas import tpu as pltpu
from jax.sharding import PartitionSpec as P

damping = 0.5
time_step = 0.2
side_weight = 0.25
layer_weight = 0.5
root_half = math.sqrt(0.5)
constant_limit = 20 << 20


def split_high(value):
    high = value.astype(jnp.bfloat16)
    low = (value - high.astype(jnp.float32)).astype(jnp.bfloat16)
    return high, low


def split_table(table):
    high = table.astype(np.float32).astype(ml_dtypes.bfloat16)
    low = (table - high.astype(np.float64)).astype(np.float32).astype(ml_dtypes.bfloat16)
    return high, low


def dot(left, right, contract=((1,), (0,))):
    return lax.dot_general(left, right, (contract, ((), ())), preferred_element_type=jnp.float32)


def line_table(count_x, count_y, width, rows):
    cells = count_x * width
    if count_x * 2 * cells * count_y * 2 * rows * 2 > constant_limit:
        return None
    place = np.arange(cells)[None, None, :, None]
    wave = (
        np.arange(count_x)[:, None, None, None] * (count_y * rows)
        + np.arange(count_y)[None, :, None, None] * rows
        + np.arange(rows)[None, None, None, :]
    )
    angle = (place * wave % (2 * cells)) * (2.0 * math.pi / (2 * cells))
    table = np.concatenate([np.cos(angle), -np.sin(angle)], 3)
    table = table.reshape(count_x, count_y, count_x, width, 2 * rows)
    high, low = split_table(table)
    return np.stack([high, low], 2)


def line_table_here(count_x, width, rows, order):
    cells = count_x * width
    count_y = len(order)
    place = jnp.arange(cells, dtype=jnp.int32)[:, None, None]
    block = lax.bitwise_xor(lax.axis_index("gy"), jnp.array(order, jnp.int32))
    wave = (
        lax.axis_index("gx") * (count_y * rows)
        + block[None, :, None] * rows
        + jnp.arange(rows, dtype=jnp.int32)[None, None, :]
    )
    angle = (place * wave % (2 * cells)).astype(jnp.float32) * (math.pi / cells)
    table = jnp.concatenate([jnp.cos(angle), -jnp.sin(angle)], 2)
    table = table.reshape(1, 1, count_x, width, count_y * 2 * rows)
    return jnp.stack(split_high(table), 2)


def column_tables(count_y, local, order):
    height = count_y * local
    wave = np.arange(2 * height)
    block = np.arange(count_y)[:, None] ^ np.array(order)[None, :]
    place = (block[:, :, None] * local + np.arange(local)).reshape(count_y, height)
    angle = (wave[None, :, None] * place[:, None, :] % (2 * height)) * (math.pi / height)
    high, low = split_table(np.concatenate([np.cos(angle), np.sin(angle)], 2))
    forward = np.concatenate([high, high, low], 2)
    angle = angle.transpose(0, 2, 1)
    high, low = split_table(np.concatenate([np.cos(angle), np.sin(angle)], 1))
    inverse = np.concatenate([high, high, low], 2)
    return forward, inverse


def column_tables_here(count_y, local, order):
    height = count_y * local
    wave = jnp.arange(2 * height, dtype=jnp.int32)
    block = lax.bitwise_xor(lax.axis_index("gy"), jnp.array(order, jnp.int32))
    place = (block[:, None] * local + jnp.arange(local, dtype=jnp.int32)).reshape(height)
    angle = (wave[:, None] * place % (2 * height)).astype(jnp.float32) * (math.pi / height)
    high, low = split_high(jnp.concatenate([jnp.cos(angle), jnp.sin(angle)], 1))
    forward = jnp.concatenate([high, high, low], 1)
    high, low = split_high(jnp.concatenate([jnp.cos(angle.T), jnp.sin(angle.T)], 0))
    inverse = jnp.concatenate([high, high, low], 1)
    return forward[None], inverse[None]


def load_kernel(order_x, order_y, *refs):
    table_ref, forward_ref, inverse_ref, table, forward, inverse, sem = refs
    gx, gy = lax.axis_index("gx"), lax.axis_index("gy")
    mine_x = gx if table_ref.shape[0] > 1 else 0
    mine_y = gy if forward_ref.shape[0] > 1 else 0
    lanes = table_ref.shape[5]
    copies = [
        pltpu.make_async_copy(forward_ref.at[mine_y], forward, sem.at[0]),
        pltpu.make_async_copy(inverse_ref.at[mine_y], inverse, sem.at[1]),
    ]
    for spot_x, number_x in enumerate(order_x):
        block_x = lax.bitwise_xor(gx, number_x)
        for spot_y in range(table_ref.shape[1]):
            block_y = lax.bitwise_xor(gy, order_y[spot_y]) if table_ref.shape[1] > 1 else 0
            columns = slice(spot_y * lanes, (spot_y + 1) * lanes)
            copies.append(
                pltpu.make_async_copy(
                    table_ref.at[mine_x, block_y, :, block_x],
                    table.at[:, spot_x, :, columns],
                    sem.at[len(copies)],
                )
            )
    for copy in copies:
        copy.start()
    for copy in copies:
        copy.wait()


def sine_cosine(angle):
    turns = jnp.floor(angle * (2.0 / math.pi) + 0.5)
    rest = angle - turns * 1.5703125
    rest = rest - turns * 4.8351287841796875e-4
    rest = rest - turns * 3.1385570764541626e-7
    square = rest * rest
    sine = rest + rest * square * (
        -1.6666654611e-1 + square * (8.3321608736e-3 - square * 1.9515295891e-4)
    )
    cosine = (
        1.0
        - 0.5 * square
        + square * square * (4.166664568298827e-2 + square * (-1.388731625493765e-3 + square * 2.443315711809948e-5))
    )
    quarter = turns.astype(jnp.int32)
    odd = (quarter & 1) == 1
    out_sine = jnp.where(odd, cosine, sine)
    out_cosine = jnp.where(odd, sine, cosine)
    out_sine = jnp.where((quarter & 2) == 2, -out_sine, out_sine)
    out_cosine = jnp.where(((quarter + 1) & 2) == 2, -out_cosine, out_cosine)
    return out_sine, out_cosine


def directions(theta, phi):
    lateral, axial = sine_cosine(theta)
    sine, cosine = sine_cosine(phi)
    return [lateral * cosine, lateral * sine, axial]


def looked_up(labels, region):
    rows = len(region.shape) > 1
    value = [region[i : i + 1, :] if rows else region[i] for i in range(region.shape[0])]
    result = jnp.zeros_like(labels) + value[0]
    for index in range(1, region.shape[0]):
        result = jnp.where(labels == float(index), value[index], result)
    return result


def pack_kernel(theta_ref, phi_ref, labels_ref, region_ref, *refs):
    raw_ref, first_ref, last_ref, rows_ref, angle, label, region, sems = refs
    height = theta_ref.shape[1]
    copies = [
        pltpu.make_async_copy(theta_ref, angle.at[0], sems.at[0]),
        pltpu.make_async_copy(phi_ref, angle.at[1], sems.at[1]),
        pltpu.make_async_copy(labels_ref, label, sems.at[2]),
        pltpu.make_async_copy(region_ref, region, sems.at[3]),
    ]
    for copy in copies:
        copy.start()
    for copy in copies:
        copy.wait()
    for index, value in enumerate((angle[0], angle[1], label[...].astype(jnp.float32))):
        raw_ref[index] = value
        put_edge(first_ref, index, value[:, 0])
        put_edge(last_ref, index, value[:, height - 1])
    for index in range(rows_ref.shape[0]):
        rows_ref[index : index + 1] = jnp.full((1, rows_ref.shape[1]), region[index], jnp.float32)


def meeting(devices):
    return [number for number in range(1, devices) if (number & (number + 1)) == 0]


def carrying(devices):
    return meeting(devices) + [devices // 2]


def edge_spots(depth, width, lanes, start, field):
    pieces = width // lanes
    return [start + (field * pieces + piece) * depth for piece in range(pieces)]


def put_edge(ref, field, edge):
    lanes = ref.shape[1]
    for piece, row in enumerate(edge_spots(*edge.shape, lanes, 0, field)):
        ref[row : row + edge.shape[0]] = edge[:, piece * lanes : (piece + 1) * lanes]


def get_edge(ref, depth, width, start, field):
    spots = edge_spots(depth, width, ref.shape[1], start, field)
    return jnp.concatenate([ref[row : row + depth] for row in spots], 1)


def lines_of(raw_refs, numbers, region, table):
    units = [directions(raw_ref[0], raw_ref[1]) for raw_ref in raw_refs]
    total = None
    for raw_ref, unit, number in zip(raw_refs, units, numbers):
        saturation = looked_up(raw_ref[2], region)
        rows = saturation.shape[0] * saturation.shape[1]
        block = [(part * saturation).reshape(rows, -1) for part in unit]
        high, low = split_high(jnp.concatenate(block, 0))
        both = dot(jnp.concatenate([high, low], 0), table[0, number])
        part = both[: 3 * rows] + both[3 * rows :] + dot(high, table[1, number])
        total = part if total is None else total + part
    return total


def early_lines_kernel(numbers, *refs):
    raw_refs, (region, table, out_ref) = refs[: len(numbers)], refs[len(numbers) :]
    out_ref[...] = lines_of(raw_refs, numbers, region, table)


def lines_kernel(numbers, order_y, *refs):
    raw_refs, operands = refs[: len(numbers)], refs[len(numbers) : len(numbers) + 5]
    early_ref, first_ref, last_ref, region, table = operands
    gy = lax.axis_index("gy")
    out_refs = refs[len(numbers) + 5 :]
    total = lines_of(raw_refs, numbers, region, table) + early_ref[...]
    lines, lanes = total.shape[0], first_ref.shape[1]
    for spot, (number, out_ref) in enumerate(zip(order_y, out_refs)):
        out_ref[:lines] = total[:, spot * lanes : (spot + 1) * lanes]
        if number in carrying(len(order_y)):
            up = lax.bitwise_xor(gy, number) > gy
            out_ref[lines:] = jnp.where(up, last_ref[...], first_ref[...])


def back_lines_kernel(numbers, count_y, *refs):
    in_refs, table, out_refs = refs[:count_y], refs[count_y], refs[count_y + 1 :]
    high, low = split_high(jnp.concatenate([ref[...] for ref in in_refs], 1))
    both = jnp.concatenate([high, low], 0)
    lines = high.shape[0]
    for number, out_ref in zip(numbers, out_refs):
        wide = dot(both, table[0, number], ((1,), (1,)))
        out_ref[...] = wide[:lines] + wide[lines:] + dot(high, table[1, number], ((1,), (1,)))


def tensor_kernel(kernel_ref, twice_ref, out_ref):
    twice = twice_ref[...]

    unroll = 8

    def step(index, carry):
        for offset in range(unroll):
            turned = dot(kernel_ref[index * unroll + offset], twice, ((0,), (0,)))
            out_ref[index * unroll + offset] = turned.astype(jnp.bfloat16)
        return carry

    lax.fori_loop(0, kernel_ref.shape[0] // unroll, step, 0)


def turn(value, sign):
    lanes = value.shape[-1]
    if lanes == 128:
        return pltpu.roll(value, lanes // 2, value.ndim - 1) * sign
    return jnp.concatenate([value[..., lanes // 2 :], value[..., : lanes // 2]], -1) * sign


def layers_forward(layer, sign):
    d0, d1, d2, d3 = layer
    r2 = turn(d2, sign)
    near, far = d1 + d3, d1 - d3
    far_turned = turn(far, sign)
    near_turned = turn(near, sign)
    even, odd = d0 + d2, d0 - d2
    out = [None] * 8
    out[0], out[4] = even + near, even - near
    out[2], out[6] = odd + far_turned, odd - far_turned
    plus, minus = d0 + r2, d0 - r2
    first = (far + near_turned) * root_half
    second = (near_turned - far) * root_half
    out[1], out[5] = plus + first, plus - first
    out[3], out[7] = minus + second, minus - second
    return out


def layers_inverse(wave, sign):
    a, b = wave[0] + wave[4], wave[0] - wave[4]
    e, f = wave[2] + wave[6], turn(wave[2] - wave[6], sign)
    p, q = wave[1] + wave[5], wave[1] - wave[5]
    s, t = wave[3] + wave[7], turn(wave[3] - wave[7], sign)
    o0, o1, o2, o3 = p + s, q - t, p - s, q + t
    return [
        a + e + o0,
        b - f + (o1 - turn(o1, sign)) * root_half,
        a - e - turn(o2, sign),
        b + f - (o3 + turn(o3, sign)) * root_half,
    ]


def apply_tensor(tensor, wave):
    out = [[], [], []]
    for level in range(8):
        xx, yy, zz, xy, xz, yz = [tensor[part][level] for part in range(6)]
        x, y, z = wave[0][level], wave[1][level], wave[2][level]
        out[0].append(xx * x + xy * y + xz * z)
        out[1].append(xy * x + yy * y + yz * z)
        out[2].append(xz * x + yz * y + zz * z)
    return out


def waves_kernel(scale, count_y, *refs):
    spec_refs, (tensor_ref, forward_ref, inverse_ref) = refs[:count_y], refs[count_y : count_y + 3]
    out_refs, (wave_ref, back_ref) = refs[count_y + 3 : -2], refs[-2:]
    lines, lanes = out_refs[0].shape
    local = 8
    planes = lines // local
    height = count_y * local
    sign = jnp.where(
        lax.broadcasted_iota(jnp.int32, (1, lanes), 1) < lanes // 2, 1.0, -1.0
    ).astype(jnp.float32)
    columns = []
    for plane in range(planes):
        value = jnp.concatenate(
            [spec_ref[plane * local : (plane + 1) * local] for spec_ref in spec_refs], 0
        )
        value = jnp.concatenate([value, turn(value, sign)], 0)
        high, low = split_high(value)
        columns.append(jnp.concatenate([high, low, high], 0))
    wave_ref[...] = dot(forward_ref[...], jnp.concatenate(columns, 1))

    chunk = 16
    depth = planes // 3
    double = 2 * height

    def step(index, carry):
        rows = pl.ds(pl.multiple_of(index * chunk, chunk), chunk)
        wave = []
        for part in range(3):
            layer = [
                wave_ref[rows, (part * depth + z) * lanes : (part * depth + z + 1) * lanes]
                for z in range(depth)
            ]
            wave.append(layers_forward(layer, sign))
        tensor = [
            [tensor_ref[part * 8 + level, rows, :].astype(jnp.float32) for level in range(8)]
            for part in range(6)
        ]
        image = apply_tensor(tensor, wave)
        for part in range(3):
            layer = layers_inverse(image[part], sign)
            for z in range(depth):
                spot = slice((part * depth + z) * lanes, (part * depth + z + 1) * lanes)
                high, low = split_high(layer[z] * scale)
                back_ref[rows, spot] = high
                back_ref[pl.ds(pl.multiple_of(double + index * chunk, chunk), chunk), spot] = low
                back_ref[pl.ds(pl.multiple_of(2 * double + index * chunk, chunk), chunk), spot] = high
        return carry

    lax.fori_loop(0, double // chunk, step, 0, unroll=True)
    back = dot(inverse_ref[...], back_ref[...])
    for plane in range(planes):
        part = slice(plane * lanes, (plane + 1) * lanes)
        value = back[:height, part] - turn(back[height:, part], sign)
        for number in range(count_y):
            out_refs[number][plane * local : (plane + 1) * local] = value[
                number * local : (number + 1) * local
            ]


def exchange_kernel(order_x, count_y, *refs):
    count_x, numbers = len(order_x), meeting(count_y)
    raw_refs, edge_refs, (ms_ref, aex_ref) = refs[:count_x], refs[count_x:-5], refs[-5:-3]
    exchange_ref, unit_ref, raw_ref = refs[-3:]
    depth, height, width = raw_ref.shape[2:]
    gx, gy = lax.axis_index("gx"), lax.axis_index("gy")

    def row_beside(field, other):
        value = None
        for number, edge_ref in zip(numbers, edge_refs):
            edge = get_edge(edge_ref, depth, width, 3 * depth * height, field)
            match = lax.bitwise_xor(gy, number) == other
            value = edge if value is None else jnp.where(match, edge, value)
        return value[:, None, :]

    for spot, number in enumerate(order_x):
        raw_ref[lax.bitwise_xor(gx, number)] = raw_refs[spot][...]
    left, right = jnp.maximum(gx - 1, 0), jnp.minimum(gx + 1, count_x - 1)
    shape = (depth, height, width)
    lane = lax.broadcasted_iota(jnp.int32, shape, 2)
    row = lax.broadcasted_iota(jnp.int32, shape, 1)

    def quantities(values):
        return directions(values[0], values[1]) + [looked_up(values[2], aex_ref)]

    raw = [raw_refs[0][f] for f in range(3)]
    here = quantities(raw)
    side = quantities([jnp.where(lane == 0, raw_ref[right, f], raw_ref[left, f]) for f in range(3)])
    above = quantities(
        [jnp.where(row == 0, row_beside(f, gy + 1), row_beside(f, gy - 1)) for f in range(3)]
    )
    saturation = looked_up(raw[2], ms_ref)
    total = [jnp.zeros(shape, jnp.float32) for _ in range(3)]

    def add(total, beside, weight):
        coupling = 2.0 * here[3] * beside[3] / (here[3] + beside[3]) * weight
        return [total[c] + coupling * (beside[c] - here[c]) for c in range(3)]

    one = jnp.float32(1.0)
    zero = jnp.float32(0.0)
    for shift, edge, there in ((1, 0, gx > 0), (width - 1, width - 1, gx < count_x - 1)):
        beside = [
            jnp.where(lane == edge, pltpu.roll(s, shift, 2), pltpu.roll(h, shift, 2))
            for s, h in zip(side, here)
        ]
        weight = jnp.where(lane == edge, jnp.where(there, one, zero), one) * side_weight
        total = add(total, beside, weight)
    for shift, edge, there in ((1, 0, gy > 0), (height - 1, height - 1, gy < count_y - 1)):
        beside = [
            jnp.where(row == edge, pltpu.roll(s, shift, 1), pltpu.roll(h, shift, 1))
            for s, h in zip(above, here)
        ]
        weight = jnp.where(row == edge, jnp.where(there, one, zero), one) * side_weight
        total = add(total, beside, weight)
    for part in range(3):
        unit_ref[part] = here[part]
    for z in range(depth):
        out = [total[c][z] for c in range(3)]
        for other in (z - 1, z + 1):
            if 0 <= other < depth:
                a, b = here[3][z], here[3][other]
                coupling = 2.0 * a * b / (a + b) * layer_weight
                out = [out[c] + coupling * (here[c][other] - here[c][z]) for c in range(3)]
        for c in range(3):
            exchange_ref[c, z] = out[c] / saturation[z]


def cross(first, second):
    return [
        first[1] * second[2] - first[2] * second[1],
        first[2] * second[0] - first[0] * second[2],
        first[0] * second[1] - first[1] * second[0],
    ]


def final_kernel(count_x, *refs):
    part_refs, (exchange_ref, unit_ref, field_ref, predicted_ref) = refs[:count_x], refs[count_x:]
    depth, height, width = unit_ref.shape[1:]
    rows = depth * height
    unit, field = [], []
    for c in range(3):
        place = slice(c * rows, (c + 1) * rows)
        total = part_refs[0][place]
        for part_ref in part_refs[1:]:
            total = total + part_ref[place]
        field.append(exchange_ref[c] + total.reshape(depth, height, width))
        unit.append(unit_ref[c])
        field_ref[c] = field[c]
    twist = cross(unit, field)
    second = cross(unit, twist)
    moved = [
        unit[c] - (time_step / (1.0 + damping * damping)) * (twist[c] + damping * second[c])
        for c in range(3)
    ]
    length = jnp.sqrt(moved[0] * moved[0] + moved[1] * moved[1] + moved[2] * moved[2])
    for c in range(3):
        predicted_ref[c] = moved[c] / length


vmem = pl.BlockSpec(memory_space=pltpu.VMEM)
smem = pl.BlockSpec(memory_space=pltpu.SMEM)
hbm = pl.BlockSpec(memory_space=pltpu.HBM)


def call(body, out, ins, operands, scratch=(), flops=0, name=None, grant=16 << 20):
    operands = [
        pltpu.with_memory_space_constraint(o, pltpu.HBM) if i is hbm else o
        for i, o in zip(ins, operands)
    ]
    size = sum(math.prod(o.shape) * o.dtype.itemsize for o in operands)
    outs = out if isinstance(out, (list, tuple)) else [out]
    size += sum(math.prod(o.shape) * jnp.dtype(o.dtype).itemsize for o in outs)
    return pl.pallas_call(
        body,
        out_shape=out,
        in_specs=ins,
        out_specs=[vmem] * len(outs) if outs is out else vmem,
        scratch_shapes=list(scratch),
        compiler_params=pltpu.CompilerParams(vmem_limit_bytes=grant),
        cost_estimate=pl.CostEstimate(flops=flops, bytes_accessed=size, transcendentals=0),
        name=name,
    )(*operands)


def f32(*shape):
    return jax.ShapeDtypeStruct(shape, jnp.float32)


def swapped(chunk, axis, number):
    devices = lax.axis_size(axis)
    return lax.ppermute(chunk, axis, [(i, i ^ number) for i in range(devices)])


def exchanged(chunks, axis, order):
    return [swapped(c, axis, n) if n else c for c, n in zip(chunks, order)]


def held(value):
    return pltpu.with_memory_space_constraint(value, pltpu.VMEM)


def chunk_order(devices):
    return list(range(devices - 1, -1, -1))


def after(value, other):
    return lax.optimization_barrier((value, other))[0]


def spread(block, axis, first):
    blocks = {0: block}
    bit = lax.axis_size(axis) // 2
    while bit:
        for number in list(blocks):
            blocks[number ^ bit] = swapped(blocks[number], axis, bit)
        if first is not None:
            blocks[bit], first = lax.optimization_barrier((blocks[bit], first))
            ready, first = first, None
        bit //= 2
    return [blocks[number] for number in range(lax.axis_size(axis))], ready


def far_sums(blocks, axis):
    blocks = {number: [block] for number, block in blocks.items()}
    terms, bit, block = [], 1, None
    while bit < lax.axis_size(axis):
        for number in sorted(blocks, reverse=True):
            if number & bit:
                block = functools.reduce(jnp.add, blocks.pop(number))
                blocks.get(number ^ bit, terms).append(swapped(block, axis, bit))
        bit *= 2
    return terms, block


def per_device(theta, phi, labels, ms_region, aex_region, kernel):
    count_x, count_y = lax.axis_size("gx"), lax.axis_size("gy")
    gx, gy = lax.axis_index("gx"), lax.axis_index("gy")
    depth, height, width = theta.shape
    rows = kernel.shape[2]
    lanes = 2 * rows
    lines = 3 * depth * height
    whole_y = count_y * height

    cells = f32(3, depth, height, width)
    order_x, order_y = list(range(count_x)), chunk_order(count_y)
    table = line_table(count_x, count_y, width, rows)
    if table is None:
        table = line_table_here(count_x, width, rows, order_y)
        columns_tables = column_tables_here(count_y, height, order_y)
    else:
        columns_tables = column_tables(count_y, height, order_y)
    sources = [jnp.asarray(t) for t in (table, *columns_tables)]
    twice = np.concatenate([np.eye(rows), np.eye(rows)], 1).astype(ml_dtypes.bfloat16)
    transform_flops = 6 * lines * count_x * width * count_y * lanes

    edge_rows = 3 * depth * width // lanes
    edge = f32(edge_rows, lanes)
    packed, first, last, ms_rows = call(
        pack_kernel,
        [cells, edge, edge, f32(*ms_region.shape, width)],
        [hbm] * 4,
        (theta, phi, labels, ms_region),
        scratch=(
            pltpu.VMEM((2, depth, height, width), jnp.float32),
            pltpu.VMEM((depth, height, width), jnp.int32),
            pltpu.SMEM(ms_region.shape, jnp.float32),
            pltpu.SemaphoreType.DMA((4,)),
        ),
        name="pack",
    )
    table, forward, inverse = call(
        functools.partial(load_kernel, order_x, order_y),
        [
            pltpu.VMEM((2, count_x, width, count_y * lanes), jnp.bfloat16),
            pltpu.VMEM(sources[1].shape[1:], jnp.bfloat16),
            pltpu.VMEM(sources[2].shape[1:], jnp.bfloat16),
        ],
        [hbm] * 3,
        tuple(sources),
        scratch=(pltpu.SemaphoreType.DMA((2 + count_x * count_y,)),),
        name="load",
    )

    gathered, table = spread(packed, "gx", table)
    tensor = call(
        tensor_kernel,
        jax.ShapeDtypeStruct((48, 2 * whole_y, lanes), jnp.bfloat16),
        [vmem, vmem],
        (kernel.reshape(48, rows, 2 * whole_y), jnp.asarray(twice)),
        flops=48 * 2 * rows * lanes * 2 * whole_y,
        name="tensor",
    )
    early, late = order_x[:-1], order_x[-1:]
    early_sums = call(
        functools.partial(early_lines_kernel, early),
        f32(lines, count_y * lanes),
        [vmem] * len(early) + [vmem, vmem],
        (*gathered[:-1], ms_rows, held(table)),
        flops=transform_flops * len(early) // count_x,
        name="early_lines",
    )
    spectrum = call(
        functools.partial(lines_kernel, late, order_y),
        [f32(lines + (edge_rows if n in carrying(count_y) else 0), lanes) for n in order_y],
        [vmem] * 6,
        (gathered[-1], early_sums, first, last, ms_rows, held(table)),
        flops=transform_flops * len(late) // count_x,
        name="lines",
    )
    columns = lax.optimization_barrier(exchanged(spectrum, "gy", order_y))
    scale = -1.0 / (2 * depth * 2 * whole_y * 2 * count_x * width)
    waves = call(
        functools.partial(waves_kernel, scale, count_y),
        [f32(lines, lanes)] * count_y,
        [vmem] * (count_y + 3),
        (*columns, tensor, forward, inverse),
        scratch=(
            pltpu.VMEM((2 * whole_y, 3 * depth * lanes), jnp.float32),
            pltpu.VMEM((6 * whole_y, 3 * depth * lanes), jnp.bfloat16),
        ),
        flops=20 * whole_y * whole_y * 3 * depth * lanes,
        name="waves",
    )
    returned = exchanged(waves, "gy", order_y)
    def back(numbers, chunks, name):
        blocks = call(
            functools.partial(back_lines_kernel, numbers, count_y),
            [f32(lines, width)] * len(numbers),
            [vmem] * (count_y + 1),
            (*chunks, held(table)),
            flops=transform_flops * len(numbers) // count_x,
            name=name,
        )
        return dict(zip(numbers, blocks))

    partial = back([n for n in order_x[2:] if n % 2], returned, "back_across")
    partial |= back([n for n in order_x[2:] if not n % 2] + [1], returned, "back_within")
    near = swapped(partial.pop(1), "gx", 1)
    parts, far_sum = far_sums(partial, "gx")
    returned, far_sum = lax.optimization_barrier((returned, far_sum))
    parts = [back([0], returned, "back_own")[0], near, *parts]
    edges = [columns[order_y.index(number)] for number in meeting(count_y)]
    edges, far_sum = lax.optimization_barrier((edges, far_sum))
    exchange, unit = call(
        functools.partial(exchange_kernel, order_x, count_y),
        [cells, cells],
        [vmem] * (count_x + len(edges)) + [smem] * 2,
        (*gathered, *edges, ms_region, aex_region),
        scratch=(pltpu.VMEM((count_x, 3, depth, height, width), jnp.float32),),
        flops=300 * depth * height * width,
        name="exchange",
    )
    field, predicted = call(
        functools.partial(final_kernel, len(parts)),
        [cells, cells],
        [vmem] * (len(parts) + 2),
        (*parts, exchange, unit),
        flops=60 * depth * height * width,
        name="predict",
    )
    return field, predicted


def solution(mesh):
    in_specs = (
        P(None, "gy", "gx"),
        P(None, "gy", "gx"),
        P(None, "gy", "gx"),
        P(),
        P(),
        P(None, None, ("gx", "gy"), None),
    )
    out_specs = (P(None, None, "gy", "gx"), P(None, None, "gy", "gx"))
    return jax.shard_map(
        per_device, mesh=mesh, in_specs=in_specs, out_specs=out_specs, check_vma=False
    )
```
